256 devices in a mesh: seq: 8 (over x, core), shard: 32 (over y, z).
Axes of the slice: x: 4, y: 4, z: 8, core: 2. Of those that a mesh axis runs over, the one named last changes fastest.
Arguments:
- tokens: bfloat16 [32, 2048, 1024], P('shard', 'seq'), may hold values from -6 to 6
- segment: int32 [32, 2048], P('shard'), may hold values from 0 to 2, as said below
- ln1_gain: float32 [1024], replicated, may hold values from 0.1 to 1.9
- ln1_shift: float32 [1024], replicated, may hold values from -1 to 1
- w_qkv: bfloat16 [1024, 3072], P('shard'), may hold values from -0.25 to 0.25
- bias_query: float32 [1024], replicated, may hold values from -1.5 to 1.5
- bias_value: float32 [1024], replicated, may hold values from -1.5 to 1.5
- w_out: bfloat16 [1024, 1024], P('shard'), may hold values from -0.75 to 0.75
- bias_out: float32 [1024], replicated, may hold values from -1 to 1
- ln2_gain: float32 [1024], replicated, may hold values from 0.1 to 1.9
- ln2_shift: float32 [1024], replicated, may hold values from -1 to 1
- w_fc: bfloat16 [1024, 4096], P('shard'), may hold values from -0.1875 to 0.1875
- bias_fc: float32 [4096], replicated, may hold values from -1.5 to 1.5
- w_proj: bfloat16 [4096, 1024], P('shard'), may hold values from -0.09375 to 0.09375
- bias_proj: float32 [1024], replicated, may hold values from -1 to 1
- cotangent: bfloat16 [32, 2048, 1024], P('shard', 'seq'), may hold values from -6 to 6
Outputs:
- output: bfloat16 [32, 2048, 1024], P('shard', 'seq')
- d_tokens: float32 [32, 2048, 1024], P('shard', 'seq')
- g_ln1_gain: float32 [1024], replicated
- g_ln1_shift: float32 [1024], replicated
- g_qkv: float32 [1024, 3072], P('shard')
- g_bias_query: float32 [1024], replicated
- g_bias_value: float32 [1024], replicated
- g_out: float32 [1024, 1024], P('shard')
- g_bias_out: float32 [1024], replicated
- g_ln2_gain: float32 [1024], replicated
- g_ln2_shift: float32 [1024], replicated
- g_fc: float32 [1024, 4096], P('shard')
- g_bias_fc: float32 [4096], replicated
- g_proj: float32 [4096, 1024], P('shard')
- g_bias_proj: float32 [1024], replicated
The draws below stay inside these ranges and needn't reach their ends.
Inputs may be any that keep to these rules, and one draw needn't show every extreme that they name: `segment`: in each group: 0 on the first 1024 positions, then 1, then 2, never falling; each continuation holds at least 256 positions.
All inputs are finite; a program needn't handle non-finite values.
Results may differ from the reference program's by a relative error of at most 0.025.
Values may be sent and summed in bfloat16 or wider, within the bound.
A program may use at most 256 MiB of HBM per device.

```python
import jax
import jax.numpy as jnp
from jax import lax

D = 1024
HEADS = 16
HDIM = 64
FF = 4096
GROUP_TOK = 2048
PROMPT = 1024
GROUPS = 32


def draw_segment(key, part):
    key = jax.random.fold_in(key, 11)
    bounds = jax.random.randint(key, (GROUPS, 1), PROMPT + GROUP_TOK // 8, PROMPT + 3 * GROUP_TOK // 8 + 1)
    place = jnp.arange(GROUP_TOK, dtype=jnp.int32)[None, :]
    return jnp.where(place < PROMPT, 0, jnp.where(place < bounds, 1, 2)).astype(jnp.int32)


def level_of(own_key, extent, shards, low, largest):
    loudness, own = 1.0, jax.random.fold_in(own_key, 6)
    for axis_at, shards_of in shards:
        draws = jnp.exp(jax.random.uniform(jax.random.fold_in(own, axis_at), (shards_of,), jnp.float32, low / len(shards), largest / len(shards)))
        loudness = loudness * jnp.repeat(draws, extent[axis_at] // shards_of).reshape([-1 if axis == axis_at else 1 for axis in range(len(extent))])
    return loudness


def bell_draw(own_key, shape, scale, most, pieces=(), held_as=jnp.bfloat16):
    values = jax.random.normal(own_key, shape, jnp.float32) * scale
    if len(pieces) > 0:
        values = level_of(own_key, shape, pieces, -0.22, 0.18) * values
    return jnp.clip(values, min=-most, max=most).astype(held_as)


def setup_inputs(seed: int = 0) -> dict:
    streams_of = jax.random.split(jax.random.key(seed), 17)
    return {
        "tokens": bell_draw(streams_of[0], (GROUPS, GROUP_TOK, D), 1.0, 6.0, ((0, 32), (1, 8))),
        "segment": draw_segment(jax.random.fold_in(streams_of[16], 71), 0),
        "ln1_gain": jnp.clip(1.0 + 0.18 * jax.random.normal(streams_of[2], (D,), jnp.float32), 0.1, 1.9),
        "ln1_shift": bell_draw(streams_of[3], (D,), 0.2, 1.0, (), jnp.float32),
        "w_qkv": bell_draw(streams_of[4], (D, 3 * D), (D // 2) ** -0.5, 0.25, ((0, 32),)),
        "bias_query": bell_draw(streams_of[5], (D,), 0.3, 1.5, (), jnp.float32),
        "bias_value": bell_draw(streams_of[6], (D,), 0.3, 1.5, (), jnp.float32),
        "w_out": bell_draw(streams_of[7], (D, D), (D // 16) ** -0.5, 0.75, ((0, 32),)),
        "bias_out": bell_draw(streams_of[8], (D,), 0.2, 1.0, (), jnp.float32),
        "ln2_gain": jnp.clip(1.0 + 0.18 * jax.random.normal(streams_of[9], (D,), jnp.float32), 0.1, 1.9),
        "ln2_shift": bell_draw(streams_of[10], (D,), 0.2, 1.0, (), jnp.float32),
        "w_fc": bell_draw(streams_of[11], (D, FF), D ** -0.5, 0.1875, ((0, 32),)),
        "bias_fc": bell_draw(streams_of[12], (FF,), 0.3, 1.5, (), jnp.float32),
        "w_proj": bell_draw(streams_of[13], (FF, D), FF ** -0.5, 0.09375, ((0, 32),)),
        "bias_proj": bell_draw(streams_of[14], (D,), 0.2, 1.0, (), jnp.float32),
        "cotangent": bell_draw(streams_of[15], (GROUPS, GROUP_TOK, D), 1.0, 6.0, ((0, 32), (1, 8))),
    }


@jax.custom_vjp
def low(v):
    return lax.optimization_barrier(v.astype(jnp.bfloat16)).astype(jnp.float32)

@jax.custom_vjp
def low_back(v):
    return v

def low_keep(v):
    return (low(v), None)

def low_pass(kept, grad):
    return (grad,)

def back_keep(v):
    return (v, None)

def back_low(kept, grad):
    return (low(grad),)
low.defvjp(low_keep, low_pass)
low_back.defvjp(back_keep, back_low)

def matmul(left, right):
    return jnp.dot(left, right, precision=lax.Precision.HIGHEST, preferred_element_type=jnp.float32)

def norm_layer(values, gain, shift):
    mean = lax.optimization_barrier(jnp.mean(values, axis=-1, keepdims=True))
    centered = values - mean
    spread = lax.optimization_barrier(jnp.mean(centered * centered, axis=-1, keepdims=True))
    return centered * lax.rsqrt(spread + 1e-05) * gain + shift

def attend(queries, keys, values, segment):
    width = min(512, GROUP_TOK)
    count = GROUP_TOK // width
    key_pos = jnp.arange(GROUP_TOK, dtype=jnp.int32)
    scale = HDIM ** (-0.5)

    def one_block(number):
        first = (number * width).astype(jnp.int32)
        block_q = lax.dynamic_slice_in_dim(queries, first, width, 0)
        block_seg = lax.dynamic_slice_in_dim(segment, first, width, 0)
        query_pos = first + jnp.arange(width, dtype=jnp.int32)
        scores = jnp.einsum('qhd,khd->hqk', block_q, keys, precision=lax.Precision.HIGHEST) * scale
        scores = low_back(scores)
        allowed = (key_pos[None, :] <= query_pos[:, None]) & ((segment[None, :] == 0) | (segment[None, :] == block_seg[:, None]))
        scores = jnp.where(allowed[None], scores, -1e+30)
        probs = low(jax.nn.softmax(scores, axis=-1))
        return jnp.einsum('hqk,khd->qhd', probs, values, precision=lax.Precision.HIGHEST)
    blocks = lax.map(jax.checkpoint(one_block), jnp.arange(count, dtype=jnp.int32))
    return blocks.reshape(GROUP_TOK, HEADS * HDIM)

def layer(inputs, segment, params):
    ln1_gain, ln1_shift, w_qkv, bias_query, bias_value, w_out, bias_out, ln2_gain, ln2_shift, w_fc, bias_fc, w_proj, bias_proj = params
    normed = low(norm_layer(inputs, ln1_gain, ln1_shift))
    bias_all = jnp.concatenate([bias_query, jnp.zeros_like(bias_query), bias_value])
    mixed = low(low_back(matmul(normed, w_qkv) + bias_all))
    split = mixed.reshape(GROUP_TOK, 3, HEADS, HDIM)
    heads = attend(split[:, 0], split[:, 1], split[:, 2], segment)
    heads = low(low_back(heads))
    branch = low_back(matmul(heads, w_out) + bias_out)
    middle = inputs + branch
    normed2 = low(norm_layer(middle, ln2_gain, ln2_shift))
    hidden = low_back(matmul(normed2, w_fc) + bias_fc)
    active = low(jax.nn.gelu(hidden, approximate=True))
    branch2 = low_back(matmul(active, w_proj) + bias_proj)
    return middle + branch2

def reference(tokens, segment, ln1_gain, ln1_shift, w_qkv, bias_query, bias_value, w_out, bias_out, ln2_gain, ln2_shift, w_fc, bias_fc, w_proj, bias_proj, cotangent):
    params = tuple((p.astype(jnp.float32) for p in (ln1_gain, ln1_shift, w_qkv, bias_query, bias_value, w_out, bias_out, ln2_gain, ln2_shift, w_fc, bias_fc, w_proj, bias_proj)))

    def one_group(carry, items):
        inputs, group_seg, group_cot = items

        def forward(values, weights):
            return layer(values, group_seg, weights)
        result, pull = jax.vjp(forward, inputs.astype(jnp.float32), params)
        d_inputs, d_params = pull(group_cot.astype(jnp.float32))
        carry = jax.tree.map(lambda a, b: a + b, carry, d_params)
        return (carry, (result.astype(jnp.bfloat16), d_inputs))
    zeros = jax.tree.map(jnp.zeros_like, params)
    grads, (output, d_tokens) = lax.scan(one_group, zeros, (tokens, segment, cotangent))
    return (output, d_tokens, grads[0], grads[1], grads[2], grads[3], grads[4], grads[5], grads[6], grads[7], grads[8], grads[9], grads[10], grads[11], grads[12])
```

```python
import functools

import jax
import jax.numpy as jnp
from jax import lax
from jax.experimental import pallas as pl
from jax.experimental.pallas import tpu as pltpu
from jax.sharding import Mesh
from jax.sharding import PartitionSpec as P

SEQ = ("x", "core")
SHARD = ("y", "z")
F32 = jnp.float32
LOW = jnp.bfloat16
MIB = 2**20
TOK = 2048
OWN = 256
TILE = 512
D = 1024
HIDDEN = 512
SPAN = 128
GELU_A = 0.7978845608028654
GELU_B = 0.044715

IN_VMEM = pl.BlockSpec(memory_space=pltpu.VMEM)
IN_SMEM = pl.BlockSpec(memory_space=pltpu.SMEM)
ANYWHERE = pl.BlockSpec(memory_space=pl.ANY)
DMA = pltpu.SemaphoreType.DMA


def shaped(shape, dtype):
    return jax.ShapeDtypeStruct(shape, dtype)


def remote(src, dst, send, recv, **device):
    return pltpu.make_async_remote_copy(
        src_ref=src,
        dst_ref=dst,
        send_sem=send,
        recv_sem=recv,
        device_id=device,
        device_id_type=pl.DeviceIdType.MESH,
    )


def axis(name):
    return lax.axis_index(name)


def ahead(name, k, count):
    return lax.rem(axis(name) + k, count)


def seq_peers():
    core = axis("core")
    return [
        {"x": ahead("x", j, 4), "core": lax.rem(core + i, 2)}
        for j in range(4)
        for i in range(2)
        if (j, i) != (0, 0)
    ]


def near_peers():
    return [{"x": ahead("x", 1, 4)}, {"x": ahead("x", 3, 4)}, {"core": 1 - axis("core")}]


def y_peers():
    return [{"y": ahead("y", k, 4)} for k in range(1, 4)]


def z_peers():
    return [{"z": ahead("z", k, 8)} for k in range(1, 8)]


def greet(peers):
    sem = pltpu.get_barrier_semaphore()
    for peer in peers:
        pl.semaphore_signal(sem, inc=1, device_id=peer, device_id_type=pl.DeviceIdType.MESH)
    return lambda: pl.semaphore_wait(sem, len(peers))


def dot(a, b):
    return jnp.dot(a, b, preferred_element_type=F32)


def dot_nt(a, b):
    return lax.dot_general(a, b, (((1,), (1,)), ((), ())), preferred_element_type=F32)


def dot_tn(a, b):
    return lax.dot_general(a, b, (((0,), (0,)), ((), ())), preferred_element_type=F32)


def whitened(values):
    mean = jnp.mean(values, axis=-1, keepdims=True)
    centered = values - mean
    spread = jnp.mean(centered * centered, axis=-1, keepdims=True)
    inverse = lax.rsqrt(spread + 1e-05)
    return centered * inverse, inverse


def norm_back(grad, gain, white, inverse):
    d_white = grad * gain
    first = jnp.mean(d_white, axis=-1, keepdims=True)
    second = jnp.mean(d_white * white, axis=-1, keepdims=True)
    return inverse * (d_white - first - white * second)


class Gather:
    def __init__(self, src, at, rows, send, recv):
        x, core = axis("x"), axis("core")
        other = 1 - core
        right, far, left = (lax.rem(x + k, 4) for k in (1, 2, 3))
        low, high = pl.ds(0, rows // 2), pl.ds(rows // 2, rows // 2)
        mine, r, f, l = (at(2 * k + core) for k in (x, right, far, left))
        mine_o, r_o, f_o, l_o = (at(2 * k + other) for k in (x, right, far, left))
        plan = [
            (src, mine, {"x": right}, l),
            (src, mine, {"x": left}, r),
            (src, mine, {"core": other}, mine_o),
            (l.at[low], l.at[low], {"x": right}, f.at[low]),
            (r.at[high], r.at[high], {"x": left}, f.at[high]),
            (l, l, {"core": other}, l_o),
            (r, r, {"core": other}, r_o),
            (f, f, {"core": other}, f_o),
        ]
        self.out = [
            remote(a, b, send.at[k], recv.at[k], **dev) for k, (a, b, dev, _) in enumerate(plan)
        ]
        self.into = [
            remote(land, land, send.at[k], recv.at[k], **dev)
            for k, (_, _, dev, land) in enumerate(plan)
        ]
        self.blocks = dict(
            mine=2 * x + core,
            mine_o=2 * x + other,
            left=2 * left + core,
            left_o=2 * left + other,
            right=2 * right + core,
            right_o=2 * right + other,
            far=2 * far + core,
            far_o=2 * far + other,
        )

    def start(self):
        for k in (0, 1, 2):
            self.out[k].start()

    def got(self, k):
        self.into[k].wait_recv()

    def pass_left(self):
        self.got(0)
        self.out[3].start()
        self.out[5].start()

    def pass_right(self):
        self.got(1)
        self.out[4].start()
        self.out[6].start()

    def pass_far(self):
        self.got(3)
        self.got(4)
        self.out[7].start()

    def sent(self):
        for copy in self.out:
            copy.wait_send()


class Reduce:
    def __init__(self, part, from_core, total, land, send, recv):
        self.part, self.from_core, self.total, self.land = part, from_core, total, land
        self.send, self.recv = send, recv
        self.x, self.core = axis("x"), axis("core")

    def core_copy(self, j):
        block = 2 * lax.rem(self.x + j, 4) + 1 - self.core
        return remote(
            self.part(block),
            self.from_core(j),
            self.send.at[j],
            self.recv.at[j],
            core=1 - self.core,
        )

    def chip_copy(self, j):
        return remote(
            self.total(j),
            self.land(j),
            self.send.at[3 + j],
            self.recv.at[3 + j],
            x=lax.rem(self.x + j, 4),
        )

    def mine(self, j):
        return self.part(2 * lax.rem(self.x + j, 4) + self.core)

    def to_core(self, j):
        self.core_copy(j).start()

    def to_chip(self, j):
        self.core_copy(j).wait_recv()
        self.total(j)[...] = (
            self.mine(j)[...].astype(F32) + self.from_core(j)[...].astype(F32)
        ).astype(LOW)
        self.chip_copy(j).start()

    def result(self):
        self.core_copy(0).wait_recv()
        total = self.mine(0)[...].astype(F32) + self.from_core(0)[...].astype(F32)
        for j in (1, 3, 2):
            self.chip_copy(j).wait_recv()
            total = total + self.land(j)[...].astype(F32)
        return total

    def sent(self):
        for j in range(4):
            self.core_copy(j).wait_send()
        for j in range(1, 4):
            self.chip_copy(j).wait_send()


def call(kernel, outs, ins, scratch, name, number=None, vmem=56):
    extra = {} if number is None else dict(collective_id=number, has_side_effects=True)
    return pl.pallas_call(
        kernel,
        out_shape=[shape for shape, _ in outs],
        in_specs=ins,
        out_specs=[spec for _, spec in outs],
        scratch_shapes=scratch,
        name=name,
        compiler_params=pltpu.CompilerParams(vmem_limit_bytes=vmem * MIB, **extra),
    )


def chosen_units(values, seq):
    lane = lax.broadcasted_iota(jnp.int32, (values.shape[0], 128), 1)
    tiles = []
    for q in range(4):
        tile = jnp.zeros((values.shape[0], 128), F32)
        for p in range(8):
            at = 128 * (8 * q + p)
            shift = lax.rem(16 * p - 16 * seq + 128, 128)
            turned = pltpu.roll(values[:, at : at + 128], shift, 1)
            tile = jnp.where((lane // 16) == p, turned, tile)
        tiles.append(tile)
    return jnp.concatenate(tiles, axis=1)


def columns_kernel(wq, wo, wf, wp, bq, bv, bf, wq_o, wo_o, wf_o, wp_o, bias_o, bf_o):
    core = axis("core")
    seq = 2 * axis("x") + core
    span = pl.ds(pl.multiple_of(SPAN * seq, SPAN), SPAN)
    for k in range(3):
        at = pl.ds(pl.multiple_of(k * D + SPAN * seq, SPAN), SPAN)
        wq_o[:, k * SPAN : (k + 1) * SPAN] = wq[:, at]
    bias_o[:, :SPAN] = bq[:, span]
    bias_o[:, SPAN : 2 * SPAN] = jnp.zeros((1, SPAN), F32)
    bias_o[:, 2 * SPAN :] = bv[:, span]
    wo_o[...] = wo[pl.ds(pl.multiple_of(16 * core, 16), 16), :]
    wp_o[...] = wp[pl.ds(pl.multiple_of(16 * seq, 16), 16), :]
    wf_o[...] = chosen_units(wf[...].astype(F32), seq).astype(LOW)
    bf_o[...] = chosen_units(jnp.broadcast_to(bf[...], (8, 4 * D)), seq)[0:1]


def columns(w_qkv, w_out, w_fc, w_proj, bias_query, bias_value, bias_fc):
    outs = [
        ((32, 3 * SPAN), LOW),
        ((16, D), LOW),
        ((32, HIDDEN), LOW),
        ((16, D), LOW),
        ((1, 3 * SPAN), F32),
        ((1, HIDDEN), F32),
    ]
    return call(
        columns_kernel, [(shaped(*o), IN_VMEM) for o in outs], [IN_VMEM] * 7, [], "columns"
    )(w_qkv, w_out, w_fc, w_proj, bias_query[None], bias_value[None], bias_fc[None])


def qkv_kernel(
    x, wq, wo, wf, wp, gain, shift, bias,
    xall_o, n1_o, qkv_o, wq_o, wo_o, wf_o, wp_o,
    xs, ns, g_send, g_recv, z_send, z_recv, y_send, y_recv, loc, x_loc, n_loc,
):
    y, z = axis("y"), axis("z")
    ready = greet(near_peers() + y_peers() + z_peers())
    owns = [(wq, wq_o.at[y, z]), (wo, wo_o.at[y, z]), (wf, wf_o.at[z]), (wp, wp_o.at[z])]
    local = [pltpu.make_async_copy(a, b, loc.at[k]) for k, (a, b) in enumerate(owns)]
    gather = Gather(x, lambda t: xs.at[t], OWN, g_send, g_recv)
    mine = gather.blocks["mine"]
    local.append(pltpu.make_async_copy(x, xs.at[mine], loc.at[4]))
    for copy in local:
        copy.start()
    ready()
    gather.start()
    to_z, from_z = [], []
    for n, (own, dst) in enumerate(owns):
        for k in range(1, 8):
            sems = (z_send.at[n, k], z_recv.at[n, k])
            to_z.append(remote(own, dst, *sems, z=ahead("z", k, 8)))
            to_z[-1].start()
            back = lax.rem(z + 8 - k, 8)
            land = (wq_o.at[y, back], wo_o.at[y, back], wf_o.at[back], wp_o.at[back])[n]
            from_z.append(remote(land, land, *sems, z=back))
    for copy in local:
        copy.wait()

    kept = []

    def put(block):
        def one(i, _):
            rows = pl.ds(pl.multiple_of(i * 128, 128), 128)
            white, _inv = whitened(xs[block, rows, :].astype(F32))
            ns[block, rows, :] = (white * gain[...] + shift[...]).astype(LOW)
            return 0

        lax.fori_loop(0, OWN // 128, one, 0)
        n = len(kept) // 2
        rows = pl.ds(pl.multiple_of(OWN * block, OWN), OWN)
        kept.append(pltpu.make_async_copy(xs.at[block], xall_o.at[rows], x_loc.at[n]))
        kept.append(pltpu.make_async_copy(ns.at[block], n1_o.at[rows], n_loc.at[n]))
        kept[-1].start()
        kept[-2].start()

    def project(block):
        rows = pl.ds(pl.multiple_of(OWN * block, OWN), OWN)
        weights = wq_o[...].reshape(D, 3 * SPAN)
        qkv_o[rows, :] = (dot(ns[block], weights) + bias[...]).astype(LOW)

    put(mine)
    gather.got(2)
    put(gather.blocks["mine_o"])
    to_y, from_y = [], []
    for n, dst in enumerate((wq_o, wo_o)):
        for k in range(7 * n, 7 * n + 7):
            from_z[k].wait_recv()
        for k in range(1, 4):
            sems = (y_send.at[n, k], y_recv.at[n, k])
            to_y.append(remote(dst.at[y], dst.at[y], *sems, y=ahead("y", k, 4)))
            to_y[-1].start()
            back = lax.rem(y + 4 - k, 4)
            from_y.append(remote(dst.at[back], dst.at[back], *sems, y=back))
    gather.pass_left()
    gather.pass_right()
    put(gather.blocks["left"])
    put(gather.blocks["right"])
    gather.got(5)
    put(gather.blocks["left_o"])
    gather.got(6)
    put(gather.blocks["right_o"])
    for k in range(3):
        from_y[k].wait_recv()
    for name in ("mine", "mine_o", "left", "right", "left_o", "right_o"):
        project(gather.blocks[name])
    gather.pass_far()
    put(gather.blocks["far"])
    project(gather.blocks["far"])
    gather.got(7)
    put(gather.blocks["far_o"])
    project(gather.blocks["far_o"])
    for k in range(14, 28):
        from_z[k].wait_recv()
    for k in range(3, 6):
        from_y[k].wait_recv()
    for copy in to_z + to_y:
        copy.wait_send()
    gather.sent()
    for copy in kept:
        copy.wait()


def qkv_of_heads(x, wq, wo, wf, wp, gain, shift, bias):
    outs = [
        (shaped((TOK, D), LOW), ANYWHERE),
        (shaped((TOK, D), LOW), ANYWHERE),
        (shaped((TOK, 3 * SPAN), LOW), IN_VMEM),
        (shaped((4, 8, 32, 3 * SPAN), LOW), IN_VMEM),
        (shaped((4, 8, 16, D), LOW), ANYWHERE),
        (shaped((8, 32, HIDDEN), LOW), ANYWHERE),
        (shaped((8, 16, D), LOW), ANYWHERE),
    ]
    scratch = [
        pltpu.VMEM((8, OWN, D), LOW),
        pltpu.VMEM((8, OWN, D), LOW),
        DMA((8,)), DMA((8,)), DMA((4, 8)), DMA((4, 8)), DMA((2, 4)), DMA((2, 4)),
        DMA((5,)), DMA((8,)), DMA((8,)),
    ]
    return call(qkv_kernel, outs, [IN_VMEM] * 8, scratch, "qkv", 1)(
        x, wq, wo, wf, wp, gain[None], shift[None], bias
    )


def head_lanes(shape, dim, head):
    return (lax.broadcasted_iota(jnp.int32, shape, dim) // 64) == head


def masked_scores(scores, cut, q_tile, k_tile):
    shape = scores.shape
    key = k_tile * TILE + lax.broadcasted_iota(jnp.int32, shape, 0)
    query = q_tile * TILE + lax.broadcasted_iota(jnp.int32, shape, 1)
    allowed = key <= query
    if q_tile >= 2:
        allowed = allowed & ((key >= cut) | (query < cut))
    return jnp.where(allowed, scores, -1e30)


def tile_rows(tile):
    if isinstance(tile, int):
        return pl.ds(tile * TILE, TILE)
    return pl.ds(pl.multiple_of(tile * TILE, TILE), TILE)


def attend_kernel(
    qkv, cut_ref, wo, wfz,
    o_all, lse, wo_o, wf_o,
    qm, vt, scores, ot, g_send, g_recv, y_send, y_recv, c_send, c_recv, loc,
):
    y, core = axis("y"), axis("core")
    me = 2 * axis("x") + core
    ready = greet(near_peers() + y_peers())
    cut = cut_ref[0, 0]
    for tile in range(4):
        rows = tile_rows(tile)
        q = qkv[rows, :SPAN].astype(F32) * 0.125
        v_t = jnp.transpose(qkv[rows, 2 * SPAN :].astype(F32))
        for head in range(2):
            qm[head, rows, :] = jnp.where(head_lanes(q.shape, 1, head), q, 0.0).astype(LOW)
            vt[head, :, rows] = jnp.where(head_lanes(v_t.shape, 0, head), v_t, 1.0).astype(LOW)
    ready()
    to_core = remote(wo, wo_o, c_send, c_recv, core=1 - core)
    to_core.start()
    to_y, from_y = [], []
    for k in range(1, 4):
        sems = (y_send.at[k], y_recv.at[k])
        to_y.append(remote(wfz, wf_o.at[y], *sems, y=ahead("y", k, 4)))
        to_y[-1].start()
        back = lax.rem(y + 4 - k, 4)
        from_y.append(remote(wf_o.at[back], wf_o.at[back], *sems, y=back))
    local = [pltpu.make_async_copy(wfz, wf_o.at[y], loc.at[4])]
    local[0].start()

    gathers = []
    for tile in range(4):
        q_rows = tile_rows(tile)
        free = min(tile, 2)

        def score(k_tile, peaks, masked, tile=tile, q_rows=q_rows):
            keys = qkv[tile_rows(k_tile), SPAN : 2 * SPAN]
            new = []
            for head in range(2):
                s = dot_nt(keys, qm[head, q_rows, :])
                if masked:
                    s = masked_scores(s, cut, tile, k_tile)
                scores[head, tile_rows(k_tile), :] = s
                new.append(jnp.maximum(peaks[head], jnp.max(s, axis=0, keepdims=True)))
            return tuple(new)

        peaks = (jnp.full((1, TILE), -3e38, F32),) * 2
        if free:
            peaks = lax.fori_loop(0, free, lambda k, p: score(k, p, False), peaks)
        for k_tile in range(free, tile + 1):
            peaks = score(k_tile, peaks, True)

        def weigh(k_tile, sums, peaks=peaks):
            rows = tile_rows(k_tile)
            new = []
            for head in range(2):
                e = jnp.exp(scores[head, rows, :] - peaks[head]).astype(LOW)
                new.append(sums[head] + dot(vt[head, :, rows], e))
            return tuple(new)

        sums = (jnp.zeros((SPAN, TILE), F32),) * 2
        sums = lax.fori_loop(0, tile + 1, weigh, sums)
        weights = (sums[0][64:65], sums[1][0:1])
        for head in range(2):
            lse[head : head + 1, q_rows] = peaks[head] + jnp.log(weights[head])
        o_t = jnp.concatenate([sums[0][:64] / weights[0], sums[1][64:] / weights[1]], axis=0)
        ot[tile] = jnp.transpose(o_t).astype(LOW)
        keep = pltpu.make_async_copy(ot.at[tile], o_all.at[me, q_rows], loc.at[tile])
        keep.start()
        local.append(keep)
        gather = Gather(
            ot.at[tile],
            lambda t, rows=q_rows: o_all.at[t, rows],
            TILE,
            g_send.at[tile],
            g_recv.at[tile],
        )
        gather.start()
        gathers.append(gather)
        if tile >= 1:
            gathers[tile - 1].pass_left()
            gathers[tile - 1].pass_right()
        if tile >= 2:
            gathers[tile - 2].pass_far()
    gathers[2].pass_far()
    gathers[3].pass_left()
    gathers[3].pass_right()
    gathers[3].pass_far()
    for gather in gathers:
        for k in (2, 5, 6, 7):
            gather.got(k)
        gather.sent()
    to_core.wait_recv()
    to_core.wait_send()
    for copy in from_y:
        copy.wait_recv()
    for copy in to_y:
        copy.wait_send()
    for copy in local:
        copy.wait()


def attend(qkv, cut, wo, wfz):
    outs = [
        (shaped((8, TOK, SPAN), LOW), ANYWHERE),
        (shaped((2, TOK), F32), IN_VMEM),
        (shaped((4, 8, 16, D), LOW), ANYWHERE),
        (shaped((4, 8, 32, HIDDEN), LOW), ANYWHERE),
    ]
    scratch = [
        pltpu.VMEM((2, TOK, SPAN), LOW),
        pltpu.VMEM((2, SPAN, TOK), LOW),
        pltpu.VMEM((2, TOK, TILE), F32),
        pltpu.VMEM((4, TILE, SPAN), LOW),
        DMA((4, 8)), DMA((4, 8)), DMA((4,)), DMA((4,)), DMA, DMA, DMA((5,)),
    ]
    return call(attend_kernel, outs, [IN_VMEM, IN_SMEM, ANYWHERE, ANYWHERE], scratch, "attend", 2)(
        qkv, cut, wo, wfz
    )


def block_order(i):
    return jnp.where(i == 0, 1, jnp.where(i == 1, 3, jnp.where(i == 2, 2, 0)))


def hidden_kernel(
    o_all, x_all, cot, wo_a, wo_b, wf_in, wpz, bo, gain, shift, bf,
    outp, mid_o, dm_o, do_all, gfc_o, gproj_o, gop_o, small_o, bfc_o,
    xs, os, cs, wo, wf, wp, n2, da, act, part, from_core, total, land, gfc, gproj, dob,
    loc, c_send, c_recv, y_send, y_recv, r_send, r_recv, a_send, a_recv, o_loc,
):
    x, core, y = axis("x"), axis("core"), axis("y")
    me = 2 * x + core
    ready = greet(seq_peers() + y_peers())
    local = [
        (o_all, os),
        (x_all, xs),
        (wo_a, wo.at[:, :, core]),
        (wo_b, wo.at[:, :, 1 - core]),
        (wf_in, wf),
        (wpz, wp.at[y]),
        (cot, cs.at[me]),
    ]
    local = [pltpu.make_async_copy(a, b, loc.at[k]) for k, (a, b) in enumerate(local)]
    for copy in local:
        copy.start()
    gfc[...] = jnp.zeros_like(gfc)
    gproj[...] = jnp.zeros_like(gproj)
    bfc_o[...] = jnp.zeros_like(bfc_o)
    ready()
    gather = Gather(cot, lambda t: cs.at[t], OWN, c_send, c_recv)
    gather.start()
    to_y, from_y = [], []
    for k in range(1, 4):
        sems = (y_send.at[k], y_recv.at[k])
        to_y.append(remote(wpz, wp.at[y], *sems, y=ahead("y", k, 4)))
        to_y[-1].start()
        back = lax.rem(y + 4 - k, 4)
        from_y.append(remote(wp.at[back], wp.at[back], *sems, y=back))
    for copy in local:
        copy.wait()

    def middle_of(rows):
        left = jnp.concatenate([os[t, rows, :] for t in range(8)], axis=1)
        return xs[rows, :].astype(F32) + dot(left, wo[...].reshape(D, D)) + bo[...]

    def forward(b, _):
        rows = tile_rows(b)
        white, _inv = whitened(middle_of(rows))
        low = (white * gain[...] + shift[...]).astype(LOW)
        n2[rows, :] = low
        v = dot(low, wf[...].reshape(D, HIDDEN)) + bf[...]
        square = v * v
        t = jnp.tanh(GELU_A * v * (1.0 + GELU_B * square))
        half = 0.5 * (1.0 + t)
        act[rows, :] = (v * half).astype(LOW)
        slope = 0.5 * GELU_A * (1.0 + 3.0 * GELU_B * square)
        da[rows, :] = half + v * (1.0 - t * t) * slope

        @pl.when(b == 2)
        def _():
            gather.pass_left()
            gather.pass_right()

        return 0

    lax.fori_loop(0, 4, forward, 0)
    for copy in from_y:
        copy.wait_recv()
    gather.got(2)
    gather.pass_far()
    for k in (5, 6, 7):
        gather.got(k)
    reduce = Reduce(
        lambda t: part.at[t],
        lambda j: from_core.at[j],
        lambda j: total.at[j],
        lambda j: land.at[j],
        r_send,
        r_recv,
    )

    def backward(i, _):
        j = block_order(i)
        chip = lax.rem(x + j, 4)
        rows = tile_rows(chip)
        c_low = cs[pl.ds(2 * chip, 2)].reshape(TILE, D)
        weights = wp[...].reshape(HIDDEN, D)
        a_low = act[rows, :]
        d_h = dot_nt(c_low, weights) * da[rows, :]
        low = d_h.astype(LOW)
        bfc_o[0:1, :] += jnp.sum(low.astype(F32), axis=0, keepdims=True)
        d_n2 = dot_nt(low, wf[...].reshape(D, HIDDEN))
        part[pl.ds(2 * chip, 2)] = d_n2.astype(LOW).reshape(2, OWN, D)
        reduce.to_core(j)
        gproj[...] += dot_tn(a_low, c_low)
        gfc[...] += dot_tn(n2[rows, :], low)
        out_low = dot(a_low, weights).astype(LOW)
        xs[rows, :] = out_low

        @pl.when(i >= 1)
        def _():
            reduce.to_chip(block_order(i - 1))

        return 0

    own_rows = pl.ds(pl.multiple_of(me * OWN, OWN), OWN)
    middle = middle_of(own_rows)
    mid_o[...] = middle
    lax.fori_loop(0, 4, backward, 0)
    out_copy = pltpu.make_async_copy(xs, outp, o_loc)
    out_copy.start()
    gfc_o[...] = gfc[...].astype(LOW)
    gproj_o[...] = gproj[...].astype(LOW)
    middle = mid_o[...]
    white, inverse = whitened(middle)
    c_own = cot[...].astype(F32)
    d_n2 = reduce.result()
    d_m = c_own + norm_back(d_n2, gain[...], white, inverse)
    dm_o[...] = d_m
    low = d_m.astype(LOW)
    d_o = dot_nt(low, wo[...].reshape(D, D)).astype(LOW)
    for t in range(8):
        dob[t] = d_o[:, SPAN * t : SPAN * (t + 1)]
    to_seq, from_seq = [], []
    for j in range(4):
        for i in range(2):
            if (j, i) == (0, 0):
                continue
            k = 2 * j + i
            to_x, back = lax.rem(x + j, 4), lax.rem(x + 4 - j, 4)
            to_c = lax.rem(core + i, 2)
            sems = (a_send.at[k], a_recv.at[k])
            to_seq.append(remote(dob.at[2 * to_x + to_c], do_all.at[me], *sems, x=to_x, core=to_c))
            to_seq[-1].start()
            land_o = do_all.at[2 * back + to_c]
            from_seq.append(remote(land_o, land_o, *sems, x=back, core=to_c))
    own_o = pltpu.make_async_copy(dob.at[me], do_all.at[me], loc.at[7])
    own_o.start()
    small_o[...] = jnp.zeros_like(small_o)
    small_o[0:1, :] = jnp.sum(low.astype(F32), axis=0, keepdims=True)
    small_o[1:2, :] = jnp.sum(d_n2 * white, axis=0, keepdims=True)
    small_o[2:3, :] = jnp.sum(d_n2, axis=0, keepdims=True)
    small_o[3:4, :] = jnp.sum(c_own, axis=0, keepdims=True)
    left = jnp.concatenate([os[t, own_rows, :] for t in range(8)], axis=1)
    g_out = dot_tn(left, low).astype(LOW)
    for t in range(8):
        gop_o[t] = g_out[:, SPAN * t : SPAN * (t + 1)]
    for copy in from_seq:
        copy.wait_recv()
    for copy in to_seq + to_y:
        copy.wait_send()
    own_o.wait()
    out_copy.wait()
    gather.sent()
    reduce.sent()


def hidden_layer(o_all, x_all, cot, wo_a, wo_b, wf, wpz, bo, gain, shift, bf):
    outs = [
        (shaped((TOK, D), LOW), ANYWHERE),
        (shaped((OWN, D), F32), IN_VMEM),
        (shaped((OWN, D), F32), IN_VMEM),
        (shaped((8, OWN, SPAN), LOW), ANYWHERE),
        (shaped((D, HIDDEN), LOW), IN_VMEM),
        (shaped((HIDDEN, D), LOW), IN_VMEM),
        (shaped((8, D, SPAN), LOW), IN_VMEM),
        (shaped((8, D), F32), IN_VMEM),
        (shaped((8, HIDDEN), F32), IN_VMEM),
    ]
    scratch = [
        pltpu.VMEM((TOK, D), LOW),
        pltpu.VMEM((8, TOK, SPAN), LOW),
        pltpu.VMEM((8, OWN, D), LOW),
        pltpu.VMEM((4, 8, 2, 16, D), LOW),
        pltpu.VMEM((4, 8, 32, HIDDEN), LOW),
        pltpu.VMEM((4, 8, 16, D), LOW),
        pltpu.VMEM((TOK, D), LOW),
        pltpu.VMEM((TOK, HIDDEN), F32),
        pltpu.VMEM((TOK, HIDDEN), LOW),
        pltpu.VMEM((8, OWN, D), LOW),
        pltpu.VMEM((4, OWN, D), LOW),
        pltpu.VMEM((4, OWN, D), LOW),
        pltpu.VMEM((4, OWN, D), LOW),
        pltpu.VMEM((D, HIDDEN), F32),
        pltpu.VMEM((HIDDEN, D), F32),
        pltpu.VMEM((8, OWN, SPAN), LOW),
        DMA((8,)), DMA((8,)), DMA((8,)), DMA((4,)), DMA((4,)), DMA((7,)), DMA((7,)),
        DMA((8,)), DMA((8,)), DMA,
    ]
    ins = [ANYWHERE, ANYWHERE, IN_VMEM] + [ANYWHERE] * 4 + [IN_VMEM] * 4
    return call(hidden_kernel, outs, ins, scratch, "hidden", 3, vmem=60)(
        o_all, x_all, cot, wo_a, wo_b, wf, wpz, bo[None], gain[None], shift[None], bf
    )


def attend_back_kernel(
    qkv, cut_ref, do_ref, o_all, lse, outp, gop, gfc, gproj, mid, bp,
    dqkv_o, out_o, fin_o, gout_o,
    qm, dom, ktm, delta, dq, dk, dv, o_own,
    so, sumo, lo, sg, sumg, lg, yf, yp, zf, zp, f_mid, p_mid,
    o_loc, ro_send, ro_recv, rg_send, rg_recv, y_send, y_recv, z_send, z_recv,
):
    y, z = axis("y"), axis("z")
    me = 2 * axis("x") + axis("core")
    ready = greet(
        [{"x": ahead("x", k, 4)} for k in range(1, 4)]
        + [{"core": 1 - axis("core")}]
        + y_peers()
        + z_peers()
    )
    own = pltpu.make_async_copy(o_all.at[me], o_own, o_loc)
    own.start()
    cut = cut_ref[0, 0]
    for tile in range(4):
        rows = tile_rows(tile)
        q = qkv[rows, :SPAN].astype(F32) * 0.125
        k_t = jnp.transpose(qkv[rows, SPAN : 2 * SPAN].astype(F32))
        d_o = do_ref[rows, :]
        for head in range(2):
            lanes = head_lanes(q.shape, 1, head)
            qm[head, rows, :] = jnp.where(lanes, q, 0.0).astype(LOW)
            dom[head, rows, :] = jnp.where(lanes, d_o.astype(F32), 0.0).astype(LOW)
            ktm[head, :, rows] = jnp.where(head_lanes(k_t.shape, 0, head), k_t, 0.0).astype(LOW)
    dk[...] = jnp.zeros_like(dk)
    dv[...] = jnp.zeros_like(dv)
    ready()
    r_out = Reduce(
        lambda t: outp.at[t], lambda j: so.at[j], lambda j: sumo.at[j], lambda j: lo.at[j],
        ro_send, ro_recv,
    )
    r_gop = Reduce(
        lambda t: gop.at[t], lambda j: sg.at[j], lambda j: sumg.at[j], lambda j: lg.at[j],
        rg_send, rg_recv,
    )
    for j in (1, 3, 2, 0):
        r_out.to_core(j)
        r_gop.to_core(j)
    to_y = []
    for k in range(1, 4):
        to = ahead("y", k, 4)
        for n, (src, dst, rows) in enumerate(((gfc, yf, 256), (gproj, yp, 128))):
            piece = src.at[pl.ds(pl.multiple_of(rows * to, rows), rows)]
            to_y.append(remote(piece, dst.at[k], y_send.at[n, k], y_recv.at[n, k], y=to))
            to_y[-1].start()
    own.wait()
    for tile in range(4):
        rows = tile_rows(tile)
        prod = do_ref[rows, :].astype(F32) * o_own[rows, :].astype(F32)
        for head in range(2):
            ones = jnp.where(head_lanes((8, SPAN), 1, head), 1.0, 0.0)
            sums = lax.dot_general(
                ones, prod, (((1,), (1,)), ((), ())),
                precision=lax.Precision.HIGHEST, preferred_element_type=F32,
            )
            delta[head : head + 1, rows] = sums[0:1]

    def do_tile(tile):
        q_rows = tile_rows(tile)
        free = min(tile, 2)

        def one(k_tile, dq_t, masked):
            rows = tile_rows(k_tile)
            keys, values = qkv[rows, SPAN : 2 * SPAN], qkv[rows, 2 * SPAN :]
            for head in range(2):
                q_h, do_h = qm[head, q_rows, :], dom[head, q_rows, :]
                s = dot_nt(keys, q_h)
                if masked:
                    s = masked_scores(s, cut, tile, k_tile)
                p = jnp.exp(s - lse[head : head + 1, q_rows])
                d_p = dot_nt(values, do_h)
                d_s = (p * (d_p - delta[head : head + 1, q_rows])).astype(LOW)
                dv[rows, :] += dot(p.astype(LOW), do_h)
                dk[rows, :] += dot(d_s, q_h)
                dq_t = dq_t + dot(ktm[head, :, rows], d_s)
            return dq_t

        dq_t = jnp.zeros((SPAN, TILE), F32)
        if free:
            dq_t = lax.fori_loop(0, free, lambda k, d: one(k, d, False), dq_t)
        for k_tile in range(free, tile + 1):
            dq_t = one(k_tile, dq_t, True)
        dq[q_rows, :] = jnp.transpose(dq_t) * 0.125

    do_tile(0)
    for j in (1, 3, 2):
        r_out.to_chip(j)
        r_gop.to_chip(j)
    do_tile(3)
    do_tile(1)
    for copy in to_y:
        copy.wait_recv()
    to_z = []
    for n, (src, dst, mid_ref, rows) in enumerate(((gfc, yf, f_mid, 256), (gproj, yp, p_mid, 128))):
        total = src[pl.ds(pl.multiple_of(rows * y, rows), rows), :].astype(F32)
        for k in range(1, 4):
            total = total + dst[k].astype(F32)
        mid_ref[...] = total.astype(LOW)
        piece_rows = rows // 8
        z_buf = (zf, zp)[n]
        for k in range(1, 8):
            to = ahead("z", k, 8)
            piece = mid_ref.at[pl.ds(pl.multiple_of(piece_rows * to, piece_rows), piece_rows)]
            to_z.append(remote(piece, z_buf.at[k], z_send.at[n, k], z_recv.at[n, k], z=to))
            to_z[-1].start()
    do_tile(2)
    dqkv_o[:, :SPAN] = dq[...].astype(LOW)
    dqkv_o[:, SPAN : 2 * SPAN] = dk[...].astype(LOW)
    dqkv_o[:, 2 * SPAN :] = dv[...].astype(LOW)
    out_o[...] = (mid[...] + r_out.result() + bp[...]).astype(LOW)
    gout_o[...] = r_gop.result().astype(LOW)
    for copy in to_z:
        copy.wait_recv()
    total = p_mid[pl.ds(pl.multiple_of(16 * z, 16), 16), :].astype(F32)
    for k in range(1, 8):
        total = total + zp[k].astype(F32)
    fin_o[0:16, :] = total.astype(LOW)
    total = f_mid[pl.ds(pl.multiple_of(32 * z, 32), 32), :].astype(F32)
    for k in range(1, 8):
        total = total + zf[k].astype(F32)
    fin_o[16:32, :HIDDEN] = total[:16].astype(LOW)
    fin_o[16:32, HIDDEN:] = total[16:].astype(LOW)
    for copy in to_y + to_z:
        copy.wait_send()
    r_out.sent()
    r_gop.sent()


def attend_back(qkv, cut, do_all, o_all, lse, outp, gop, gfc, gproj, mid, bp):
    outs = [
        (shaped((TOK, 3 * SPAN), LOW), IN_VMEM),
        (shaped((OWN, D), LOW), IN_VMEM),
        (shaped((32, D), LOW), IN_VMEM),
        (shaped((D, SPAN), LOW), IN_VMEM),
    ]
    block, g_block = (4, OWN, D), (4, D, SPAN)
    scratch = [
        pltpu.VMEM((2, TOK, SPAN), LOW),
        pltpu.VMEM((2, TOK, SPAN), LOW),
        pltpu.VMEM((2, SPAN, TOK), LOW),
        pltpu.VMEM((2, TOK), F32),
        pltpu.VMEM((TOK, SPAN), F32),
        pltpu.VMEM((TOK, SPAN), F32),
        pltpu.VMEM((TOK, SPAN), F32),
        pltpu.VMEM((TOK, SPAN), LOW),
        pltpu.VMEM(block, LOW), pltpu.VMEM(block, LOW), pltpu.VMEM(block, LOW),
        pltpu.VMEM(g_block, LOW), pltpu.VMEM(g_block, LOW), pltpu.VMEM(g_block, LOW),
        pltpu.VMEM((4, 256, HIDDEN), LOW), pltpu.VMEM((4, 128, D), LOW),
        pltpu.VMEM((8, 32, HIDDEN), LOW), pltpu.VMEM((8, 16, D), LOW),
        pltpu.VMEM((256, HIDDEN), LOW), pltpu.VMEM((128, D), LOW),
        DMA, DMA((7,)), DMA((7,)), DMA((7,)), DMA((7,)),
        DMA((2, 4)), DMA((2, 4)), DMA((2, 8)), DMA((2, 8)),
    ]
    ins = [IN_VMEM, IN_SMEM, IN_VMEM, ANYWHERE] + [IN_VMEM] * 7
    return call(attend_back_kernel, outs, ins, scratch, "attend_back", 4, vmem=60)(
        qkv, cut, do_all.reshape(TOK, SPAN), o_all, lse, outp.reshape(8, OWN, D), gop, gfc, gproj,
        mid, bp[None],
    )


def finish_kernel(
    dqkv, n1, wq, gout, xown, dm, gain, fin_in, small, bfc,
    dtok_o, fin_o, vec_o,
    part, from_core, total, land, gq, gy, gz, g_mid, fin, sums, x_buf, v16, z_buf, y_buf, v_out,
    r_send, r_recv, y_send, y_recv, z_send, z_recv, f_send, f_recv, s_send, s_recv, loc,
):
    x, core, y, z = axis("x"), axis("core"), axis("y"), axis("z")
    me = 2 * x + core
    ready = greet(seq_peers() + y_peers() + z_peers())

    gq[:, : 3 * SPAN] = dot_tn(n1[...], dqkv[...]).astype(LOW)
    gq[:, 3 * SPAN :] = gout[...]
    ready()
    to_y = []
    for k in range(1, 4):
        to = ahead("y", k, 4)
        piece = gq.at[pl.ds(pl.multiple_of(256 * to, 256), 256)]
        to_y.append(remote(piece, gy.at[k], y_send.at[k], y_recv.at[k], y=to))
        to_y[-1].start()
    reduce = Reduce(
        lambda t: part.at[t],
        lambda j: from_core.at[j],
        lambda j: total.at[j],
        lambda j: land.at[j],
        r_send,
        r_recv,
    )

    def one(i, _):
        j = block_order(i)
        chip = lax.rem(x + j, 4)
        d_n1 = dot_nt(dqkv[tile_rows(chip), :], wq[...].reshape(D, 3 * SPAN))
        part[pl.ds(2 * chip, 2)] = d_n1.astype(LOW).reshape(2, OWN, D)
        reduce.to_core(j)

        @pl.when(i >= 1)
        def _():
            reduce.to_chip(block_order(i - 1))

        return 0

    lax.fori_loop(0, 4, one, 0)
    biases = jnp.sum(dqkv[...].astype(F32), axis=0, keepdims=True)
    v16[...] = jnp.zeros_like(v16)
    v16[8:9, :] = biases[:, :SPAN]
    v16[9:10, :] = biases[:, 2 * SPAN :]
    for k in range(4):
        v16[10 + k : 11 + k, :] = bfc[0:1, SPAN * k : SPAN * (k + 1)]
    for copy in to_y:
        copy.wait_recv()
    g_total = gq[pl.ds(pl.multiple_of(256 * y, 256), 256), :].astype(F32)
    for k in range(1, 4):
        g_total = g_total + gy[k].astype(F32)
    g_mid[...] = g_total.astype(LOW)
    to_z = []
    for k in range(1, 8):
        to = ahead("z", k, 8)
        piece = g_mid.at[pl.ds(pl.multiple_of(32 * to, 32), 32)]
        to_z.append(remote(piece, gz.at[k], z_send.at[0, k], z_recv.at[0, k], z=to))
        to_z[-1].start()
    white, inverse = whitened(xown[...].astype(F32))
    for copy in to_z:
        copy.wait_recv()
    g_total = g_mid[pl.ds(pl.multiple_of(32 * z, 32), 32), :].astype(F32)
    for k in range(1, 8):
        g_total = g_total + gz[k].astype(F32)
    fin[0:32, :] = fin_in[...]
    fin[32:48, :HIDDEN] = g_total[:16].astype(LOW)
    fin[32:48, HIDDEN:] = g_total[16:].astype(LOW)

    def spread(src, dst, send, recv):
        copies, waits = [], []
        for j in range(4):
            for i in range(2):
                if (j, i) == (0, 0):
                    continue
                k = 2 * j + i
                to_x, back = lax.rem(x + j, 4), lax.rem(x + 4 - j, 4)
                to_c = lax.rem(core + i, 2)
                sems = (send.at[k], recv.at[k])
                copies.append(
                    remote(src(2 * to_x + to_c), dst.at[me], *sems, x=to_x, core=to_c)
                )
                copies[-1].start()
                landed = dst.at[2 * back + to_c]
                waits.append(remote(landed, landed, *sems, x=back, core=to_c))
        return copies, waits

    fin_copies, fin_waits = spread(lambda t: fin, fin_o, f_send, f_recv)
    own = [pltpu.make_async_copy(fin, fin_o.at[me], loc.at[0])]
    own[0].start()
    d_n1 = reduce.result()
    dtok_o[...] = dm[...] + norm_back(d_n1, gain[...], white, inverse)
    rows = [
        jnp.sum(d_n1 * white, axis=0, keepdims=True),
        jnp.sum(d_n1, axis=0, keepdims=True),
        small[0:4, :],
        jnp.zeros((2, D), F32),
    ]
    rows = jnp.concatenate(rows, axis=0)
    for t in range(8):
        sums[t] = rows[:, SPAN * t : SPAN * (t + 1)]
    copies, waits = spread(lambda t: sums.at[t], x_buf, s_send.at[0], s_recv.at[0])
    x_buf[me] = sums[me]
    for copy in waits:
        copy.wait_recv()
    acc = x_buf[0]
    for k in range(1, 8):
        acc = acc + x_buf[k]
    v16[0:8, :] = acc
    z_buf[z] = v16[...]
    waits = []
    for k in range(1, 8):
        sems = (z_send.at[1, k], z_recv.at[1, k])
        copies.append(remote(v16, z_buf.at[z], *sems, z=ahead("z", k, 8)))
        copies[-1].start()
        back = lax.rem(z + 8 - k, 8)
        waits.append(remote(z_buf.at[back], z_buf.at[back], *sems, z=back))
    for copy in waits:
        copy.wait_recv()
    acc = z_buf[0]
    for k in range(1, 8):
        acc = acc + z_buf[k]
    y_buf[y] = acc
    waits = []
    for k in range(1, 4):
        sems = (y_send.at[3 + k], y_recv.at[3 + k])
        copies.append(remote(y_buf.at[y], y_buf.at[y], *sems, y=ahead("y", k, 4)))
        copies[-1].start()
        back = lax.rem(y + 4 - k, 4)
        waits.append(remote(y_buf.at[back], y_buf.at[back], *sems, y=back))
    for copy in waits:
        copy.wait_recv()
    v_out[...] = ((y_buf[0] + y_buf[1]) + y_buf[2]) + y_buf[3]
    vec_copies, waits = spread(lambda t: v_out, vec_o, s_send.at[1], s_recv.at[1])
    vec_o[me] = v_out[...]
    for copy in waits + fin_waits:
        copy.wait_recv()
    for copy in copies + vec_copies + fin_copies + to_y + to_z:
        copy.wait_send()
    for copy in own:
        copy.wait()
    reduce.sent()


def finish(dqkv, n1, wq, gout, xown, dm, gain, fin_in, small, bfc):
    outs = [
        (shaped((OWN, D), F32), IN_VMEM),
        (shaped((8, 48, D), LOW), IN_VMEM),
        (shaped((8, 16, SPAN), F32), IN_VMEM),
    ]
    block = (4, OWN, D)
    scratch = [
        pltpu.VMEM((8, OWN, D), LOW),
        pltpu.VMEM(block, LOW), pltpu.VMEM(block, LOW), pltpu.VMEM(block, LOW),
        pltpu.VMEM((D, HIDDEN), LOW),
        pltpu.VMEM((4, 256, HIDDEN), LOW),
        pltpu.VMEM((8, 32, HIDDEN), LOW),
        pltpu.VMEM((256, HIDDEN), LOW),
        pltpu.VMEM((48, D), LOW),
        pltpu.VMEM((8, 8, SPAN), F32),
        pltpu.VMEM((8, 8, SPAN), F32),
        pltpu.VMEM((16, SPAN), F32),
        pltpu.VMEM((8, 16, SPAN), F32),
        pltpu.VMEM((4, 16, SPAN), F32),
        pltpu.VMEM((16, SPAN), F32),
        DMA((7,)), DMA((7,)), DMA((7,)), DMA((7,)), DMA((2, 8)), DMA((2, 8)),
        DMA((8,)), DMA((8,)), DMA((2, 8)), DMA((2, 8)), DMA((1,)),
    ]
    return call(finish_kernel, outs, [IN_VMEM] * 10, scratch, "finish", 5)(
        dqkv, n1, wq, gout, xown, dm, gain[None], fin_in, small, bfc
    )


def results_kernel(fin, vec, dtok, out, out_o, dtok_o, gq_o, go_o, gf_o, gp_o, vec_o, bf_o):
    out_o[...] = out[...]
    dtok_o[...] = dtok[...]
    lane = lax.broadcasted_iota(jnp.int32, (40, 128), 1) // 16
    units = []
    for t in range(8):
        gp_o[16 * t : 16 * (t + 1), :] = fin[t, 0:16, :].astype(F32)
        span = slice(SPAN * t, SPAN * (t + 1))
        for half in range(2):
            rows = slice(16 * half, 16 * (half + 1))
            at = HIDDEN * half
            for k in range(3):
                gq_o[rows, D * k + SPAN * t : D * k + SPAN * (t + 1)] = fin[
                    t, 32:48, at + SPAN * k : at + SPAN * (k + 1)
                ].astype(F32)
            go_o[rows, span] = fin[t, 32:48, at + 3 * SPAN : at + 4 * SPAN].astype(F32)
        bias = jnp.concatenate([vec[t, 10 + k : 11 + k, :] for k in range(4)], axis=1)
        units.append(
            jnp.concatenate(
                [
                    fin[t, 16:32, :HIDDEN].astype(F32),
                    fin[t, 16:32, HIDDEN:].astype(F32),
                    jnp.broadcast_to(bias, (8, HIDDEN)),
                ],
                axis=0,
            )
        )
        vec_o[:, span] = vec[t, 0:10, :]
    for s in range(32):
        q, p = s // 8, s % 8
        tile = jnp.zeros((40, 128), F32)
        for t in range(8):
            turned = pltpu.roll(units[t][:, 128 * q : 128 * (q + 1)], (16 * t - 16 * p) % 128, 1)
            tile = jnp.where(lane == t, turned, tile)
        gf_o[:, 128 * s : 128 * (s + 1)] = tile[:32]
        bf_o[:, 128 * s : 128 * (s + 1)] = tile[32:33]


def results(fin, vec, dtok, out):
    outs = [
        ((OWN, D), LOW),
        ((OWN, D), F32),
        ((32, 3 * D), F32),
        ((32, D), F32),
        ((32, 4 * D), F32),
        ((128, D), F32),
        ((10, D), F32),
        ((1, 4 * D), F32),
    ]
    return call(results_kernel, [(shaped(*o), IN_VMEM) for o in outs], [IN_VMEM] * 4, [], "results")(
        fin, vec, dtok, out
    )


def per_device(
    tokens, segment, ln1_gain, ln1_shift, w_qkv, bias_query, bias_value, w_out, bias_out,
    ln2_gain, ln2_shift, w_fc, bias_fc, w_proj, bias_proj, cotangent,
):
    own = tokens[0]
    cut = jnp.sum((segment < 2).astype(jnp.int32)).reshape(1, 1)
    wq, wo, wf, wp, bias, bf = columns(
        w_qkv, w_out, w_fc, w_proj, bias_query, bias_value, bias_fc
    )
    x_all, n1, qkv, wq_all, wo_a, wfz, wpz = qkv_of_heads(
        own, wq, wo, wf, wp, ln1_gain, ln1_shift, bias
    )
    o_all, lse, wo_b, wf_all = attend(qkv, cut, wo_a, wfz)
    outp, mid, dm, do_all, gfc, gproj, gop, small, bfc = hidden_layer(
        o_all, x_all, cotangent[0], wo_a, wo_b, wf_all, wpz, bias_out, ln2_gain, ln2_shift, bf
    )
    dqkv, out, fin_in, gout = attend_back(
        qkv, cut, do_all, o_all, lse, outp, gop, gfc, gproj, mid, bias_proj
    )
    dtok, fin, vec = finish(dqkv, n1, wq_all, gout, own, dm, ln1_gain, fin_in, small, bfc)
    out, dtok, gq, go, gf, gp, vecs, bfs = results(fin, vec, dtok, out)
    return (
        out[None], dtok[None], vecs[0], vecs[1], gq, vecs[8], vecs[9], go, vecs[2], vecs[3],
        vecs[4], gf, bfs[0], gp, vecs[5],
    )


def solution(mesh):
    finer = Mesh(mesh.devices.reshape(4, 2, 4, 8), ("x", "core", "y", "z"))
    rows, whole = P(SHARD, None), P()
    tokens = P(SHARD, SEQ, None)
    return jax.shard_map(
        per_device,
        mesh=finer,
        in_specs=(
            tokens, rows, whole, whole, rows, whole, whole, rows, whole, whole, whole, rows,
            whole, rows, whole, tokens,
        ),
        out_specs=(
            tokens, tokens, whole, whole, rows, whole, whole, rows, whole, whole, whole, rows,
            whole, rows, whole,
        ),
        check_vma=False,
    )
```

```python
import functools

import jax
import jax.numpy as jnp
from jax import lax
from jax.experimental import pallas as pl
from jax.experimental.pallas import tpu as pltpu
from jax.sharding import Mesh
from jax.sharding import PartitionSpec as P

SEQ = ("x", "core")
SHARD = ("y", "z")
F32 = jnp.float32
LOW = jnp.bfloat16
MIB = 2**20
TOK = 2048
OWN = 256
TILE = 512
D = 1024
HIDDEN = 512
SPAN = 128
GELU_A = 0.7978845608028654
GELU_B = 0.044715

IN_VMEM = pl.BlockSpec(memory_space=pltpu.VMEM)
IN_SMEM = pl.BlockSpec(memory_space=pltpu.SMEM)
ANYWHERE = pl.BlockSpec(memory_space=pl.ANY)
DMA = pltpu.SemaphoreType.DMA


def shaped(shape, dtype):
    return jax.ShapeDtypeStruct(shape, dtype)


def remote(src, dst, send, recv, **device):
    return pltpu.make_async_remote_copy(
        src_ref=src,
        dst_ref=dst,
        send_sem=send,
        recv_sem=recv,
        device_id=device,
        device_id_type=pl.DeviceIdType.MESH,
    )


def axis(name):
    return lax.axis_index(name)


def ahead(name, k, count):
    return lax.rem(axis(name) + k, count)


def seq_peers():
    core = axis("core")
    return [
        {"x": ahead("x", j, 4), "core": lax.rem(core + i, 2)}
        for j in range(4)
        for i in range(2)
        if (j, i) != (0, 0)
    ]


def near_peers():
    return [{"x": ahead("x", 1, 4)}, {"x": ahead("x", 3, 4)}, {"core": 1 - axis("core")}]


def y_peers():
    return [{"y": ahead("y", k, 4)} for k in range(1, 4)]


def z_peers():
    return [{"z": ahead("z", k, 8)} for k in range(1, 8)]


def greet(peers):
    sem = pltpu.get_barrier_semaphore()
    for peer in peers:
        pl.semaphore_signal(sem, inc=1, device_id=peer, device_id_type=pl.DeviceIdType.MESH)
    return lambda: pl.semaphore_wait(sem, len(peers))


def dot(a, b):
    return jnp.dot(a, b, preferred_element_type=F32)


def dot_nt(a, b):
    return lax.dot_general(a, b, (((1,), (1,)), ((), ())), preferred_element_type=F32)


def dot_tn(a, b):
    return lax.dot_general(a, b, (((0,), (0,)), ((), ())), preferred_element_type=F32)


def whitened(values):
    mean = jnp.mean(values, axis=-1, keepdims=True)
    centered = values - mean
    spread = jnp.mean(centered * centered, axis=-1, keepdims=True)
    inverse = lax.rsqrt(spread + 1e-05)
    return centered * inverse, inverse


def norm_back(grad, gain, white, inverse):
    d_white = grad * gain
    first = jnp.mean(d_white, axis=-1, keepdims=True)
    second = jnp.mean(d_white * white, axis=-1, keepdims=True)
    return inverse * (d_white - first - white * second)


class Gather:
    def __init__(self, src, at, rows, send, recv, cut=None):
        x, core = axis("x"), axis("core")
        other = 1 - core
        right, far, left = (lax.rem(x + k, 4) for k in (1, 2, 3))
        cut = cut or rows // 2
        low, high = pl.ds(0, cut), pl.ds(cut, rows - cut)
        mine, r, f, l = (at(2 * k + core) for k in (x, right, far, left))
        mine_o, r_o, f_o, l_o = (at(2 * k + other) for k in (x, right, far, left))
        plan = [
            (src, mine, {"x": right}, l),
            (src, mine, {"x": left}, r),
            (src, mine, {"core": other}, mine_o),
            (l.at[low], l.at[low], {"x": right}, f.at[low]),
            (r.at[high], r.at[high], {"x": left}, f.at[high]),
            (l, l, {"core": other}, l_o),
            (r, r, {"core": other}, r_o),
            (f, f, {"core": other}, f_o),
        ]

        def out(k):
            a, b, device, _ = plan[k]
            return remote(a, b, send.at[k], recv.at[k], **device)

        def into(k):
            _, _, device, land = plan[k]
            return remote(land, land, send.at[k], recv.at[k], **device)

        self.out, self.into = out, into
        self.blocks = dict(
            mine=2 * x + core,
            mine_o=2 * x + other,
            left=2 * left + core,
            left_o=2 * left + other,
            right=2 * right + core,
            right_o=2 * right + other,
            far=2 * far + core,
            far_o=2 * far + other,
        )

    def start(self):
        for k in (0, 1, 2):
            self.out(k).start()

    def got(self, k):
        self.into(k).wait_recv()

    def pass_left(self):
        self.got(0)
        self.out(3).start()
        self.out(5).start()

    def pass_right(self):
        self.got(1)
        self.out(4).start()
        self.out(6).start()

    def pass_far(self):
        self.got(3)
        self.got(4)
        self.out(7).start()

    def sent(self):
        for k in range(8):
            self.out(k).wait_send()


class Reduce:
    def __init__(self, part, from_core, total, from_side, land, rows, send, recv):
        self.part, self.from_core, self.total = part, from_core, total
        self.from_side, self.land = from_side, land
        self.send, self.recv = send, recv
        self.x, self.core = axis("x"), axis("core")
        self.half = rows // 2

    def chip(self, j):
        return lax.rem(self.x + j, 4)

    def core_copy(self, j):
        return remote(
            self.part(2 * self.chip(j) + 1 - self.core),
            self.from_core(j),
            self.send.at[j],
            self.recv.at[j],
            core=1 - self.core,
        )

    def side_copy(self, j):
        rows = pl.ds(0 if j == 1 else self.half, self.half)
        n = 4 + j // 2
        return remote(
            self.total(2).at[rows],
            self.from_side(j),
            self.send.at[n],
            self.recv.at[n],
            x=self.chip(j),
        )

    def chip_copy(self, j):
        n = 6 + j // 2
        return remote(self.total(j), self.land(j), self.send.at[n], self.recv.at[n], x=self.chip(j))

    def pair(self, j, rows):
        mine = self.part(2 * self.chip(j) + self.core)
        return mine[rows, :].astype(F32) + self.from_core(j)[rows, :].astype(F32)

    def to_core(self, j):
        self.core_copy(j).start()

    def to_far(self):
        self.core_copy(2).wait_recv()
        self.total(2)[...] = self.pair(2, slice(None)).astype(LOW)
        self.side_copy(1).start()
        self.side_copy(3).start()

    def to_side(self, j):
        self.core_copy(j).wait_recv()
        self.side_copy(j).wait_recv()
        low, high = slice(0, self.half), slice(self.half, 2 * self.half)
        joined, alone = (low, high) if j == 1 else (high, low)
        more = self.from_side(j)[...].astype(F32)
        self.total(j)[joined, :] = (self.pair(j, joined) + more).astype(LOW)
        self.total(j)[alone, :] = self.pair(j, alone).astype(LOW)
        self.chip_copy(j).start()

    def result(self):
        self.core_copy(0).wait_recv()
        total = self.pair(0, slice(None))
        for j in (1, 3):
            self.chip_copy(j).wait_recv()
            total = total + self.land(j)[...].astype(F32)
        return total

    def sent(self):
        for j in range(4):
            self.core_copy(j).wait_send()
        for j in (1, 3):
            self.side_copy(j).wait_send()
            self.chip_copy(j).wait_send()


def call(kernel, outs, ins, scratch, name, number=None, vmem=56):
    extra = {} if number is None else dict(collective_id=number, has_side_effects=True)
    return pl.pallas_call(
        kernel,
        out_shape=[shape for shape, _ in outs],
        in_specs=ins,
        out_specs=[spec for _, spec in outs],
        scratch_shapes=scratch,
        name=name,
        compiler_params=pltpu.CompilerParams(vmem_limit_bytes=vmem * MIB, **extra),
    )


def chosen_units(values, seq):
    lane = lax.broadcasted_iota(jnp.int32, (values.shape[0], 128), 1)
    tiles = []
    for q in range(4):
        tile = jnp.zeros((values.shape[0], 128), F32)
        for p in range(8):
            at = 128 * (8 * q + p)
            shift = lax.rem(16 * p - 16 * seq + 128, 128)
            turned = pltpu.roll(values[:, at : at + 128], shift, 1)
            tile = jnp.where((lane // 16) == p, turned, tile)
        tiles.append(tile)
    return jnp.concatenate(tiles, axis=1)


def columns_kernel(wq, wo, wf, wp, bq, bv, bf, wq_o, wo_o, wf_o, wp_o, bias_o, bf_o):
    core = axis("core")
    seq = 2 * axis("x") + core
    span = pl.ds(pl.multiple_of(SPAN * seq, SPAN), SPAN)
    for k in range(3):
        at = pl.ds(pl.multiple_of(k * D + SPAN * seq, SPAN), SPAN)
        wq_o[:, k * SPAN : (k + 1) * SPAN] = wq[:, at]
    bias_o[:, :SPAN] = bq[:, span]
    bias_o[:, SPAN : 2 * SPAN] = jnp.zeros((1, SPAN), F32)
    bias_o[:, 2 * SPAN :] = bv[:, span]
    wo_o[...] = wo[pl.ds(pl.multiple_of(16 * core, 16), 16), :]
    wp_o[...] = wp[pl.ds(pl.multiple_of(16 * seq, 16), 16), :]
    wf_o[...] = chosen_units(wf[...].astype(F32), seq).astype(LOW)
    bf_o[...] = chosen_units(jnp.broadcast_to(bf[...], (8, 4 * D)), seq)[0:1]


def columns(w_qkv, w_out, w_fc, w_proj, bias_query, bias_value, bias_fc):
    outs = [
        ((32, 3 * SPAN), LOW),
        ((16, D), LOW),
        ((32, HIDDEN), LOW),
        ((16, D), LOW),
        ((1, 3 * SPAN), F32),
        ((1, HIDDEN), F32),
    ]
    return call(
        columns_kernel, [(shaped(*o), IN_VMEM) for o in outs], [IN_VMEM] * 7, [], "columns"
    )(w_qkv, w_out, w_fc, w_proj, bias_query[None], bias_value[None], bias_fc[None])


def head_lanes(shape, dim, head):
    return (lax.broadcasted_iota(jnp.int32, shape, dim) // 64) == head


def masked_scores(scores, cut, q_tile, k_tile):
    shape = scores.shape
    key = k_tile * TILE + lax.broadcasted_iota(jnp.int32, shape, 0)
    query = q_tile * TILE + lax.broadcasted_iota(jnp.int32, shape, 1)
    allowed = key <= query
    if q_tile >= 2:
        allowed = allowed & ((key >= cut) | (query < cut))
    return jnp.where(allowed, scores, -1e30)


def tile_rows(tile):
    if isinstance(tile, int):
        return pl.ds(tile * TILE, TILE)
    return pl.ds(pl.multiple_of(tile * TILE, TILE), TILE)


def middle_kernel(
    x_own, wq, wo_in, wf_in, wp_in, gain1, shift1, bias, cut_ref, cot, bo, gain, shift, bf,
    xall_o, qkv, wq_o,
    o_o, lse, outp, mid_o, dm_o, do_all, gfc_o, gproj_o, gop_o, small_o, bfc_o, woz, wfz, wpz,
    qm, vt, scores, xs, os, cs, wo, wf, wp, n2, da, act, part, from_core, total, from_side, land, dob,
    loc, x_loc, x_send, x_recv, z_send, z_recv, g_send, g_recv, c_send, c_recv, wo_send, wo_recv,
    y_send, y_recv, r_send, r_recv, a_send, a_recv, o_loc,
):
    x, core, y, z = axis("x"), axis("core"), axis("y"), axis("z")
    me = 2 * x + core
    ready = greet(seq_peers() + y_peers() + z_peers())
    cut = cut_ref[0, 0]
    tokens = Gather(x_own, lambda t: xs.at[pl.ds(t * OWN, OWN)], OWN, x_send, x_recv)
    cots = Gather(cot, lambda t: cs.at[t], OWN, c_send, c_recv)
    blocks = tokens.blocks
    half = wo.at[:, :, core]
    own_z = [(wq, wq_o.at[y, z]), (wo_in, woz.at[z]), (wf_in, wfz.at[z]), (wp_in, wpz.at[z])]
    whole_z = [wq_o.at[y], woz, wfz, wpz]
    local = own_z + [(x_own, xs.at[pl.ds(pl.multiple_of(OWN * me, OWN), OWN)]), (cot, cs.at[me])]
    local = [pltpu.make_async_copy(a, b, loc.at[k]) for k, (a, b) in enumerate(local)]
    for copy in local:
        copy.start()
    sends, arrivals, own_y = [], {}, {}

    def along_z(n):
        arrivals["z", n] = []
        own, dst = own_z[n]
        for k in range(1, 8):
            sems = (z_send.at[n, k], z_recv.at[n, k])
            sends.append(remote(own, dst, *sems, z=ahead("z", k, 8)))
            sends[-1].start()
            back = lax.rem(z + 8 - k, 8)
            land_z = whole_z[n].at[back]
            arrivals["z", n].append(remote(land_z, land_z, *sems, z=back))

    def along_y(n):
        arrivals["y", n] = []
        src, to = [(wq_o.at[y], wq_o), (woz, half), (wfz, wf), (wpz, wp)][n]
        for k in range(1, 4):
            sems = (y_send.at[n, k], y_recv.at[n, k])
            sends.append(remote(src, to.at[y], *sems, y=ahead("y", k, 4)))
            sends[-1].start()
            back = lax.rem(y + 4 - k, 4)
            arrivals["y", n].append(remote(to.at[back], to.at[back], *sems, y=back))
        if n:
            own_y[n] = pltpu.make_async_copy(src, to.at[y], loc.at[5 + n])
            own_y[n].start()

    def arrived(*key):
        for copy in arrivals[key]:
            copy.wait_recv()
        if key[0] == "y" and key[1]:
            own_y[key[1]].wait()

    ready()
    along_z(0)
    tokens.start()
    for copy in local:
        copy.wait()
    local = []

    def block_rows(block):
        return pl.ds(pl.multiple_of(OWN * block, OWN), OWN)

    def put(name):
        base = OWN * blocks[name]

        def one(i, _):
            rows = pl.ds(pl.multiple_of(base + i * 128, 128), 128)
            white, _inv = whitened(xs[rows, :].astype(F32))
            n2[rows, :] = (white * gain1[...] + shift1[...]).astype(LOW)
            return 0

        lax.fori_loop(0, OWN // 128, one, 0)
        rows = block_rows(blocks[name])
        n = len(local)
        local.append(pltpu.make_async_copy(xs.at[rows], xall_o.at[rows], x_loc.at[n]))
        local[-1].start()

    def project(name):
        rows = block_rows(blocks[name])
        weights = wq_o[...].reshape(D, 3 * SPAN)
        qkv[rows, :] = (dot(n2[rows, :], weights) + bias[...]).astype(LOW)

    put("mine")
    arrived("z", 0)
    along_y(0)
    along_z(1)
    tokens.got(2)
    put("mine_o")
    arrived("z", 1)
    along_z(2)
    tokens.pass_left()
    tokens.pass_right()
    put("left")
    put("right")
    tokens.got(5)
    put("left_o")
    tokens.got(6)
    put("right_o")
    arrived("y", 0)
    along_y(1)
    for name in ("mine", "mine_o", "left", "right"):
        project(name)
    tokens.pass_far()
    cots.start()
    put("far")
    for name in ("left_o", "right_o", "far"):
        project(name)
    tokens.got(7)
    put("far_o")
    project("far_o")
    arrived("z", 2)
    along_z(3)
    along_y(2)
    for tile in range(4):
        rows = tile_rows(tile)
        q = qkv[rows, :SPAN].astype(F32) * 0.125
        v_t = jnp.transpose(qkv[rows, 2 * SPAN :].astype(F32))
        for head in range(2):
            qm[head, rows, :] = jnp.where(head_lanes(q.shape, 1, head), q, 0.0).astype(LOW)
            vt[head, :, rows] = jnp.where(head_lanes(v_t.shape, 0, head), v_t, 1.0).astype(LOW)

    def heads_of(tile):
        rows = tile_rows(tile)
        return Gather(
            o_o.at[rows], lambda t: os.at[t, rows], TILE, g_send.at[tile], g_recv.at[tile]
        )

    def pass_near(tile):
        gather = heads_of(tile)
        gather.pass_left()
        gather.pass_right()

    for tile in range(4):
        q_rows = tile_rows(tile)
        free = min(tile, 2)
        outs = []
        for head in range(2):

            def score(k_tile, peak, masked, tile=tile, q_rows=q_rows, head=head):
                rows = tile_rows(k_tile)
                s = dot_nt(qkv[rows, SPAN : 2 * SPAN], qm[head, q_rows, :])
                if masked:
                    s = masked_scores(s, cut, tile, k_tile)
                scores[rows, :] = s
                return jnp.maximum(peak, jnp.max(s, axis=0, keepdims=True))

            peak = jnp.full((1, TILE), -3e38, F32)
            for k_tile in range(tile + 1):
                peak = score(k_tile, peak, k_tile >= free)

            sums = jnp.zeros((SPAN, TILE), F32)
            for k_tile in range(tile + 1):
                rows = tile_rows(k_tile)
                e = jnp.exp(scores[rows, :] - peak).astype(LOW)
                sums = sums + dot(vt[head, :, rows], e)
            weight = sums[64:65] if head == 0 else sums[0:1]
            lse[head : head + 1, q_rows] = peak + jnp.log(weight)
            outs.append(sums[64 * head : 64 * (head + 1)] / weight)
        o_o[q_rows, :] = jnp.transpose(jnp.concatenate(outs, axis=0)).astype(LOW)
        keep = pltpu.make_async_copy(o_o.at[q_rows], os.at[me, q_rows], o_loc.at[tile])
        keep.start()
        local.append(keep)
        heads_of(tile).start()
        if tile >= 1:
            pass_near(tile - 1)
        if tile >= 2:
            heads_of(tile - 2).pass_far()
        if tile == 1:
            arrived("y", 1)
            to_core = remote(half, half, wo_send, wo_recv, core=1 - core)
            to_core.start()
        if tile == 2:
            arrived("z", 3)
            along_y(3)
        if tile == 3:
            cots.pass_left()
            cots.pass_right()
    for copy in local:
        copy.wait()
    tokens.sent()
    to_core.wait_recv()
    arrived("y", 2)

    def middle_of(rows):
        left = jnp.concatenate([os[t, rows, :] for t in range(8)], axis=1)
        return xs[rows, :].astype(F32) + dot(left, wo[...].reshape(D, D)) + bo[...]

    def forward(b, _):
        rows = tile_rows(b)
        gather = heads_of(b)

        @pl.when(b == 1)
        def _():
            heads_of(2).pass_far()
            pass_near(3)

        @pl.when(b == 3)
        def _():
            heads_of(3).pass_far()
            cots.pass_far()

        for k in (2, 5, 6, 7):
            gather.got(k)
        white, _inv = whitened(middle_of(rows))
        low = (white * gain[...] + shift[...]).astype(LOW)
        n2[rows, :] = low
        v = dot(low, wf[...].reshape(D, HIDDEN)) + bf[...]
        square = v * v
        t = jnp.tanh(GELU_A * v * (1.0 + GELU_B * square))
        half = 0.5 * (1.0 + t)
        act[rows, :] = (v * half).astype(LOW)
        slope = 0.5 * GELU_A * (1.0 + 3.0 * GELU_B * square)
        da[rows, :] = (half + v * (1.0 - t * t) * slope).astype(LOW)
        return 0

    lax.fori_loop(0, 4, forward, 0)
    arrived("y", 3)
    for k in (2, 5, 6, 7):
        cots.got(k)
    reduce = Reduce(
        lambda t: part.at[t],
        lambda j: from_core.at[j],
        lambda j: total.at[j - 1],
        lambda j: from_side.at[j // 2],
        lambda j: land.at[j // 2],
        OWN,
        r_send,
        r_recv,
    )
    weights = wp[...].reshape(HIDDEN, D)
    bfc_o[...] = jnp.zeros_like(bfc_o)

    def backward(j):
        chip = lax.rem(x + j, 4)
        rows = tile_rows(chip)
        c_low = cs[pl.ds(2 * chip, 2)].reshape(TILE, D)
        low = (dot_nt(c_low, weights) * da[rows, :].astype(F32)).astype(LOW)
        da[rows, :] = low
        bfc_o[0:1, :] += jnp.sum(low.astype(F32), axis=0, keepdims=True)
        d_n2 = dot_nt(low, wf[...].reshape(D, HIDDEN))
        part[pl.ds(2 * chip, 2)] = d_n2.astype(LOW).reshape(2, OWN, D)

    order = (2, 1, 3, 0)

    def back_step(i, _):
        j = jnp.where(i == 0, 2, jnp.where(i == 1, 1, jnp.where(i == 2, 3, 0)))
        backward(j)
        for n, j in enumerate(order):

            @pl.when(i == n)
            def _(n=n, j=j):
                reduce.to_core(j)
                if n == 1:
                    reduce.to_far()
                if n == 3:
                    reduce.to_side(1)
                    reduce.to_side(3)

        return 0

    lax.fori_loop(0, 4, back_step, 0)
    own_rows = pl.ds(pl.multiple_of(me * OWN, OWN), OWN)
    middle = middle_of(own_rows)
    mid_o[...] = middle
    gproj_o[...] = dot_tn(act[...], cs[...].reshape(TOK, D)).astype(LOW)
    gfc_o[...] = dot_tn(n2[...], da[...]).astype(LOW)

    def output_part(b, _):
        rows = tile_rows(b)
        xs[rows, :] = dot(act[rows, :], weights).astype(LOW)
        return 0

    lax.fori_loop(0, 4, output_part, 0)
    out_copy = pltpu.make_async_copy(xs, outp, o_loc.at[0])
    out_copy.start()
    white, inverse = whitened(mid_o[...])
    c_own = cot[...].astype(F32)
    d_n2 = reduce.result()
    d_m = c_own + norm_back(d_n2, gain[...], white, inverse)
    dm_o[...] = d_m
    low = d_m.astype(LOW)
    d_o = dot_nt(low, wo[...].reshape(D, D)).astype(LOW)
    for t in range(8):
        dob[t] = d_o[:, SPAN * t : SPAN * (t + 1)]
    to_seq, from_seq = [], []
    for j in range(4):
        for i in range(2):
            if (j, i) == (0, 0):
                continue
            k = 2 * j + i
            to_x, back = lax.rem(x + j, 4), lax.rem(x + 4 - j, 4)
            to_c = lax.rem(core + i, 2)
            sems = (a_send.at[k], a_recv.at[k])
            to_seq.append(remote(dob.at[2 * to_x + to_c], do_all.at[me], *sems, x=to_x, core=to_c))
            to_seq[-1].start()
            land_o = do_all.at[2 * back + to_c]
            from_seq.append(remote(land_o, land_o, *sems, x=back, core=to_c))
    own_o = pltpu.make_async_copy(dob.at[me], do_all.at[me], loc.at[0])
    own_o.start()
    small_o[...] = jnp.zeros_like(small_o)
    small_o[0:1, :] = jnp.sum(low.astype(F32), axis=0, keepdims=True)
    small_o[1:2, :] = jnp.sum(d_n2 * white, axis=0, keepdims=True)
    small_o[2:3, :] = jnp.sum(d_n2, axis=0, keepdims=True)
    small_o[3:4, :] = jnp.sum(c_own, axis=0, keepdims=True)
    left = jnp.concatenate([os[t, own_rows, :] for t in range(8)], axis=1)
    g_out = dot_tn(left, low).astype(LOW)
    for t in range(8):
        gop_o[t] = g_out[:, SPAN * t : SPAN * (t + 1)]
    for copy in from_seq:
        copy.wait_recv()
    for copy in to_seq + sends + [to_core]:
        copy.wait_send()
    own_o.wait()
    out_copy.wait()
    cots.sent()
    for tile in range(4):
        heads_of(tile).sent()
    reduce.sent()


def middle(x, wq, wo, wf, wp, gain1, shift1, bias, cut, cot, bo, gain, shift, bf):
    outs = [
        (shaped((TOK, D), LOW), ANYWHERE),
        (shaped((TOK, 3 * SPAN), LOW), IN_VMEM),
        (shaped((4, 8, 32, 3 * SPAN), LOW), IN_VMEM),
        (shaped((TOK, SPAN), LOW), IN_VMEM),
        (shaped((2, TOK), F32), IN_VMEM),
        (shaped((TOK, D), LOW), ANYWHERE),
        (shaped((OWN, D), F32), IN_VMEM),
        (shaped((OWN, D), F32), IN_VMEM),
        (shaped((8, OWN, SPAN), LOW), ANYWHERE),
        (shaped((D, HIDDEN), LOW), IN_VMEM),
        (shaped((HIDDEN, D), LOW), IN_VMEM),
        (shaped((8, D, SPAN), LOW), IN_VMEM),
        (shaped((8, D), F32), IN_VMEM),
        (shaped((8, HIDDEN), F32), IN_VMEM),
        (shaped((8, 16, D), LOW), ANYWHERE),
        (shaped((8, 32, HIDDEN), LOW), ANYWHERE),
        (shaped((8, 16, D), LOW), ANYWHERE),
    ]
    scratch = [
        pltpu.VMEM((2, TOK, SPAN), LOW),
        pltpu.VMEM((2, SPAN, TOK), LOW),
        pltpu.VMEM((TOK, TILE), F32),
        pltpu.VMEM((TOK, D), LOW),
        pltpu.VMEM((8, TOK, SPAN), LOW),
        pltpu.VMEM((8, OWN, D), LOW),
        pltpu.VMEM((4, 8, 2, 16, D), LOW),
        pltpu.VMEM((4, 8, 32, HIDDEN), LOW),
        pltpu.VMEM((4, 8, 16, D), LOW),
        pltpu.VMEM((TOK, D), LOW),
        pltpu.VMEM((TOK, HIDDEN), LOW),
        pltpu.VMEM((TOK, HIDDEN), LOW),
        pltpu.VMEM((8, OWN, D), LOW),
        pltpu.VMEM((4, OWN, D), LOW),
        pltpu.VMEM((3, OWN, D), LOW),
        pltpu.VMEM((2, OWN // 2, D), LOW),
        pltpu.VMEM((2, OWN, D), LOW),
        pltpu.VMEM((8, OWN, SPAN), LOW),
        DMA((9,)), DMA((8,)), DMA((8,)), DMA((8,)), DMA((4, 8)), DMA((4, 8)),
        DMA((4, 8)), DMA((4, 8)), DMA((8,)), DMA((8,)), DMA, DMA,
        DMA((4, 4)), DMA((4, 4)), DMA((8,)), DMA((8,)), DMA((8,)), DMA((8,)), DMA((4,)),
    ]
    ins = [IN_VMEM] * 8 + [IN_SMEM] + [IN_VMEM] * 5
    outs = call(middle_kernel, outs, ins, scratch, "middle", 2, vmem=60)(
        x, wq, wo, wf, wp, gain1[None], shift1[None], bias, cut, cot, bo[None], gain[None],
        shift[None], bf,
    )
    return outs[:14]


def ending_kernel(
    qkv, cut_ref, do_ref, o_own, lse, outp_in, x_all, gop, gfc, gproj, wq, gain, shift, small, bfc,
    out_o, dn1_o, fin_o, vec_o,
    qm, dom, ktm, delta, dqt, dk, dv, dqkv, outp, xs, part, g_acc, gq, rows1,
    so, sumo, eo, lo, sg, sumg, eg, lg, sn, sumn, en, ln, yf, yp, zf, zp, f_mid, p_mid,
    gy, gz, g_mid, fin, sums, x_buf, v16, z_buf, y_buf, v_out,
    loc, ro_send, ro_recv, rg_send, rg_recv, rn_send, rn_recv, y_send, y_recv, z_send, z_recv,
    f_send, f_recv, s_send, s_recv,
):
    x, core, y, z = axis("x"), axis("core"), axis("y"), axis("z")
    me = 2 * x + core
    ready = greet(seq_peers() + y_peers() + z_peers())
    local = [pltpu.make_async_copy(outp_in, outp, loc.at[0])]
    local.append(pltpu.make_async_copy(x_all, xs, loc.at[1]))
    for copy in local:
        copy.start()
    cut = cut_ref[0, 0]

    def prepare(tile, _):
        rows = tile_rows(tile)
        q = qkv[rows, :SPAN].astype(F32) * 0.125
        k_t = jnp.transpose(qkv[rows, SPAN : 2 * SPAN].astype(F32))
        d_o = do_ref[rows, :].astype(F32)
        prod = d_o * o_own[rows, :].astype(F32)
        for head in range(2):
            lanes = head_lanes(q.shape, 1, head)
            qm[head, rows, :] = jnp.where(lanes, q, 0.0).astype(LOW)
            dom[head, rows, :] = jnp.where(lanes, d_o, 0.0).astype(LOW)
            ktm[head, :, rows] = jnp.where(head_lanes(k_t.shape, 0, head), k_t, 0.0).astype(LOW)
            ones = jnp.where(head_lanes((8, SPAN), 1, head), 1.0, 0.0)
            dots = lax.dot_general(
                ones, prod, (((1,), (1,)), ((), ())),
                precision=lax.Precision.HIGHEST, preferred_element_type=F32,
            )
            delta[head : head + 1, rows] = dots[0:1]
        return 0

    lax.fori_loop(0, 4, prepare, 0)
    for ref in (dqt, dk, dv, g_acc, rows1, v16):
        ref[...] = jnp.zeros_like(ref)
    ready()
    for copy in local:
        copy.wait()
    r_out = Reduce(
        lambda t: outp.at[t], lambda j: so.at[j], lambda j: sumo.at[j - 1], lambda j: eo.at[j // 2],
        lambda j: lo.at[j // 2], OWN, ro_send, ro_recv,
    )
    r_gop = Reduce(
        lambda t: gop.at[t], lambda j: sg.at[j], lambda j: sumg.at[j - 1], lambda j: eg.at[j // 2],
        lambda j: lg.at[j // 2], D, rg_send, rg_recv,
    )
    r_dn1 = Reduce(
        lambda t: part.at[t], lambda j: sn.at[j], lambda j: sumn.at[j - 1], lambda j: en.at[j // 2],
        lambda j: ln.at[j // 2], OWN, rn_send, rn_recv,
    )
    for j in (2, 1, 3, 0):
        r_gop.to_core(j)
        r_out.to_core(j)
    to_y = []
    for k in range(1, 4):
        peer = ahead("y", k, 4)
        for n, (src, dst, rows) in enumerate(((gfc, yf, 256), (gproj, yp, 128))):
            piece = src.at[pl.ds(pl.multiple_of(rows * peer, rows), rows)]
            to_y.append(remote(piece, dst.at[k], y_send.at[n, k], y_recv.at[n, k], y=peer))
            to_y[-1].start()

    def order(n):
        j = jnp.where(n == 0, 2, jnp.where(n == 1, 1, jnp.where(n == 2, 3, 0)))
        return lax.rem(x + j, 4)

    def pair(first, second):
        q_tile, k_tile = jnp.maximum(first, second), jnp.minimum(first, second)
        q_rows, k_rows = tile_rows(q_tile), tile_rows(k_tile)
        keys, values = qkv[k_rows, SPAN : 2 * SPAN], qkv[k_rows, 2 * SPAN :]
        key = k_tile * TILE + lax.broadcasted_iota(jnp.int32, (TILE, 1), 0)
        query = q_tile * TILE + lax.broadcasted_iota(jnp.int32, (1, TILE), 1)
        key_code = jnp.where((key >= TOK // 2) & (key < cut), 1, 0)
        query_code = jnp.where(query >= cut, 1, 2)
        allowed = (key <= query) & (key_code < query_code)
        for head in range(2):
            q_h, do_h = qm[head, q_rows, :], dom[head, q_rows, :]
            s = jnp.where(allowed, dot_nt(keys, q_h), -1e30)
            p = jnp.exp(s - lse[head : head + 1, q_rows])
            d_p = dot_nt(values, do_h)
            d_s = (p * (d_p - delta[head : head + 1, q_rows])).astype(LOW)
            dv[k_rows, :] += dot(p.astype(LOW), do_h)
            dk[k_rows, :] += dot(d_s, q_h)
            dqt[q_tile] += dot(ktm[head, :, k_rows], d_s)

    def complete(tile):
        rows = tile_rows(tile)
        low = jnp.concatenate(
            [jnp.transpose(dqt[tile]) * 0.125, dk[rows, :], dv[rows, :]], axis=1
        ).astype(LOW)
        dqkv[rows, :] = low
        d_n1 = dot_nt(low, wq[...].reshape(D, 3 * SPAN))
        part[pl.ds(2 * tile, 2)] = d_n1.astype(LOW).reshape(2, OWN, D)

    def account(tile):
        rows = tile_rows(tile)
        low = dqkv[rows, :]
        white, _inv = whitened(xs[rows, :].astype(F32))
        n1 = (white * gain[...] + shift[...]).astype(LOW)
        d_n1 = part[pl.ds(2 * tile, 2)].reshape(TILE, D).astype(F32)
        rows1[0:1, :] += jnp.sum(d_n1 * white, axis=0, keepdims=True)
        rows1[1:2, :] += jnp.sum(d_n1, axis=0, keepdims=True)
        wide = low.astype(F32)
        v16[8:9, :] += jnp.sum(wide[:, :SPAN], axis=0, keepdims=True)
        v16[9:10, :] += jnp.sum(wide[:, 2 * SPAN :], axis=0, keepdims=True)
        g_acc[...] += dot_tn(n1, low)

    def summed(own, others, count):
        total = own.astype(F32)
        for k in range(1, count):
            total = total + others[k].astype(F32)
        return total

    to_z = []

    def reduced_y():
        for copy in to_y:
            copy.wait_recv()
        lists = ((gfc, yf, f_mid, zf, 256), (gproj, yp, p_mid, zp, 128))
        for n, (src, dst, mid_ref, z_land, rows) in enumerate(lists):
            own = src[pl.ds(pl.multiple_of(rows * y, rows), rows), :]
            mid_ref[...] = summed(own, dst, 4).astype(LOW)
            share = rows // 8
            for k in range(1, 8):
                peer = ahead("z", k, 8)
                piece = mid_ref.at[pl.ds(pl.multiple_of(share * peer, share), share)]
                to_z.append(remote(piece, z_land.at[k], z_send.at[n, k], z_recv.at[n, k], z=peer))
                to_z[-1].start()

    for step, j in enumerate((2, 1, 3, 0)):
        tile = order(step)

        def one(r, _, tile=tile):
            pair(tile, order(r))
            return 0

        lax.fori_loop(step, 4, one, 0)
        if step == 0:
            r_gop.to_far()
            r_out.to_far()
        if step == 1:
            for side in (1, 3):
                r_gop.to_side(side)
                r_out.to_side(side)
        complete(tile)
        r_dn1.to_core(j)
        if step == 1:
            r_dn1.to_far()
        if step == 3:
            r_dn1.to_side(1)
            r_dn1.to_side(3)
        account(tile)
        if step == 2:
            reduced_y()

    gq[:, : 3 * SPAN] = g_acc[...].astype(LOW)
    gq[:, 3 * SPAN :] = r_gop.result().astype(LOW)
    gq_y = []
    for k in range(1, 4):
        peer = ahead("y", k, 4)
        piece = gq.at[pl.ds(pl.multiple_of(256 * peer, 256), 256)]
        gq_y.append(remote(piece, gy.at[k], y_send.at[2, k], y_recv.at[2, k], y=peer))
        gq_y[-1].start()

    def spread(src, dst, send, recv):
        copies, waits = [], []
        for j in range(4):
            for i in range(2):
                if (j, i) == (0, 0):
                    continue
                k = 2 * j + i
                to_x, back = lax.rem(x + j, 4), lax.rem(x + 4 - j, 4)
                to_c = lax.rem(core + i, 2)
                sems = (send.at[k], recv.at[k])
                copies.append(remote(src(2 * to_x + to_c), dst.at[me], *sems, x=to_x, core=to_c))
                copies[-1].start()
                landed = dst.at[2 * back + to_c]
                waits.append(remote(landed, landed, *sems, x=back, core=to_c))
        return copies, waits

    vectors = jnp.concatenate([rows1[0:2, :], small[0:4, :], jnp.zeros((2, D), F32)], axis=0)
    for t in range(8):
        sums[t] = vectors[:, SPAN * t : SPAN * (t + 1)]
    copies, waits = spread(lambda t: sums.at[t], x_buf, s_send.at[0], s_recv.at[0])
    x_buf[me] = sums[me]
    out_o[...] = r_out.result()
    for copy in to_z:
        copy.wait_recv()
    fin[0:16, :] = summed(p_mid[pl.ds(pl.multiple_of(16 * z, 16), 16), :], zp, 8).astype(LOW)
    total = summed(f_mid[pl.ds(pl.multiple_of(32 * z, 32), 32), :], zf, 8)
    fin[16:32, :HIDDEN] = total[:16].astype(LOW)
    fin[16:32, HIDDEN:] = total[16:].astype(LOW)
    for k in range(4):
        v16[10 + k : 11 + k, :] = bfc[0:1, SPAN * k : SPAN * (k + 1)]
    for copy in waits:
        copy.wait_recv()
    v16[0:8, :] = summed(x_buf[0], x_buf, 8)
    z_buf[z] = v16[...]
    waits = []
    for k in range(1, 8):
        sems = (z_send.at[3, k], z_recv.at[3, k])
        copies.append(remote(v16, z_buf.at[z], *sems, z=ahead("z", k, 8)))
        copies[-1].start()
        back = lax.rem(z + 8 - k, 8)
        waits.append(remote(z_buf.at[back], z_buf.at[back], *sems, z=back))
    for copy in gq_y:
        copy.wait_recv()
    own = gq[pl.ds(pl.multiple_of(256 * y, 256), 256), :]
    g_mid[...] = summed(own, gy, 4).astype(LOW)
    gq_z = []
    for k in range(1, 8):
        peer = ahead("z", k, 8)
        piece = g_mid.at[pl.ds(pl.multiple_of(32 * peer, 32), 32)]
        gq_z.append(remote(piece, gz.at[k], z_send.at[2, k], z_recv.at[2, k], z=peer))
        gq_z[-1].start()
    for copy in waits:
        copy.wait_recv()
    y_buf[y] = summed(z_buf[0], z_buf, 8)
    waits = []
    for k in range(1, 4):
        sems = (y_send.at[3, k], y_recv.at[3, k])
        copies.append(remote(y_buf.at[y], y_buf.at[y], *sems, y=ahead("y", k, 4)))
        copies[-1].start()
        back = lax.rem(y + 4 - k, 4)
        waits.append(remote(y_buf.at[back], y_buf.at[back], *sems, y=back))
    for copy in gq_z:
        copy.wait_recv()
    total = summed(g_mid[pl.ds(pl.multiple_of(32 * z, 32), 32), :], gz, 8)
    fin[32:48, :HIDDEN] = total[:16].astype(LOW)
    fin[32:48, HIDDEN:] = total[16:].astype(LOW)
    finals = Gather(fin, lambda t: fin_o.at[t], 48, f_send, f_recv, cut=32)
    finals.start()
    own_fin = pltpu.make_async_copy(fin, fin_o.at[me], loc.at[2])
    own_fin.start()
    for copy in waits:
        copy.wait_recv()
    v_out[...] = summed(y_buf[0], y_buf, 4)
    vec_copies, waits = spread(lambda t: v_out, vec_o, s_send.at[1], s_recv.at[1])
    vec_o[me] = v_out[...]
    finals.pass_left()
    finals.pass_right()
    dn1_o[...] = r_dn1.result()
    finals.pass_far()
    for k in (2, 5, 6, 7):
        finals.got(k)
    for copy in waits:
        copy.wait_recv()
    for copy in copies + vec_copies + to_y + to_z + gq_y + gq_z:
        copy.wait_send()
    own_fin.wait()
    finals.sent()
    for reduce in (r_out, r_gop, r_dn1):
        reduce.sent()


def reduce_scratch(rows, columns):
    return [
        pltpu.VMEM((4, rows, columns), LOW),
        pltpu.VMEM((3, rows, columns), LOW),
        pltpu.VMEM((2, rows // 2, columns), LOW),
        pltpu.VMEM((2, rows, columns), LOW),
    ]


def ending(qkv, cut, d_o, o_own, lse, outp, x_all, gop, gfc, gproj, wq, gain, shift, small, bfc):
    outs = [
        (shaped((OWN, D), F32), IN_VMEM),
        (shaped((OWN, D), F32), IN_VMEM),
        (shaped((8, 48, D), LOW), IN_VMEM),
        (shaped((8, 16, SPAN), F32), IN_VMEM),
    ]
    scratch = [
        pltpu.VMEM((2, TOK, SPAN), LOW),
        pltpu.VMEM((2, TOK, SPAN), LOW),
        pltpu.VMEM((2, SPAN, TOK), LOW),
        pltpu.VMEM((2, TOK), F32),
        pltpu.VMEM((4, SPAN, TILE), F32),
        pltpu.VMEM((TOK, SPAN), F32),
        pltpu.VMEM((TOK, SPAN), F32),
        pltpu.VMEM((TOK, 3 * SPAN), LOW),
        pltpu.VMEM((8, OWN, D), LOW),
        pltpu.VMEM((TOK, D), LOW),
        pltpu.VMEM((8, OWN, D), LOW),
        pltpu.VMEM((D, 3 * SPAN), F32),
        pltpu.VMEM((D, HIDDEN), LOW),
        pltpu.VMEM((8, D), F32),
        *reduce_scratch(OWN, D), *reduce_scratch(D, SPAN), *reduce_scratch(OWN, D),
        pltpu.VMEM((4, 256, HIDDEN), LOW), pltpu.VMEM((4, 128, D), LOW),
        pltpu.VMEM((8, 32, HIDDEN), LOW), pltpu.VMEM((8, 16, D), LOW),
        pltpu.VMEM((256, HIDDEN), LOW), pltpu.VMEM((128, D), LOW),
        pltpu.VMEM((4, 256, HIDDEN), LOW),
        pltpu.VMEM((8, 32, HIDDEN), LOW),
        pltpu.VMEM((256, HIDDEN), LOW),
        pltpu.VMEM((48, D), LOW),
        pltpu.VMEM((8, 8, SPAN), F32),
        pltpu.VMEM((8, 8, SPAN), F32),
        pltpu.VMEM((16, SPAN), F32),
        pltpu.VMEM((8, 16, SPAN), F32),
        pltpu.VMEM((4, 16, SPAN), F32),
        pltpu.VMEM((16, SPAN), F32),
        DMA((3,)), DMA((8,)), DMA((8,)), DMA((8,)), DMA((8,)), DMA((8,)), DMA((8,)),
        DMA((4, 4)), DMA((4, 4)), DMA((4, 8)), DMA((4, 8)),
        DMA((8,)), DMA((8,)), DMA((2, 8)), DMA((2, 8)),
    ]
    ins = [IN_VMEM, IN_SMEM] + [IN_VMEM] * 3 + [ANYWHERE] * 2 + [IN_VMEM] * 8
    return call(ending_kernel, outs, ins, scratch, "ending", 4, vmem=60)(
        qkv, cut, d_o.reshape(TOK, SPAN), o_own, lse, outp.reshape(8, OWN, D), x_all, gop, gfc,
        gproj, wq, gain[None], shift[None], small, bfc,
    )


def results_kernel(
    fin, vec, dn1, out, mid, dm, x_own, gain, bp,
    out_o, dtok_o, gq_o, go_o, gf_o, gp_o, vec_o, bf_o,
):
    out_o[...] = (mid[...] + out[...] + bp[...]).astype(LOW)
    white, inverse = whitened(x_own[...].astype(F32))
    dtok_o[...] = dm[...] + norm_back(dn1[...], gain[...], white, inverse)
    lane = lax.broadcasted_iota(jnp.int32, (40, 128), 1) // 16
    units = []
    for t in range(8):
        gp_o[16 * t : 16 * (t + 1), :] = fin[t, 0:16, :].astype(F32)
        span = slice(SPAN * t, SPAN * (t + 1))
        for half in range(2):
            rows = slice(16 * half, 16 * (half + 1))
            at = HIDDEN * half
            for k in range(3):
                gq_o[rows, D * k + SPAN * t : D * k + SPAN * (t + 1)] = fin[
                    t, 32:48, at + SPAN * k : at + SPAN * (k + 1)
                ].astype(F32)
            go_o[rows, span] = fin[t, 32:48, at + 3 * SPAN : at + 4 * SPAN].astype(F32)
        bias = jnp.concatenate([vec[t, 10 + k : 11 + k, :] for k in range(4)], axis=1)
        units.append(
            jnp.concatenate(
                [
                    fin[t, 16:32, :HIDDEN].astype(F32),
                    fin[t, 16:32, HIDDEN:].astype(F32),
                    jnp.broadcast_to(bias, (8, HIDDEN)),
                ],
                axis=0,
            )
        )
        vec_o[:, span] = vec[t, 0:10, :]
    for s in range(32):
        q, p = s // 8, s % 8
        tile = jnp.zeros((40, 128), F32)
        for t in range(8):
            turned = pltpu.roll(units[t][:, 128 * q : 128 * (q + 1)], (16 * t - 16 * p) % 128, 1)
            tile = jnp.where(lane == t, turned, tile)
        gf_o[:, 128 * s : 128 * (s + 1)] = tile[:32]
        bf_o[:, 128 * s : 128 * (s + 1)] = tile[32:33]


def results(fin, vec, dn1, out, mid, dm, x_own, gain, bp):
    outs = [
        ((OWN, D), LOW),
        ((OWN, D), F32),
        ((32, 3 * D), F32),
        ((32, D), F32),
        ((32, 4 * D), F32),
        ((128, D), F32),
        ((10, D), F32),
        ((1, 4 * D), F32),
    ]
    return call(results_kernel, [(shaped(*o), IN_VMEM) for o in outs], [IN_VMEM] * 9, [], "results")(
        fin, vec, dn1, out, mid, dm, x_own, gain[None], bp[None]
    )


def per_device(
    tokens, segment, ln1_gain, ln1_shift, w_qkv, bias_query, bias_value, w_out, bias_out,
    ln2_gain, ln2_shift, w_fc, bias_fc, w_proj, bias_proj, cotangent,
):
    own = tokens[0]
    cut = jnp.sum((segment < 2).astype(jnp.int32)).reshape(1, 1)
    wq, wo, wf, wp, bias, bf = columns(
        w_qkv, w_out, w_fc, w_proj, bias_query, bias_value, bias_fc
    )
    x_all, qkv, wq_all, o_own, lse, outp, mid, dm, do_all, gfc, gproj, gop, small, bfc = middle(
        own, wq, wo, wf, wp, ln1_gain, ln1_shift, bias, cut, cotangent[0], bias_out, ln2_gain,
        ln2_shift, bf,
    )
    out_sum, dn1, fin, vec = ending(
        qkv, cut, do_all, o_own, lse, outp, x_all, gop, gfc, gproj, wq_all, ln1_gain, ln1_shift,
        small, bfc,
    )
    out, dtok, gq, go, gf, gp, vecs, bfs = results(
        fin, vec, dn1, out_sum, mid, dm, own, ln1_gain, bias_proj
    )
    return (
        out[None], dtok[None], vecs[0], vecs[1], gq, vecs[8], vecs[9], go, vecs[2], vecs[3],
        vecs[4], gf, bfs[0], gp, vecs[5],
    )


def solution(mesh):
    finer = Mesh(mesh.devices.reshape(4, 2, 4, 8), ("x", "core", "y", "z"))
    rows, whole = P(SHARD, None), P()
    tokens = P(SHARD, SEQ, None)
    return jax.shard_map(
        per_device,
        mesh=finer,
        in_specs=(
            tokens, rows, whole, whole, rows, whole, whole, rows, whole, whole, whole, rows,
            whole, rows, whole, tokens,
        ),
        out_specs=(
            tokens, tokens, whole, whole, rows, whole, whole, rows, whole, whole, whole, rows,
            whole, rows, whole,
        ),
        check_vma=False,
    )
```

```python
import functools

import jax
import jax.numpy as jnp
from jax import lax
from jax.experimental import pallas as pl
from jax.experimental.pallas import tpu as pltpu
from jax.sharding import Mesh
from jax.sharding import PartitionSpec as P

SEQ = ("x", "core")
SHARD = ("y", "z")
F32 = jnp.float32
LOW = jnp.bfloat16
MIB = 2**20
TOK = 2048
OWN = 256
TILE = 512
D = 1024
HIDDEN = 512
SPAN = 128
GELU_A = 0.7978845608028654
GELU_B = 0.044715

IN_VMEM = pl.BlockSpec(memory_space=pltpu.VMEM)
IN_SMEM = pl.BlockSpec(memory_space=pltpu.SMEM)
ANYWHERE = pl.BlockSpec(memory_space=pl.ANY)
DMA = pltpu.SemaphoreType.DMA


def shaped(shape, dtype):
    return jax.ShapeDtypeStruct(shape, dtype)


def remote(src, dst, send, recv, **device):
    return pltpu.make_async_remote_copy(
        src_ref=src,
        dst_ref=dst,
        send_sem=send,
        recv_sem=recv,
        device_id=device,
        device_id_type=pl.DeviceIdType.MESH,
    )


def axis(name):
    return lax.axis_index(name)


def ahead(name, k, count):
    return lax.rem(axis(name) + k, count)


def seq_peers():
    core = axis("core")
    return [
        {"x": ahead("x", j, 4), "core": lax.rem(core + i, 2)}
        for j in range(4)
        for i in range(2)
        if (j, i) != (0, 0)
    ]


def near_peers():
    return [{"x": ahead("x", 1, 4)}, {"x": ahead("x", 3, 4)}, {"core": 1 - axis("core")}]


def y_peers():
    return [{"y": ahead("y", k, 4)} for k in range(1, 4)]


def z_peers():
    return [{"z": ahead("z", k, 8)} for k in range(1, 8)]


def greet(peers):
    sem = pltpu.get_barrier_semaphore()
    for peer in peers:
        pl.semaphore_signal(sem, inc=1, device_id=peer, device_id_type=pl.DeviceIdType.MESH)
    return lambda: pl.semaphore_wait(sem, len(peers))


def dot(a, b):
    return jnp.dot(a, b, preferred_element_type=F32)


def dot_nt(a, b):
    return lax.dot_general(a, b, (((1,), (1,)), ((), ())), preferred_element_type=F32)


def dot_tn(a, b):
    return lax.dot_general(a, b, (((0,), (0,)), ((), ())), preferred_element_type=F32)


def whitened(values):
    mean = jnp.mean(values, axis=-1, keepdims=True)
    centered = values - mean
    spread = jnp.mean(centered * centered, axis=-1, keepdims=True)
    inverse = lax.rsqrt(spread + 1e-05)
    return centered * inverse, inverse


def norm_back(grad, gain, white, inverse):
    d_white = grad * gain
    first = jnp.mean(d_white, axis=-1, keepdims=True)
    second = jnp.mean(d_white * white, axis=-1, keepdims=True)
    return inverse * (d_white - first - white * second)


class Gather:
    def __init__(self, src, at, seven, rows, send, recv, cut=None):
        x, core = axis("x"), axis("core")
        other = 1 - core
        right, far, left = (lax.rem(x + k, 4) for k in (1, 2, 3))
        cut = cut or rows // 2
        low, high = pl.ds(0, cut), pl.ds(cut, rows - cut)
        mine, r, f, l = (at(2 * k + core) for k in (x, right, far, left))
        self.seven = seven
        self.send, self.recv = send, recv
        self.single = recv.shape[0] == 4
        slots = (0, 1, 3, 2, 2) + ((3, 3, 3) if self.single else (4, 5, 6))
        self.plan = [
            (src, mine, {"x": right}),
            (src, mine, {"x": left}),
            (src, mine, {"core": other}),
            (l.at[low], l.at[low], {"x": right}),
            (r.at[high], r.at[high], {"x": left}),
            (l, l, {"core": other}),
            (r, r, {"core": other}),
            (f, f, {"core": other}),
        ]
        self.slots = slots
        self.block = mine
        self.blocks = dict(
            mine=2 * x + core,
            mine_o=2 * x + other,
            left=2 * left + core,
            left_o=2 * left + other,
            right=2 * right + core,
            right_o=2 * right + other,
            far=2 * far + core,
            far_o=2 * far + other,
        )

    def copy(self, k):
        src, dst, device = self.plan[k]
        return remote(src, dst, self.send, self.recv.at[self.slots[k]], **device)

    def start(self):
        for k in (0, 1, 2):
            self.copy(k).start()

    def got(self, slot):
        remote(self.block, self.block, self.send, self.recv.at[slot], core=0).wait_recv()

    def got_others(self, four):
        remote(four, four, self.send, self.recv.at[3], core=0).wait_recv()

    def pass_left(self):
        self.got(0)
        self.copy(3).start()
        self.copy(5).start()

    def pass_right(self):
        self.got(1)
        self.copy(4).start()
        self.copy(6).start()

    def pass_far(self):
        self.got(2)
        self.copy(7).start()

    def sent(self):
        remote(self.seven, self.seven, self.send, self.recv.at[0], core=0).wait_send()


def all_sent(ref, send):
    remote(ref, ref, send, send, core=0).wait_send()


def all_here(ref, recv):
    remote(ref, ref, recv, recv, core=0).wait_recv()


class Reduce:
    def __init__(self, part, from_core, total, from_side, land, seven, rows, send, recv, source=None):
        self.seven = seven
        self.source = source or part
        self.part, self.from_core, self.total = part, from_core, total
        self.from_side, self.land = from_side, land
        self.send, self.recv = send, recv
        self.x, self.core = axis("x"), axis("core")
        self.half = rows // 2

    def chip(self, j):
        return lax.rem(self.x + j, 4)

    def core_copy(self, j):
        return remote(
            self.source(2 * self.chip(j) + 1 - self.core),
            self.from_core(j),
            self.send,
            self.recv.at[j],
            core=1 - self.core,
        )

    def side_copy(self, j):
        rows = pl.ds(0 if j == 1 else self.half, self.half)
        n = 4 + j // 2
        return remote(
            self.total(2).at[rows],
            self.from_side(j),
            self.send,
            self.recv.at[n],
            x=self.chip(j),
        )

    def chip_copy(self, j):
        n = 6 + j // 2
        return remote(self.total(j), self.land(j), self.send, self.recv.at[n], x=self.chip(j))

    def pair(self, j, rows):
        mine = self.part(2 * self.chip(j) + self.core)
        return mine[rows, :].astype(F32) + self.from_core(j)[rows, :].astype(F32)

    def to_core(self, j):
        self.core_copy(j).start()

    def to_far(self):
        self.core_copy(2).wait_recv()
        self.total(2)[...] = self.pair(2, slice(None)).astype(LOW)
        self.side_copy(1).start()
        self.side_copy(3).start()

    def to_side(self, j):
        self.core_copy(j).wait_recv()
        self.side_copy(j).wait_recv()
        low, high = slice(0, self.half), slice(self.half, 2 * self.half)
        joined, alone = (low, high) if j == 1 else (high, low)
        more = self.from_side(j)[...].astype(F32)
        self.total(j)[joined, :] = (self.pair(j, joined) + more).astype(LOW)
        self.total(j)[alone, :] = self.pair(j, alone).astype(LOW)
        self.chip_copy(j).start()

    def result(self):
        self.core_copy(0).wait_recv()
        total = self.pair(0, slice(None))
        for j in (1, 3):
            self.chip_copy(j).wait_recv()
            total = total + self.land(j)[...].astype(F32)
        return total

    def sent(self):
        all_sent(self.seven, self.send)


def call(kernel, outs, ins, scratch, name, number=None, vmem=56):
    extra = {} if number is None else dict(collective_id=number, has_side_effects=True)
    return pl.pallas_call(
        kernel,
        out_shape=[shape for shape, _ in outs],
        in_specs=ins,
        out_specs=[spec for _, spec in outs],
        scratch_shapes=scratch,
        name=name,
        compiler_params=pltpu.CompilerParams(vmem_limit_bytes=vmem * MIB, **extra),
    )


def chosen_units(values, seq):
    lane = lax.broadcasted_iota(jnp.int32, (values.shape[0], 128), 1)
    tiles = []
    for q in range(4):
        tile = jnp.zeros((values.shape[0], 128), F32)
        for p in range(8):
            at = 128 * (8 * q + p)
            shift = lax.rem(16 * p - 16 * seq + 128, 128)
            turned = pltpu.roll(values[:, at : at + 128], shift, 1)
            tile = jnp.where((lane // 16) == p, turned, tile)
        tiles.append(tile)
    return jnp.concatenate(tiles, axis=1)


def own_columns(wq, wo, wf, wp, bq, bv, bf, wq_o, wo_o, wf_o, wp_o, bias_o, bf_o):
    core = axis("core")
    seq = 2 * axis("x") + core
    span = pl.ds(pl.multiple_of(SPAN * seq, SPAN), SPAN)
    for k in range(3):
        at = pl.ds(pl.multiple_of(k * D + SPAN * seq, SPAN), SPAN)
        wq_o[:, k * SPAN : (k + 1) * SPAN] = wq[:, at]
    wo_o[...] = wo[pl.ds(pl.multiple_of(16 * core, 16), 16), :]
    wp_o[...] = wp[pl.ds(pl.multiple_of(16 * seq, 16), 16), :]
    bias_o[:, :SPAN] = bq[:, span]
    bias_o[:, SPAN : 2 * SPAN] = jnp.zeros((1, SPAN), F32)
    bias_o[:, 2 * SPAN :] = bv[:, span]
    wf_o[...] = chosen_units(wf[...].astype(F32), seq).astype(LOW)
    bf_o[...] = chosen_units(jnp.broadcast_to(bf[...], (8, 4 * D)), seq)[0:1]


def segment_cut(segment):
    return jnp.sum(jnp.where(segment[...] < 2, 1, 0))


def head_lanes(shape, dim, head):
    return (lax.broadcasted_iota(jnp.int32, shape, dim) // 64) == head


def masked_scores(scores, cut, q_tile, k_tile):
    shape = scores.shape
    key = k_tile * TILE + lax.broadcasted_iota(jnp.int32, shape, 0)
    query = q_tile * TILE + lax.broadcasted_iota(jnp.int32, shape, 1)
    allowed = key <= query
    if q_tile >= 2:
        allowed = allowed & ((key >= cut) | (query < cut))
    return jnp.where(allowed, scores, -1e30)


def tile_rows(tile):
    if isinstance(tile, int):
        return pl.ds(tile * TILE, TILE)
    return pl.ds(pl.multiple_of(tile * TILE, TILE), TILE)


def spread(src, dst, send, recv):
    x, core = axis("x"), axis("core")
    me = 2 * x + core
    for j in (2, 1, 3, 0):
        for i in range(2):
            if (j, i) != (0, 0):
                to_x, to_c = lax.rem(x + j, 4), lax.rem(core + i, 2)
                remote(src(2 * to_x + to_c), dst.at[me], send, recv, x=to_x, core=to_c).start()


def middle_kernel(
    x_own, w_qkv, w_out, w_fc, w_proj, bias_q, bias_v, bias_f, gain1, shift1, segment, cot, bo, gain,
    shift,
    xall_o, qkv_out, wq_out, o_out, lse, outp, mid_out, dm_out, do_all, gfc_out, gproj_out, gop_out,
    small_o, bfc_o, woz, wfz, wpz,
    wq, wo_in, wf_in, wp_in, bias, bf, qkv, wq_o, o_o, mid_o, dm_o, gfc_o, gproj_o, gop_o, qm, vt, scores, xs, os, cs, wo, wf, wp, n2, da, act, part, from_core, total, from_side, land, dob,
    yp, p_mid, loc, x_loc, out_loc, x_send, x_recv, z_send, z_recv, g_send, g_recv, c_send, c_recv, wo_send, wo_recv,
    y_send, y_recv, r_send, r_recv, a_send, a_recv, o_loc,
):
    x, core, y, z = axis("x"), axis("core"), axis("y"), axis("z")
    me = 2 * x + core
    ready = greet(seq_peers() + y_peers() + z_peers())
    own_columns(
        w_qkv, w_out, w_fc, w_proj, bias_q, bias_v, bias_f, wq, wo_in, wf_in, wp_in, bias, bf
    )
    cut = segment_cut(segment)
    written = []

    def write(src, dst):
        n = len(written)
        written.append(pltpu.make_async_copy(src, dst, out_loc.at[n]))
        written[-1].start()

    tokens = Gather(
        x_own, lambda t: xs.at[pl.ds(t * OWN, OWN)], xs.at[pl.ds(0, 7 * OWN)], OWN, x_send, x_recv
    )
    cots = Gather(cot, lambda t: cs.at[t], cs.at[pl.ds(0, 7)], OWN, c_send, c_recv)
    blocks = tokens.blocks
    half = wo.at[:, :, core]
    own_z = [(wq, wq_o.at[y, z]), (wo_in, woz.at[z]), (wf_in, wfz.at[z]), (wp_in, wpz.at[z])]
    whole_z = [wq_o.at[y], woz, wfz, wpz]
    local = own_z + [(x_own, xs.at[pl.ds(pl.multiple_of(OWN * me, OWN), OWN)]), (cot, cs.at[me])]
    local = [pltpu.make_async_copy(a, b, loc.at[k]) for k, (a, b) in enumerate(local)]
    for copy in local:
        copy.start()
    sends, own_y = [], {}

    def along_z(n):
        own, dst = own_z[n]
        for k in range(1, 8):
            remote(own, dst, z_send.at[n], z_recv.at[n], z=ahead("z", k, 8)).start()
        sends.append((whole_z[n].at[pl.ds(0, 7)], z_send.at[n]))

    def along_y(n):
        src, to = [(wq_o.at[y], wq_o), (woz, half), (wfz, wf), (wpz, wp)][n]
        for k in range(1, 4):
            remote(src, to.at[y], y_send.at[n], y_recv.at[n], y=ahead("y", k, 4)).start()
        sends.append((to.at[pl.ds(0, 3)], y_send.at[n]))
        if n:
            own_y[n] = pltpu.make_async_copy(src, to.at[y], loc.at[5 + n])
            own_y[n].start()

    def arrived(along, n):
        if along == "z":
            all_here(whole_z[n].at[pl.ds(0, 7)], z_recv.at[n])
        else:
            all_here((wq_o, half, wf, wp)[n].at[pl.ds(0, 3)], y_recv.at[n])
            if n:
                own_y[n].wait()

    ready()
    along_z(0)
    tokens.start()
    for copy in local:
        copy.wait()
    local = []

    def block_rows(block):
        return pl.ds(pl.multiple_of(OWN * block, OWN), OWN)

    def put(name):
        base = OWN * blocks[name]

        def one(i, _):
            rows = pl.ds(pl.multiple_of(base + i * 128, 128), 128)
            white, _inv = whitened(xs[rows, :].astype(F32))
            n2[rows, :] = (white * gain1[...] + shift1[...]).astype(LOW)
            return 0

        lax.fori_loop(0, OWN // 128, one, 0)
        rows = block_rows(blocks[name])
        pltpu.make_async_copy(xs.at[rows], xall_o.at[rows], x_loc).start()

    def project(name):
        rows = block_rows(blocks[name])
        weights = wq_o[...].reshape(D, 3 * SPAN)
        qkv[rows, :] = (dot(n2[rows, :], weights) + bias[...]).astype(LOW)

    put("mine")
    arrived("z", 0)
    along_y(0)
    along_z(1)
    tokens.got(3)
    put("mine_o")
    arrived("z", 1)
    along_z(2)
    tokens.pass_left()
    tokens.pass_right()
    put("left")
    put("right")
    tokens.got(4)
    put("left_o")
    tokens.got(5)
    put("right_o")
    arrived("y", 0)
    along_y(1)
    write(wq_o, wq_out)
    for name in ("mine", "mine_o", "left", "right"):
        project(name)
    tokens.pass_far()
    cots.start()
    put("far")
    for name in ("left_o", "right_o", "far"):
        project(name)
    tokens.got(6)
    put("far_o")
    project("far_o")
    write(qkv, qkv_out)
    arrived("z", 2)
    along_z(3)
    along_y(2)
    for tile in range(4):
        rows = tile_rows(tile)
        q = qkv[rows, :SPAN].astype(F32) * 0.125
        v_t = jnp.transpose(qkv[rows, 2 * SPAN :].astype(F32))
        for head in range(2):
            qm[head, rows, :] = jnp.where(head_lanes(q.shape, 1, head), q, 0.0).astype(LOW)
            vt[head, :, rows] = jnp.where(head_lanes(v_t.shape, 0, head), v_t, 1.0).astype(LOW)

    def heads_of(tile):
        rows = tile_rows(tile)
        return Gather(
            o_o.at[rows],
            lambda t: os.at[t, rows],
            None,
            TILE,
            g_send,
            g_recv.at[pl.ds(4 * tile, 4)],
        )

    def pass_near(tile):
        gather = heads_of(tile)
        gather.pass_left()
        gather.pass_right()

    for tile in range(4):
        q_rows = tile_rows(tile)
        free = min(tile, 2)
        outs = []
        for head in range(2):

            def score(k_tile, peak, masked, tile=tile, q_rows=q_rows, head=head):
                rows = tile_rows(k_tile)
                s = dot_nt(qkv[rows, SPAN : 2 * SPAN], qm[head, q_rows, :])
                if masked:
                    s = masked_scores(s, cut, tile, k_tile)
                scores[rows, :] = s
                return jnp.maximum(peak, jnp.max(s, axis=0, keepdims=True))

            peak = jnp.full((1, TILE), -3e38, F32)
            for k_tile in range(tile + 1):
                peak = score(k_tile, peak, k_tile >= free)

            sums = jnp.zeros((SPAN, TILE), F32)
            for k_tile in range(tile + 1):
                rows = tile_rows(k_tile)
                e = jnp.exp(scores[rows, :] - peak).astype(LOW)
                sums = sums + dot(vt[head, :, rows], e)
            weight = sums[64:65] if head == 0 else sums[0:1]
            lse[head : head + 1, q_rows] = peak + jnp.log(weight)
            outs.append(sums[64 * head : 64 * (head + 1)] / weight)
        o_o[q_rows, :] = jnp.transpose(jnp.concatenate(outs, axis=0)).astype(LOW)
        pltpu.make_async_copy(o_o.at[q_rows], os.at[me, q_rows], o_loc).start()
        heads_of(tile).start()
        if tile >= 1:
            pass_near(tile - 1)
        if tile == 2:
            heads_of(0).pass_far()
        if tile == 1:
            arrived("y", 1)
            to_core = remote(half, half, wo_send, wo_recv, core=1 - core)
            to_core.start()
        if tile == 2:
            arrived("z", 3)
            along_y(3)
    write(o_o, o_out)
    pltpu.make_async_copy(xs, xall_o, x_loc).wait()
    pltpu.make_async_copy(o_o, os.at[me], o_loc).wait()
    tokens.sent()
    to_core.wait_recv()

    def middle_of(rows):
        left = jnp.concatenate([os[t, rows, :] for t in range(8)], axis=1)
        return xs[rows, :].astype(F32) + dot(left, wo[...].reshape(D, D)) + bo[...]

    def forward(b, _):
        rows = tile_rows(b)
        gather = heads_of(b)

        @pl.when(b == 0)
        def _():
            heads_of(1).pass_far()

        @pl.when(b == 1)
        def _():
            heads_of(2).pass_far()
            pass_near(3)
            cots.pass_left()
            cots.pass_right()

        @pl.when(b == 2)
        def _():
            heads_of(3).pass_far()

        @pl.when(b == 3)
        def _():
            cots.pass_far()

        gather.got_others(os.at[pl.ds(0, 4), rows])
        white, _inv = whitened(middle_of(rows))
        low = (white * gain[...] + shift[...]).astype(LOW)
        n2[rows, :] = low

        @pl.when(b == 0)
        def _():
            arrived("y", 2)

        v = dot(low, wf[...].reshape(D, HIDDEN)) + bf[...]
        square = v * v
        t = jnp.tanh(GELU_A * v * (1.0 + GELU_B * square))
        half = 0.5 * (1.0 + t)
        act[rows, :] = (v * half).astype(LOW)
        slope = 0.5 * GELU_A * (1.0 + 3.0 * GELU_B * square)
        da[rows, :] = (half + v * (1.0 - t * t) * slope).astype(LOW)
        return 0

    lax.fori_loop(0, 4, forward, 0)
    arrived("y", 3)
    cots.got_others(cs.at[pl.ds(0, 4)])
    reduce = Reduce(
        lambda t: part.at[t],
        lambda j: from_core.at[j],
        lambda j: total.at[j - 1],
        lambda j: from_side.at[j // 2],
        lambda j: land.at[j // 2],
        part.at[pl.ds(0, 7)],
        OWN,
        r_send,
        r_recv,
    )
    weights = wp[...].reshape(HIDDEN, D)
    bfc_o[...] = jnp.zeros_like(bfc_o)

    def backward(j):
        chip = lax.rem(x + j, 4)
        rows = tile_rows(chip)
        c_low = cs[pl.ds(2 * chip, 2)].reshape(TILE, D)
        low = (dot_nt(c_low, weights) * da[rows, :].astype(F32)).astype(LOW)
        da[rows, :] = low
        bfc_o[0:1, :] += jnp.sum(low.astype(F32), axis=0, keepdims=True)
        d_n2 = dot_nt(low, wf[...].reshape(D, HIDDEN))
        part[pl.ds(2 * chip, 2)] = d_n2.astype(LOW).reshape(2, OWN, D)

    order = (2, 1, 3, 0)

    def back_step(i, _):
        j = jnp.where(i == 0, 2, jnp.where(i == 1, 1, jnp.where(i == 2, 3, 0)))
        backward(j)
        for n, j in enumerate(order):

            @pl.when(i == n)
            def _(n=n, j=j):
                reduce.to_core(j)
                if n == 0:
                    reduce.to_far()
                if n == 3:
                    reduce.to_side(1)
                    reduce.to_side(3)

        return 0

    lax.fori_loop(0, 4, back_step, 0)
    own_rows = pl.ds(pl.multiple_of(me * OWN, OWN), OWN)
    middle = middle_of(own_rows)
    mid_o[...] = middle
    write(mid_o, mid_out)
    gproj_o[...] = dot_tn(act[...], cs[...].reshape(TOK, D)).astype(LOW)
    for k in range(1, 4):
        peer = ahead("y", k, 4)
        piece = gproj_o.at[pl.ds(pl.multiple_of(128 * peer, 128), 128)]
        remote(piece, yp.at[k], y_send.at[4], y_recv.at[4], y=peer).start()
    gfc_o[...] = dot_tn(n2[...], da[...]).astype(LOW)
    write(gfc_o, gfc_out)

    def output_part(b, _):
        rows = tile_rows(b)
        xs[rows, :] = dot(act[rows, :], weights).astype(LOW)
        return 0

    lax.fori_loop(0, 4, output_part, 0)
    write(xs, outp)
    white, inverse = whitened(mid_o[...])
    c_own = cot[...].astype(F32)
    d_n2 = reduce.result()
    d_m = c_own + norm_back(d_n2, gain[...], white, inverse)
    dm_o[...] = d_m
    low = d_m.astype(LOW)
    d_o = dot_nt(low, wo[...].reshape(D, D)).astype(LOW)
    for t in range(8):
        dob[t] = d_o[:, SPAN * t : SPAN * (t + 1)]
    spread(lambda t: dob.at[t], do_all, a_send, a_recv)
    write(dob.at[me], do_all.at[me])
    write(dm_o, dm_out)
    small_o[...] = jnp.zeros_like(small_o)
    small_o[0:1, :] = jnp.sum(low.astype(F32), axis=0, keepdims=True)
    small_o[1:2, :] = jnp.sum(d_n2 * white, axis=0, keepdims=True)
    small_o[2:3, :] = jnp.sum(d_n2, axis=0, keepdims=True)
    small_o[3:4, :] = jnp.sum(c_own, axis=0, keepdims=True)
    left = jnp.concatenate([os[t, own_rows, :] for t in range(8)], axis=1)
    g_out = dot_tn(left, low).astype(LOW)
    for t in range(2):
        gop_o[t] = g_out[:, HIDDEN * t : HIDDEN * (t + 1)]
    write(gop_o, gop_out)
    all_here(yp.at[pl.ds(0, 3)], y_recv.at[4])
    p_sum = gproj_o[pl.ds(pl.multiple_of(128 * y, 128), 128), :].astype(F32)
    for k in range(1, 4):
        p_sum = p_sum + yp[k].astype(F32)
    p_mid[...] = p_sum.astype(LOW)
    write(p_mid, gproj_out)
    all_here(do_all.at[pl.ds(0, 7)], a_recv)
    all_sent(dob.at[pl.ds(0, 7)], a_send)
    for ref, sem in sends:
        all_sent(ref, sem)
    all_sent(yp.at[pl.ds(0, 3)], y_send.at[4])
    to_core.wait_send()
    for copy in written:
        copy.wait()
    cots.sent()
    all_sent(os.at[pl.ds(0, 7)], g_send)
    reduce.sent()


def middle(
    x, w_qkv, w_out, w_fc, w_proj, bias_q, bias_v, bias_f, gain1, shift1, segment, cot, bo, gain, shift
):
    outs = [
        (shaped((TOK, D), LOW), ANYWHERE),
        (shaped((TOK, 3 * SPAN), LOW), ANYWHERE),
        (shaped((4, 8, 32, 3 * SPAN), LOW), ANYWHERE),
        (shaped((TOK, SPAN), LOW), ANYWHERE),
        (shaped((2, TOK), F32), IN_VMEM),
        (shaped((TOK, D), LOW), ANYWHERE),
        (shaped((OWN, D), F32), ANYWHERE),
        (shaped((OWN, D), F32), ANYWHERE),
        (shaped((8, OWN, SPAN), LOW), ANYWHERE),
        (shaped((D, HIDDEN), LOW), ANYWHERE),
        (shaped((128, D), LOW), ANYWHERE),
        (shaped((2, D, HIDDEN), LOW), ANYWHERE),
        (shaped((8, D), F32), IN_VMEM),
        (shaped((8, HIDDEN), F32), IN_VMEM),
        (shaped((8, 16, D), LOW), ANYWHERE),
        (shaped((8, 32, HIDDEN), LOW), ANYWHERE),
        (shaped((8, 16, D), LOW), ANYWHERE),
    ]
    scratch = [
        pltpu.VMEM((32, 3 * SPAN), LOW),
        pltpu.VMEM((16, D), LOW),
        pltpu.VMEM((32, HIDDEN), LOW),
        pltpu.VMEM((16, D), LOW),
        pltpu.VMEM((1, 3 * SPAN), F32),
        pltpu.VMEM((1, HIDDEN), F32),
        pltpu.VMEM((TOK, 3 * SPAN), LOW),
        pltpu.VMEM((4, 8, 32, 3 * SPAN), LOW),
        pltpu.VMEM((TOK, SPAN), LOW),
        pltpu.VMEM((OWN, D), F32),
        pltpu.VMEM((OWN, D), F32),
        pltpu.VMEM((D, HIDDEN), LOW),
        pltpu.VMEM((HIDDEN, D), LOW),
        pltpu.VMEM((2, D, HIDDEN), LOW),
        pltpu.VMEM((2, TOK, SPAN), LOW),
        pltpu.VMEM((2, SPAN, TOK), LOW),
        pltpu.VMEM((TOK, TILE), F32),
        pltpu.VMEM((TOK, D), LOW),
        pltpu.VMEM((8, TOK, SPAN), LOW),
        pltpu.VMEM((8, OWN, D), LOW),
        pltpu.VMEM((4, 8, 2, 16, D), LOW),
        pltpu.VMEM((4, 8, 32, HIDDEN), LOW),
        pltpu.VMEM((4, 8, 16, D), LOW),
        pltpu.VMEM((TOK, D), LOW),
        pltpu.VMEM((TOK, HIDDEN), LOW),
        pltpu.VMEM((TOK, HIDDEN), LOW),
        pltpu.VMEM((8, OWN, D), LOW),
        pltpu.VMEM((4, OWN, D), LOW),
        pltpu.VMEM((3, OWN, D), LOW),
        pltpu.VMEM((2, OWN // 2, D), LOW),
        pltpu.VMEM((2, OWN, D), LOW),
        pltpu.VMEM((8, OWN, SPAN), LOW),
        pltpu.VMEM((4, 128, D), LOW),
        pltpu.VMEM((128, D), LOW),
        DMA((9,)), DMA, DMA((10,)), DMA, DMA((7,)), DMA((4,)), DMA((4,)),
        DMA, DMA((16,)), DMA, DMA((4,)), DMA, DMA,
        DMA((5,)), DMA((5,)), DMA, DMA((8,)), DMA, DMA, DMA,
    ]
    return call(middle_kernel, outs, [IN_VMEM] * 15, scratch, "middle", 2, vmem=60)(
        x, w_qkv, w_out, w_fc, w_proj, bias_q[None], bias_v[None], bias_f[None], gain1[None],
        shift1[None], segment, cot, bo[None], gain[None], shift[None],
    )[:14]


def ending_kernel(
    qkv_in, segment, do_in, o_in, lse, outp_in, x_all, gop_in, gfc_in, p_mid_in, wq_in, mid_in, dm_in,
    gain, shift, bp, small, bfc,
    out_o, dtok_o, fin_o, vec_o,
    qkv, do_ref, o_own, gop, gfc, p_mid, wq, mid, dm,
    qm, dom, ktm, delta, dqt, dk, dv, dqkv, outp, xs, part, g_acc, gq, go, rows1,
    so, sumo, eo, lo, g_side, sn, sumn, en, ln, yf, zf, zp, f_mid,
    gy, gz, g_mid, gv, gvz, gvy, v_mid, oy, oz, o_mid, fin, sums, x_buf, v16, z_buf, y_buf, v_out, out_low, dtok,
    loc, ro_send, ro_recv, g_send, g_recv, rn_send, rn_recv, y_send, y_recv, z_send, z_recv,
    f_send, f_recv, s_send, s_recv,
):
    x, core, y, z = axis("x"), axis("core"), axis("y"), axis("z")
    me = 2 * x + core
    ready = greet(seq_peers() + y_peers() + z_peers())
    loads = [
        (qkv_in, qkv), (do_in, do_ref), (o_in, o_own), (gop_in, gop), (gfc_in, gfc),
        (p_mid_in, p_mid), (wq_in, wq), (x_all, xs), (outp_in, outp), (mid_in, mid), (dm_in, dm),
    ]
    loads = [pltpu.make_async_copy(a, b, loc.at[k]) for k, (a, b) in enumerate(loads)]
    for copy in loads:
        copy.start()
    for ref in (dqt, dk, dv, g_acc, rows1, v16):
        ref[...] = jnp.zeros_like(ref)
    cut = segment_cut(segment)
    for copy in loads[:3]:
        copy.wait()

    def prepare(tile, _):
        rows = tile_rows(tile)
        q = qkv[rows, :SPAN].astype(F32) * 0.125
        k_t = jnp.transpose(qkv[rows, SPAN : 2 * SPAN].astype(F32))
        d_o = do_ref[rows, :].astype(F32)
        prod = d_o * o_own[rows, :].astype(F32)
        for head in range(2):
            lanes = head_lanes(q.shape, 1, head)
            qm[head, rows, :] = jnp.where(lanes, q, 0.0).astype(LOW)
            dom[head, rows, :] = jnp.where(lanes, d_o, 0.0).astype(LOW)
            ktm[head, :, rows] = jnp.where(head_lanes(k_t.shape, 0, head), k_t, 0.0).astype(LOW)
            ones = jnp.where(head_lanes((8, SPAN), 1, head), 1.0, 0.0)
            dots = lax.dot_general(
                ones, prod, (((1,), (1,)), ((), ())),
                precision=lax.Precision.HIGHEST, preferred_element_type=F32,
            )
            delta[head : head + 1, rows] = dots[0:1]
        return 0

    lax.fori_loop(0, 4, prepare, 0)
    ready()
    for copy in loads[3:6]:
        copy.wait()
    r_out = Reduce(
        lambda t: outp.at[t], lambda j: so.at[j], lambda j: sumo.at[j - 1], lambda j: eo.at[j // 2],
        lambda j: lo.at[j // 2], outp.at[pl.ds(0, 7)], OWN, ro_send, ro_recv,
        source=lambda t: outp_in.at[t],
    )
    r_dn1 = Reduce(
        lambda t: part.at[t], lambda j: sn.at[j], lambda j: sumn.at[j - 1], lambda j: en.at[j // 2],
        lambda j: ln.at[j // 2], part.at[pl.ds(0, 7)], OWN, rn_send, rn_recv,
    )
    to_core = remote(gop_in.at[1 - core], g_side, g_send, g_recv, core=1 - core)
    to_core.start()
    for j in (2, 1, 3, 0):
        r_out.to_core(j)
    sends = []

    def pieces_to_z(src, land, n):
        rows = land.shape[1]
        for k in range(1, 8):
            peer = ahead("z", k, 8)
            piece = src.at[pl.ds(pl.multiple_of(rows * peer, rows), rows)]
            remote(piece, land.at[k], z_send.at[n], z_recv.at[n], z=peer).start()
        sends.append((land.at[pl.ds(0, 7)], z_send.at[n]))

    def rows_to_y(src, land, n):
        rows = land.shape[1]
        for k in range(1, 4):
            peer = ahead("y", k, 4)
            piece = src.at[pl.ds(pl.multiple_of(rows * peer, rows), rows)]
            remote(piece, land.at[k], y_send.at[n], y_recv.at[n], y=peer).start()
        sends.append((land.at[pl.ds(0, 3)], y_send.at[n]))

    def from_y(src, land, n):
        rows = land.shape[1]
        all_here(land.at[pl.ds(0, 3)], y_recv.at[n])
        return summed(src[pl.ds(pl.multiple_of(rows * y, rows), rows), :], land, 4)

    def from_z(src, land, n):
        rows = land.shape[1]
        all_here(land.at[pl.ds(0, 7)], z_recv.at[n])
        return summed(src[pl.ds(pl.multiple_of(rows * z, rows), rows), :], land, 8)

    rows_to_y(gfc, yf, 0)
    pieces_to_z(p_mid, zp, 0)

    def order(n):
        j = jnp.where(n == 0, 2, jnp.where(n == 1, 1, jnp.where(n == 2, 3, 0)))
        return lax.rem(x + j, 4)

    def pair(first, second):
        q_tile, k_tile = jnp.maximum(first, second), jnp.minimum(first, second)
        q_rows, k_rows = tile_rows(q_tile), tile_rows(k_tile)
        keys, values = qkv[k_rows, SPAN : 2 * SPAN], qkv[k_rows, 2 * SPAN :]
        key = k_tile * TILE + lax.broadcasted_iota(jnp.int32, (TILE, 1), 0)
        query = q_tile * TILE + lax.broadcasted_iota(jnp.int32, (1, TILE), 1)
        key_code = jnp.where((key >= TOK // 2) & (key < cut), 1, 0)
        query_code = jnp.where(query >= cut, 1, 2)
        allowed = (key <= query) & (key_code < query_code)
        for head in range(2):
            q_h, do_h = qm[head, q_rows, :], dom[head, q_rows, :]
            s = jnp.where(allowed, dot_nt(keys, q_h), -1e30)
            p = jnp.exp(s - lse[head : head + 1, q_rows])
            d_p = dot_nt(values, do_h)
            d_s = (p * (d_p - delta[head : head + 1, q_rows])).astype(LOW)
            dv[k_rows, :] += dot(p.astype(LOW), do_h)
            dk[k_rows, :] += dot(d_s, q_h)
            dqt[q_tile] += dot(ktm[head, :, k_rows], d_s)

    def complete(tile):
        rows = tile_rows(tile)
        low = jnp.concatenate(
            [jnp.transpose(dqt[tile]) * 0.125, dk[rows, :], dv[rows, :]], axis=1
        ).astype(LOW)
        dqkv[rows, :] = low
        d_n1 = dot_nt(low, wq[...].reshape(D, 3 * SPAN))
        part[pl.ds(2 * tile, 2)] = d_n1.astype(LOW).reshape(2, OWN, D)

    def account(tile):
        rows = tile_rows(tile)
        low = dqkv[rows, :]
        white, _inv = whitened(xs[rows, :].astype(F32))
        n1 = (white * gain[...] + shift[...]).astype(LOW)
        d_n1 = part[pl.ds(2 * tile, 2)].reshape(TILE, D).astype(F32)
        rows1[0:1, :] += jnp.sum(d_n1 * white, axis=0, keepdims=True)
        rows1[1:2, :] += jnp.sum(d_n1, axis=0, keepdims=True)
        wide = low.astype(F32)
        v16[8:9, :] += jnp.sum(wide[:, :SPAN], axis=0, keepdims=True)
        v16[9:10, :] += jnp.sum(wide[:, 2 * SPAN :], axis=0, keepdims=True)
        g_acc[...] += dot_tn(n1, low)

    def summed(own, others, count):
        total = own.astype(F32)
        for k in range(1, count):
            total = total + others[k].astype(F32)
        return total

    for step, j in enumerate((2, 1, 3, 0)):
        tile = order(step)

        def one(r, _, tile=tile):
            pair(tile, order(r))
            return 0

        if step == 0:
            lax.fori_loop(0, 2, one, 0)
            for copy in loads[6:]:
                copy.wait()
            r_out.to_far()
            to_core.wait_recv()
            go[...] = (gop[core].astype(F32) + g_side[...].astype(F32)).astype(LOW)
            rows_to_y(go, oy, 1)
            lax.fori_loop(2, 4, one, 0)
        else:
            lax.fori_loop(step, 4, one, 0)
        if step == 1:
            r_out.to_side(1)
            r_out.to_side(3)
        complete(tile)
        r_dn1.to_core(j)
        account(tile)
        if step == 0:
            r_dn1.to_far()
        if step == 1:
            r_dn1.to_side(1)
            f_mid[...] = from_y(gfc, yf, 0).astype(LOW)
            pieces_to_z(f_mid, zf, 1)
        if step == 2:
            r_dn1.to_side(3)
            o_mid[...] = from_y(go, oy, 1).astype(LOW)
            pieces_to_z(o_mid, oz, 3)

    qk, v_at = slice(0, 2 * SPAN), slice(2 * SPAN, 3 * SPAN)
    gq[...] = g_acc[:, qk].astype(LOW)
    rows_to_y(gq, gy, 2)
    for k in range(32):
        at = 128 * (k % 8) + 32 * (k // 8)
        gv[at : at + 32, :] = g_acc[32 * k : 32 * k + 32, v_at].astype(LOW)
    pieces_to_z(gv, gvz, 2)
    vectors = jnp.concatenate([rows1[0:2, :], small[0:4, :], jnp.zeros((2, D), F32)], axis=0)
    for t in range(8):
        sums[t] = vectors[:, SPAN * t : SPAN * (t + 1)]
    spread(lambda t: sums.at[t], x_buf, s_send.at[0], s_recv.at[0])
    x_buf[me] = sums[me]

    def in_halves(row, total):
        fin[row : row + 16, :HIDDEN] = total[:16].astype(LOW)
        fin[row : row + 16, HIDDEN:] = total[16:].astype(LOW)

    fin[0:16, :] = from_z(p_mid, zp, 0).astype(LOW)
    in_halves(16, from_z(f_mid, zf, 1))
    early = pl.ds(0, 32)
    finals = Gather(
        fin.at[early],
        lambda t: fin_o.at[t, early],
        fin_o.at[pl.ds(0, 7), early],
        32,
        f_send.at[0],
        f_recv.at[pl.ds(0, 4)],
    )
    finals.start()
    written = [pltpu.make_async_copy(fin.at[early], fin_o.at[me, early], loc.at[11])]
    written[0].start()
    for k in range(4):
        v16[10 + k : 11 + k, :] = bfc[0:1, SPAN * k : SPAN * (k + 1)]
    g_mid[...] = from_y(gq, gy, 2).astype(LOW)
    pieces_to_z(g_mid, gz, 5)
    all_here(x_buf.at[pl.ds(0, 7)], s_recv.at[0])
    v16[0:8, :] = summed(x_buf[0], x_buf, 8)
    z_buf[z] = v16[...]
    for k in range(1, 8):
        remote(v16, z_buf.at[z], z_send.at[4], z_recv.at[4], z=ahead("z", k, 8)).start()
    sends.append((z_buf.at[pl.ds(0, 7)], z_send.at[4]))
    v_mid[...] = from_z(gv, gvz, 2).astype(LOW)
    rows_to_y(v_mid, gvy, 3)
    finals.pass_left()
    finals.pass_right()
    own_rows = pl.ds(pl.multiple_of(me * OWN, OWN), OWN)
    white, inverse = whitened(xs[own_rows, :].astype(F32))
    out_low[...] = (mid[...] + r_out.result() + bp[...]).astype(LOW)
    written.append(pltpu.make_async_copy(out_low, out_o, loc.at[13]))
    written[1].start()
    all_here(z_buf.at[pl.ds(0, 7)], z_recv.at[4])
    y_buf[y] = summed(z_buf[0], z_buf, 8)
    for k in range(1, 4):
        peer = ahead("y", k, 4)
        remote(y_buf.at[y], y_buf.at[y], y_send.at[4], y_recv.at[4], y=peer).start()
    sends.append((y_buf.at[pl.ds(0, 3)], y_send.at[4]))
    total = from_z(g_mid, gz, 5)
    fin[48:64, 0 : 2 * SPAN] = total[:16].astype(LOW)
    fin[48:64, HIDDEN : HIDDEN + 2 * SPAN] = total[16:].astype(LOW)
    total = from_y(v_mid, gvy, 3)
    fin[48:64, v_at] = total[:16].astype(LOW)
    fin[48:64, HIDDEN + 2 * SPAN : HIDDEN + 3 * SPAN] = total[16:].astype(LOW)
    fin[48:64, 3 * SPAN : HIDDEN] = jnp.zeros((16, SPAN), LOW)
    fin[48:64, HIDDEN + 3 * SPAN :] = jnp.zeros((16, SPAN), LOW)
    in_halves(32, from_z(o_mid, oz, 3))
    late = pl.ds(32, 32)
    spread(lambda t: fin.at[late], fin_o.at[:, late], f_send.at[1], f_recv.at[4])
    written.append(pltpu.make_async_copy(fin.at[late], fin_o.at[me, late], loc.at[12]))
    written[2].start()
    finals.pass_far()
    all_here(y_buf.at[pl.ds(0, 3)], y_recv.at[4])
    v_out[...] = summed(y_buf[0], y_buf, 4)
    spread(lambda t: v_out, vec_o, s_send.at[1], s_recv.at[1])
    vec_o[me] = v_out[...]
    d_n1 = r_dn1.result()
    dtok[...] = dm[...] + norm_back(d_n1, gain[...], white, inverse)
    written.append(pltpu.make_async_copy(dtok, dtok_o, loc.at[14]))
    written[3].start()
    finals.got_others(fin_o.at[pl.ds(0, 4), early])
    all_here(fin_o.at[pl.ds(0, 7), late], f_recv.at[4])
    all_here(vec_o.at[pl.ds(0, 7)], s_recv.at[1])
    finals.sent()
    all_sent(fin_o.at[pl.ds(0, 7), late], f_send.at[1])
    all_sent(x_buf.at[pl.ds(0, 7)], s_send.at[0])
    all_sent(vec_o.at[pl.ds(0, 7)], s_send.at[1])
    for ref, sem in sends:
        all_sent(ref, sem)
    to_core.wait_send()
    for copy in written:
        copy.wait()
    for reduce in (r_out, r_dn1):
        reduce.sent()


def reduce_scratch(rows, columns):
    return [
        pltpu.VMEM((4, rows, columns), LOW),
        pltpu.VMEM((3, rows, columns), LOW),
        pltpu.VMEM((2, rows // 2, columns), LOW),
        pltpu.VMEM((2, rows, columns), LOW),
    ]


def ending(
    qkv, segment, d_o, o_own, lse, outp, x_all, gop, gfc, gproj, wq, mid, dm, gain, shift, bp, small, bfc
):
    outs = [
        (shaped((OWN, D), LOW), ANYWHERE),
        (shaped((OWN, D), F32), ANYWHERE),
        (shaped((8, 64, D), LOW), ANYWHERE),
        (shaped((8, 16, SPAN), F32), IN_VMEM),
    ]
    scratch = [
        pltpu.VMEM((TOK, 3 * SPAN), LOW),
        pltpu.VMEM((TOK, SPAN), LOW),
        pltpu.VMEM((TOK, SPAN), LOW),
        pltpu.VMEM((2, D, HIDDEN), LOW),
        pltpu.VMEM((D, HIDDEN), LOW),
        pltpu.VMEM((128, D), LOW),
        pltpu.VMEM((4, 8, 32, 3 * SPAN), LOW),
        pltpu.VMEM((OWN, D), F32),
        pltpu.VMEM((OWN, D), F32),
        pltpu.VMEM((2, TOK, SPAN), LOW),
        pltpu.VMEM((2, TOK, SPAN), LOW),
        pltpu.VMEM((2, SPAN, TOK), LOW),
        pltpu.VMEM((2, TOK), F32),
        pltpu.VMEM((4, SPAN, TILE), F32),
        pltpu.VMEM((TOK, SPAN), F32),
        pltpu.VMEM((TOK, SPAN), F32),
        pltpu.VMEM((TOK, 3 * SPAN), LOW),
        pltpu.VMEM((8, OWN, D), LOW),
        pltpu.VMEM((TOK, D), LOW),
        pltpu.VMEM((8, OWN, D), LOW),
        pltpu.VMEM((D, 3 * SPAN), F32),
        pltpu.VMEM((D, 2 * SPAN), LOW),
        pltpu.VMEM((D, HIDDEN), LOW),
        pltpu.VMEM((8, D), F32),
        *reduce_scratch(OWN, D), pltpu.VMEM((D, HIDDEN), LOW), *reduce_scratch(OWN, D),
        pltpu.VMEM((4, 256, HIDDEN), LOW),
        pltpu.VMEM((8, 32, HIDDEN), LOW), pltpu.VMEM((8, 16, D), LOW),
        pltpu.VMEM((256, HIDDEN), LOW),
        pltpu.VMEM((4, 256, 2 * SPAN), LOW),
        pltpu.VMEM((8, 32, 2 * SPAN), LOW),
        pltpu.VMEM((256, 2 * SPAN), LOW),
        pltpu.VMEM((D, SPAN), LOW),
        pltpu.VMEM((8, 128, SPAN), LOW),
        pltpu.VMEM((4, 32, SPAN), LOW),
        pltpu.VMEM((128, SPAN), LOW),
        pltpu.VMEM((4, 256, HIDDEN), LOW),
        pltpu.VMEM((8, 32, HIDDEN), LOW),
        pltpu.VMEM((256, HIDDEN), LOW),
        pltpu.VMEM((64, D), LOW),
        pltpu.VMEM((8, 8, SPAN), F32),
        pltpu.VMEM((8, 8, SPAN), F32),
        pltpu.VMEM((16, SPAN), F32),
        pltpu.VMEM((8, 16, SPAN), F32),
        pltpu.VMEM((4, 16, SPAN), F32),
        pltpu.VMEM((16, SPAN), F32),
        pltpu.VMEM((OWN, D), LOW),
        pltpu.VMEM((OWN, D), F32),
        DMA((15,)), DMA, DMA((8,)), DMA, DMA, DMA, DMA((8,)),
        DMA((5,)), DMA((5,)), DMA((6,)), DMA((6,)), DMA((2,)), DMA((5,)), DMA((2,)), DMA((2,)),
    ]
    ins = [ANYWHERE, IN_VMEM, ANYWHERE, ANYWHERE, IN_VMEM] + [ANYWHERE] * 8 + [IN_VMEM] * 5
    return call(ending_kernel, outs, ins, scratch, "ending", 4, vmem=60)(
        qkv, segment, d_o.reshape(TOK, SPAN), o_own, lse, outp.reshape(8, OWN, D), x_all, gop, gfc,
        gproj, wq, mid, dm, gain[None], shift[None], bp[None], small, bfc,
    )


def results_kernel(fin, vec, out, dtok, out_o, dtok_o, gq_o, go_o, gf_o, gp_o, *rest):
    vectors, bf_o, out_s, dtok_s, loc = rest[:10], *rest[10:]
    inward = [
        pltpu.make_async_copy(out, out_s, loc.at[0]),
        pltpu.make_async_copy(dtok, dtok_s, loc.at[1]),
    ]
    outward = [
        pltpu.make_async_copy(out_s, out_o, loc.at[2]),
        pltpu.make_async_copy(dtok_s, dtok_o, loc.at[3]),
    ]
    for copy in inward:
        copy.start()
    lane = lax.broadcasted_iota(jnp.int32, (40, 128), 1) // 16
    units = []
    for t in range(8):
        gp_o[16 * t : 16 * (t + 1), :] = fin[t, 0:16, :].astype(F32)
        span = slice(SPAN * t, SPAN * (t + 1))
        for half in range(2):
            rows = slice(16 * half, 16 * (half + 1))
            at = HIDDEN * half
            for k in range(3):
                gq_o[rows, D * k + SPAN * t : D * k + SPAN * (t + 1)] = fin[
                    t, 48:64, at + SPAN * k : at + SPAN * (k + 1)
                ].astype(F32)
        bias = jnp.concatenate([vec[t, 10 + k : 11 + k, :] for k in range(4)], axis=1)
        units.append(
            jnp.concatenate(
                [
                    fin[t, 16:32, :HIDDEN].astype(F32),
                    fin[t, 16:32, HIDDEN:].astype(F32),
                    jnp.broadcast_to(bias, (8, HIDDEN)),
                ],
                axis=0,
            )
        )
        for k, vector in enumerate(vectors):
            vector[:, span] = vec[t, k : k + 1, :]
    for core in range(2):
        for half in range(2):
            at = slice(HIDDEN * half, HIDDEN * (half + 1))
            total = fin[core, 32:48, at].astype(F32)
            for chip in range(1, 4):
                total = total + fin[2 * chip + core, 32:48, at].astype(F32)
            go_o[16 * half : 16 * (half + 1), HIDDEN * core : HIDDEN * (core + 1)] = total
    for into, out_of in zip(inward, outward):
        into.wait()
        out_of.start()
    for s in range(32):
        q, p = s // 8, s % 8
        tile = jnp.zeros((40, 128), F32)
        for t in range(8):
            turned = pltpu.roll(units[t][:, 128 * q : 128 * (q + 1)], (16 * t - 16 * p) % 128, 1)
            tile = jnp.where(lane == t, turned, tile)
        gf_o[:, 128 * s : 128 * (s + 1)] = tile[:32]
        bf_o[:, 128 * s : 128 * (s + 1)] = tile[32:33]
    for copy in outward:
        copy.wait()


def results(fin, vec, out, dtok):
    outs = [
        (shaped((OWN, D), LOW), ANYWHERE),
        (shaped((OWN, D), F32), ANYWHERE),
        (shaped((32, 3 * D), F32), IN_VMEM),
        (shaped((32, D), F32), IN_VMEM),
        (shaped((32, 4 * D), F32), IN_VMEM),
        (shaped((128, D), F32), IN_VMEM),
    ]
    outs += [(shaped((1, D), F32), IN_VMEM)] * 10 + [(shaped((1, 4 * D), F32), IN_VMEM)]
    ins = [IN_VMEM, IN_VMEM, ANYWHERE, ANYWHERE]
    scratch = [pltpu.VMEM((OWN, D), LOW), pltpu.VMEM((OWN, D), F32), DMA((4,))]
    return call(results_kernel, outs, ins, scratch, "results")(fin, vec, out, dtok)


def per_device(
    tokens, segment, ln1_gain, ln1_shift, w_qkv, bias_query, bias_value, w_out, bias_out,
    ln2_gain, ln2_shift, w_fc, bias_fc, w_proj, bias_proj, cotangent,
):
    x_all, qkv, wq, o_own, lse, outp, mid, dm, do_all, gfc, gproj, gop, small, bfc = middle(
        tokens[0], w_qkv, w_out, w_fc, w_proj, bias_query, bias_value, bias_fc, ln1_gain, ln1_shift,
        segment, cotangent[0], bias_out, ln2_gain, ln2_shift,
    )
    out, dtok, fin, vec = ending(
        qkv, segment, do_all, o_own, lse, outp, x_all, gop, gfc, gproj, wq, mid, dm, ln1_gain,
        ln1_shift, bias_proj, small, bfc,
    )
    out, dtok, gq, go, gf, gp, *vectors = results(fin, vec, out, dtok)
    v = [vector[0] for vector in vectors]
    return (
        out[None], dtok[None], v[0], v[1], gq, v[8], v[9], go, v[2], v[3], v[4], gf, v[10], gp, v[5],
    )


def solution(mesh):
    finer = Mesh(mesh.devices.reshape(4, 2, 4, 8), ("x", "core", "y", "z"))
    rows, whole = P(SHARD, None), P()
    tokens = P(SHARD, SEQ, None)
    return jax.shard_map(
        per_device,
        mesh=finer,
        in_specs=(
            tokens, rows, whole, whole, rows, whole, whole, rows, whole, whole, whole, rows,
            whole, rows, whole, tokens,
        ),
        out_specs=(
            tokens, tokens, whole, whole, rows, whole, whole, rows, whole, whole, whole, rows,
            whole, rows, whole,
        ),
        check_vma=False,
    )
```

```python
import functools

import jax
import jax.numpy as jnp
from jax import lax
from jax.experimental import pallas as pl
from jax.experimental.pallas import tpu as pltpu
from jax.sharding import Mesh
from jax.sharding import PartitionSpec as P

SEQ = ("x", "core")
SHARD = ("y", "z")
F32 = jnp.float32
LOW = jnp.bfloat16
MIB = 2**20
TOK = 2048
OWN = 256
TILE = 512
D = 1024
HIDDEN = 512
SPAN = 128
GELU_A = 0.7978845608028654
GELU_B = 0.044715

IN_VMEM = pl.BlockSpec(memory_space=pltpu.VMEM)
IN_SMEM = pl.BlockSpec(memory_space=pltpu.SMEM)
ANYWHERE = pl.BlockSpec(memory_space=pl.ANY)
DMA = pltpu.SemaphoreType.DMA


def shaped(shape, dtype):
    return jax.ShapeDtypeStruct(shape, dtype)


def remote(src, dst, send, recv, **device):
    return pltpu.make_async_remote_copy(
        src_ref=src,
        dst_ref=dst,
        send_sem=send,
        recv_sem=recv,
        device_id=device,
        device_id_type=pl.DeviceIdType.MESH,
    )


def axis(name):
    return lax.axis_index(name)


def ahead(name, k, count):
    return lax.rem(axis(name) + k, count)


def seq_peers():
    core = axis("core")
    return [
        {"x": ahead("x", j, 4), "core": lax.rem(core + i, 2)}
        for j in range(4)
        for i in range(2)
        if (j, i) != (0, 0)
    ]


def near_peers():
    return [{"x": ahead("x", 1, 4)}, {"x": ahead("x", 3, 4)}, {"core": 1 - axis("core")}]


def y_peers():
    return [{"y": ahead("y", k, 4)} for k in range(1, 4)]


def z_peers():
    return [{"z": ahead("z", k, 8)} for k in range(1, 8)]


def greet(peers):
    sem = pltpu.get_barrier_semaphore()
    for peer in peers:
        pl.semaphore_signal(sem, inc=1, device_id=peer, device_id_type=pl.DeviceIdType.MESH)
    return lambda: pl.semaphore_wait(sem, len(peers))


def dot(a, b):
    return jnp.dot(a, b, preferred_element_type=F32)


def dot_nt(a, b):
    return lax.dot_general(a, b, (((1,), (1,)), ((), ())), preferred_element_type=F32)


def dot_tn(a, b):
    return lax.dot_general(a, b, (((0,), (0,)), ((), ())), preferred_element_type=F32)


def whitened(values):
    mean = jnp.mean(values, axis=-1, keepdims=True)
    centered = values - mean
    spread = jnp.mean(centered * centered, axis=-1, keepdims=True)
    inverse = lax.rsqrt(spread + 1e-05)
    return centered * inverse, inverse


def norm_back(grad, gain, white, inverse):
    d_white = grad * gain
    first = jnp.mean(d_white, axis=-1, keepdims=True)
    second = jnp.mean(d_white * white, axis=-1, keepdims=True)
    return inverse * (d_white - first - white * second)


class Gather:
    def __init__(self, src, at, seven, rows, send, recv, cut=None):
        x, core = axis("x"), axis("core")
        other = 1 - core
        right, far, left = (lax.rem(x + k, 4) for k in (1, 2, 3))
        cut = cut or rows // 2
        low, high = pl.ds(0, cut), pl.ds(cut, rows - cut)
        mine, r, f, l = (at(2 * k + core) for k in (x, right, far, left))
        self.seven = seven
        self.send, self.recv = send, recv
        self.single = recv.shape[0] == 4
        slots = (0, 1, 3, 2, 2) + ((3, 3, 3) if self.single else (4, 5, 6))
        self.plan = [
            (src, mine, {"x": right}),
            (src, mine, {"x": left}),
            (src, mine, {"core": other}),
            (l.at[low], l.at[low], {"x": right}),
            (r.at[high], r.at[high], {"x": left}),
            (l, l, {"core": other}),
            (r, r, {"core": other}),
            (f, f, {"core": other}),
        ]
        self.slots = slots
        self.block = mine
        self.blocks = dict(
            mine=2 * x + core,
            mine_o=2 * x + other,
            left=2 * left + core,
            left_o=2 * left + other,
            right=2 * right + core,
            right_o=2 * right + other,
            far=2 * far + core,
            far_o=2 * far + other,
        )

    def copy(self, k):
        src, dst, device = self.plan[k]
        return remote(src, dst, self.send, self.recv.at[self.slots[k]], **device)

    def start(self):
        for k in (0, 1, 2):
            self.copy(k).start()

    def got(self, slot):
        remote(self.block, self.block, self.send, self.recv.at[slot], core=0).wait_recv()

    def got_others(self, four):
        remote(four, four, self.send, self.recv.at[3], core=0).wait_recv()

    def pass_left(self):
        self.got(0)
        self.copy(3).start()
        self.copy(5).start()

    def pass_right(self):
        self.got(1)
        self.copy(4).start()
        self.copy(6).start()

    def pass_far(self):
        self.got(2)
        self.copy(7).start()

    def sent(self):
        remote(self.seven, self.seven, self.send, self.recv.at[0], core=0).wait_send()


def all_sent(ref, send):
    remote(ref, ref, send, send, core=0).wait_send()


def all_here(ref, recv):
    remote(ref, ref, recv, recv, core=0).wait_recv()


class Reduce:
    def __init__(self, part, from_core, total, from_side, land, seven, rows, send, recv, source=None, mine=None):
        self.seven = seven
        self.source = source or part
        self.mine = mine or (lambda j: part(2 * self.chip(j) + self.core))
        self.part, self.from_core, self.total = part, from_core, total
        self.from_side, self.land = from_side, land
        self.send, self.recv = send, recv
        self.x, self.core = axis("x"), axis("core")
        self.half = rows // 2

    def chip(self, j):
        return lax.rem(self.x + j, 4)

    def core_copy(self, j):
        return remote(
            self.source(2 * self.chip(j) + 1 - self.core),
            self.from_core(j),
            self.send,
            self.recv.at[j],
            core=1 - self.core,
        )

    def side_copy(self, j):
        rows = pl.ds(0 if j == 1 else self.half, self.half)
        n = 4 + j // 2
        return remote(
            self.total(2).at[rows],
            self.from_side(j),
            self.send,
            self.recv.at[n],
            x=self.chip(j),
        )

    def chip_copy(self, j, rows):
        n = 6 + j // 2
        return remote(
            self.total(j).at[rows],
            self.land(j).at[rows],
            self.send,
            self.recv.at[n],
            x=self.chip(j),
        )

    def pair(self, j, rows):
        return self.mine(j)[rows, :].astype(F32) + self.from_core(j)[rows, :].astype(F32)

    def to_core(self, j):
        self.core_copy(j).start()

    def to_far(self):
        self.core_copy(2).wait_recv()
        self.total(2)[...] = self.pair(2, slice(None)).astype(LOW)
        self.side_copy(1).start()
        self.side_copy(3).start()

    def halves(self, j):
        low, high = pl.ds(0, self.half), pl.ds(self.half, self.half)
        return (low, high) if j == 1 else (high, low)

    def to_side_alone(self, j):
        self.core_copy(j).wait_recv()
        rows = self.halves(j)[1]
        self.total(j)[rows, :] = self.pair(j, rows).astype(LOW)
        self.chip_copy(j, rows).start()

    def to_side_joined(self, j):
        self.side_copy(j).wait_recv()
        rows = self.halves(j)[0]
        more = self.from_side(j)[...].astype(F32)
        self.total(j)[rows, :] = (self.pair(j, rows) + more).astype(LOW)
        self.chip_copy(j, rows).start()

    def result(self):
        self.core_copy(0).wait_recv()
        total = self.pair(0, slice(None))
        for j in (1, 3):
            self.chip_copy(j, pl.ds(0, 2 * self.half)).wait_recv()
            total = total + self.land(j)[...].astype(F32)
        return total

    def sent(self):
        all_sent(self.seven, self.send)


def call(kernel, outs, ins, scratch, name, number=None, vmem=56):
    extra = {} if number is None else dict(collective_id=number, has_side_effects=True)
    return pl.pallas_call(
        kernel,
        out_shape=[shape for shape, _ in outs],
        in_specs=ins,
        out_specs=[spec for _, spec in outs],
        scratch_shapes=scratch,
        name=name,
        compiler_params=pltpu.CompilerParams(vmem_limit_bytes=vmem * MIB, **extra),
    )


def chosen_units(values, seq):
    lane = lax.broadcasted_iota(jnp.int32, (values.shape[0], 128), 1)
    tiles = []
    for q in range(4):
        tile = jnp.zeros((values.shape[0], 128), F32)
        for p in range(8):
            at = 128 * (8 * q + p)
            shift = lax.rem(16 * p - 16 * seq + 128, 128)
            turned = pltpu.roll(values[:, at : at + 128], shift, 1)
            tile = jnp.where((lane // 16) == p, turned, tile)
        tiles.append(tile)
    return jnp.concatenate(tiles, axis=1)


def segment_cut(segment):
    return jnp.sum(jnp.where(segment[...] < 2, 1, 0))


def head_lanes(shape, dim, head):
    return (lax.broadcasted_iota(jnp.int32, shape, dim) // 64) == head


def masked_scores(scores, cut, q_tile, k_tile):
    shape = scores.shape
    key = k_tile * TILE + lax.broadcasted_iota(jnp.int32, shape, 0)
    query = q_tile * TILE + lax.broadcasted_iota(jnp.int32, shape, 1)
    allowed = key <= query
    if q_tile >= 2:
        allowed = allowed & ((key >= cut) | (query < cut))
    return jnp.where(allowed, scores, -1e30)


def tile_rows(tile):
    if isinstance(tile, int):
        return pl.ds(tile * TILE, TILE)
    return pl.ds(pl.multiple_of(tile * TILE, TILE), TILE)


def spread(src, dst, send, recv):
    x, core = axis("x"), axis("core")
    me = 2 * x + core
    for j in (2, 1, 3, 0):
        for i in range(2):
            if (j, i) != (0, 0):
                to_x, to_c = lax.rem(x + j, 4), lax.rem(core + i, 2)
                remote(src(2 * to_x + to_c), dst.at[me], send, recv, x=to_x, core=to_c).start()


def middle_kernel(
    x_own, w_qkv, w_out, w_fc, w_proj, bias_q, bias_v, bias_f, gain1, shift1, segment, cot, bo, gain,
    shift,
    xall_o, n1_out, qm_out, ktm_out, qkv_out, wq_out, o_out, lse, outp, mid_out, dm_out, do_all, gfc_out, gproj_out, gop_out,
    small_o, bfc_o, woz, wfz, wpz,
    w_fc_s, wq, wo_in, wf_in, wp_in, bias, bf, qkv, wq_o, o_o, mid_o, dm_o, gfc_o, gproj_o, gop_o, qm, vt, scores, xs, os, cs, wo, wf, wp, n2, da, act, part, from_core, total, from_side, land, dob,
    yp, p_mid, in_loc, loc, x_loc, out_loc, x_send, x_recv, z_send, z_recv, g_send, g_recv, c_send, c_recv, wo_send, wo_recv,
    y_send, y_recv, r_send, r_recv, a_send, a_recv, o_loc,
):
    x, core, y, z = axis("x"), axis("core"), axis("y"), axis("z")
    me = 2 * x + core
    ready = greet(seq_peers() + y_peers() + z_peers())
    span = pl.ds(pl.multiple_of(SPAN * me, SPAN), SPAN)
    inputs = [(w_fc, w_fc_s)]
    for k in range(3):
        at = pl.ds(pl.multiple_of(k * D + SPAN * me, SPAN), SPAN)
        inputs.append((w_qkv.at[:, at], wq.at[:, k * SPAN : (k + 1) * SPAN]))
    inputs.append((w_out.at[pl.ds(pl.multiple_of(16 * core, 16), 16)], wo_in))
    inputs.append((w_proj.at[pl.ds(pl.multiple_of(16 * me, 16), 16)], wp_in))
    inputs = [pltpu.make_async_copy(a, b, in_loc.at[k]) for k, (a, b) in enumerate(inputs)]
    for copy in inputs:
        copy.start()
    bias[:, :SPAN] = bias_q[:, span]
    bias[:, SPAN : 2 * SPAN] = jnp.zeros((1, SPAN), F32)
    bias[:, 2 * SPAN :] = bias_v[:, span]
    bf[...] = chosen_units(jnp.broadcast_to(bias_f[...], (8, 4 * D)), me)[0:1]
    for copy in inputs:
        copy.wait()
    wf_in[...] = chosen_units(w_fc_s[...].astype(F32), me).astype(LOW)
    cut = segment_cut(segment)
    written = []

    def write(src, dst):
        n = len(written)
        written.append(pltpu.make_async_copy(src, dst, out_loc.at[n]))
        written[-1].start()

    tokens = Gather(
        x_own, lambda t: xs.at[pl.ds(t * OWN, OWN)], xs.at[pl.ds(0, 7 * OWN)], OWN, x_send, x_recv
    )
    cots = Gather(cot, lambda t: cs.at[t], cs.at[pl.ds(0, 7)], OWN, c_send, c_recv)
    blocks = tokens.blocks
    half = wo.at[:, :, core]
    own_z = [(wq, wq_o.at[y, z]), (wo_in, woz.at[z]), (wf_in, wfz.at[z]), (wp_in, wpz.at[z])]
    whole_z = [wq_o.at[y], woz, wfz, wpz]
    local = own_z + [(x_own, xs.at[pl.ds(pl.multiple_of(OWN * me, OWN), OWN)]), (cot, cs.at[me])]
    local = [pltpu.make_async_copy(a, b, loc.at[k]) for k, (a, b) in enumerate(local)]
    for copy in local:
        copy.start()
    sends, own_y = [], {}

    def along_z(n):
        own, dst = own_z[n]
        for k in range(1, 8):
            remote(own, dst, z_send.at[n], z_recv.at[n], z=ahead("z", k, 8)).start()
        sends.append((whole_z[n].at[pl.ds(0, 7)], z_send.at[n]))

    def along_y(n):
        src, to = [(wq_o.at[y], wq_o), (woz, half), (wfz, wf), (wpz, wp)][n]
        for k in range(1, 4):
            remote(src, to.at[y], y_send.at[n], y_recv.at[n], y=ahead("y", k, 4)).start()
        sends.append((to.at[pl.ds(0, 3)], y_send.at[n]))
        if n:
            own_y[n] = pltpu.make_async_copy(src, to.at[y], loc.at[5 + n])
            own_y[n].start()

    def arrived(along, n):
        if along == "z":
            all_here(whole_z[n].at[pl.ds(0, 7)], z_recv.at[n])
        else:
            all_here((wq_o, half, wf, wp)[n].at[pl.ds(0, 3)], y_recv.at[n])
            if n:
                own_y[n].wait()

    ready()
    along_z(0)
    tokens.start()
    for copy in local:
        copy.wait()
    local = []

    def block_rows(block):
        return pl.ds(pl.multiple_of(OWN * block, OWN), OWN)

    def put(name):
        base = OWN * blocks[name]

        def one(i, _):
            rows = pl.ds(pl.multiple_of(base + i * 128, 128), 128)
            white, _inv = whitened(xs[rows, :].astype(F32))
            n2[rows, :] = (white * gain1[...] + shift1[...]).astype(LOW)
            return 0

        lax.fori_loop(0, OWN // 128, one, 0)
        rows = block_rows(blocks[name])
        pltpu.make_async_copy(xs.at[rows], xall_o.at[rows], x_loc.at[0]).start()
        pltpu.make_async_copy(n2.at[rows], n1_out.at[rows], x_loc.at[1]).start()

    def project(name):
        rows = block_rows(blocks[name])
        weights = wq_o[...].reshape(D, 3 * SPAN)
        qkv[rows, :] = (dot(n2[rows, :], weights) + bias[...]).astype(LOW)

    put("mine")
    arrived("z", 0)
    along_y(0)
    along_z(1)
    tokens.got(3)
    put("mine_o")
    arrived("z", 1)
    along_z(2)
    tokens.pass_left()
    tokens.pass_right()
    put("left")
    put("right")
    tokens.got(4)
    put("left_o")
    tokens.got(5)
    put("right_o")
    arrived("y", 0)
    along_y(1)
    write(wq_o, wq_out)
    for name in ("mine", "mine_o", "left", "right"):
        project(name)
    tokens.pass_far()
    cots.start()
    put("far")
    for name in ("left_o", "right_o", "far"):
        project(name)
    tokens.got(6)
    put("far_o")
    project("far_o")
    write(qkv, qkv_out)
    arrived("z", 2)
    along_z(3)
    along_y(2)
    for tile in range(4):
        rows = tile_rows(tile)
        q = qkv[rows, :SPAN].astype(F32) * 0.125
        v_t = jnp.transpose(qkv[rows, 2 * SPAN :].astype(F32))
        for head in range(2):
            qm[head, rows, :] = jnp.where(head_lanes(q.shape, 1, head), q, 0.0).astype(LOW)
            vt[head, :, rows] = jnp.where(head_lanes(v_t.shape, 0, head), v_t, 1.0).astype(LOW)

    def heads_of(tile):
        rows = tile_rows(tile)
        return Gather(
            o_o.at[rows],
            lambda t: os.at[t, rows],
            None,
            TILE,
            g_send,
            g_recv.at[pl.ds(4 * tile, 4)],
        )

    def pass_near(tile):
        gather = heads_of(tile)
        gather.pass_left()
        gather.pass_right()

    for tile in range(4):
        q_rows = tile_rows(tile)
        free = min(tile, 2)
        outs = []
        for head in range(2):

            def score(k_tile, peak, masked, tile=tile, q_rows=q_rows, head=head):
                rows = tile_rows(k_tile)
                s = dot_nt(qkv[rows, SPAN : 2 * SPAN], qm[head, q_rows, :])
                if masked:
                    s = masked_scores(s, cut, tile, k_tile)
                scores[rows, :] = s
                return jnp.maximum(peak, jnp.max(s, axis=0, keepdims=True))

            peak = jnp.full((1, TILE), -3e38, F32)
            for k_tile in range(tile + 1):
                peak = score(k_tile, peak, k_tile >= free)

            sums = jnp.zeros((SPAN, TILE), F32)
            for k_tile in range(tile + 1):
                rows = tile_rows(k_tile)
                e = jnp.exp(scores[rows, :] - peak).astype(LOW)
                sums = sums + dot(vt[head, :, rows], e)
            weight = sums[64:65] if head == 0 else sums[0:1]
            lse[head : head + 1, q_rows] = peak + jnp.log(weight)
            outs.append(sums[64 * head : 64 * (head + 1)] / weight)
        o_o[q_rows, :] = jnp.transpose(jnp.concatenate(outs, axis=0)).astype(LOW)
        pltpu.make_async_copy(o_o.at[q_rows], os.at[me, q_rows], o_loc).start()
        heads_of(tile).start()
        if tile >= 1:
            pass_near(tile - 1)
        if tile == 2:
            heads_of(0).pass_far()
        if tile == 1:
            arrived("y", 1)
            to_core = remote(half, half, wo_send, wo_recv, core=1 - core)
            to_core.start()
        if tile == 2:
            arrived("z", 3)
            along_y(3)
    write(o_o, o_out)
    pltpu.make_async_copy(xs, xall_o, x_loc.at[0]).wait()
    pltpu.make_async_copy(n2, n1_out, x_loc.at[1]).wait()
    pltpu.make_async_copy(o_o, os.at[me], o_loc).wait()
    tokens.sent()
    to_core.wait_recv()

    def middle_of(rows):
        left = jnp.concatenate([os[t, rows, :] for t in range(8)], axis=1)
        return xs[rows, :].astype(F32) + dot(left, wo[...].reshape(D, D)) + bo[...]

    def forward(b, _):
        rows = tile_rows(b)
        gather = heads_of(b)

        @pl.when(b == 0)
        def _():
            heads_of(1).pass_far()

        @pl.when(b == 1)
        def _():
            heads_of(2).pass_far()
            pass_near(3)
            cots.pass_left()
            cots.pass_right()

        @pl.when(b == 2)
        def _():
            heads_of(3).pass_far()

        @pl.when(b == 3)
        def _():
            cots.pass_far()

        gather.got_others(os.at[pl.ds(0, 4), rows])
        white, _inv = whitened(middle_of(rows))
        low = (white * gain[...] + shift[...]).astype(LOW)
        n2[rows, :] = low

        @pl.when(b == 0)
        def _():
            arrived("y", 2)

        v = dot(low, wf[...].reshape(D, HIDDEN)) + bf[...]
        square = v * v
        t = jnp.tanh(GELU_A * v * (1.0 + GELU_B * square))
        half = 0.5 * (1.0 + t)
        act[rows, :] = (v * half).astype(LOW)
        slope = 0.5 * GELU_A * (1.0 + 3.0 * GELU_B * square)
        da[rows, :] = (half + v * (1.0 - t * t) * slope).astype(LOW)
        return 0

    lax.fori_loop(0, 4, forward, 0)
    arrived("y", 3)
    cots.got_others(cs.at[pl.ds(0, 4)])
    reduce = Reduce(
        lambda t: part.at[t],
        lambda j: from_core.at[j],
        lambda j: total.at[j - 1],
        lambda j: from_side.at[j // 2],
        lambda j: land.at[j // 2],
        part.at[pl.ds(0, 7)],
        OWN,
        r_send,
        r_recv,
    )
    weights = wp[...].reshape(HIDDEN, D)
    bfc_o[...] = jnp.zeros_like(bfc_o)

    def backward(j):
        chip = lax.rem(x + j, 4)
        rows = tile_rows(chip)
        c_low = cs[pl.ds(2 * chip, 2)].reshape(TILE, D)
        low = (dot_nt(c_low, weights) * da[rows, :].astype(F32)).astype(LOW)
        da[rows, :] = low
        bfc_o[0:1, :] += jnp.sum(low.astype(F32), axis=0, keepdims=True)
        d_n2 = dot_nt(low, wf[...].reshape(D, HIDDEN))
        part[pl.ds(2 * chip, 2)] = d_n2.astype(LOW).reshape(2, OWN, D)

    order = (2, 1, 3, 0)

    def back_step(i, _):
        j = jnp.where(i == 0, 2, jnp.where(i == 1, 1, jnp.where(i == 2, 3, 0)))
        backward(j)
        for n, j in enumerate(order):

            @pl.when(i == n)
            def _(n=n, j=j):
                reduce.to_core(j)
                if n == 0:
                    reduce.to_far()
                if n == 2:
                    reduce.to_side_alone(1)
                if n == 3:
                    reduce.to_side_alone(3)
                    reduce.to_side_joined(1)
                    reduce.to_side_joined(3)

        return 0

    lax.fori_loop(0, 4, back_step, 0)
    own_rows = pl.ds(pl.multiple_of(me * OWN, OWN), OWN)
    middle = middle_of(own_rows)
    mid_o[...] = middle
    write(mid_o, mid_out)
    gproj_o[...] = dot_tn(act[...], cs[...].reshape(TOK, D)).astype(LOW)
    for k in range(1, 4):
        peer = ahead("y", k, 4)
        piece = gproj_o.at[pl.ds(pl.multiple_of(128 * peer, 128), 128)]
        remote(piece, yp.at[k], y_send.at[4], y_recv.at[4], y=peer).start()
    gfc_o[...] = dot_tn(n2[...], da[...]).astype(LOW)
    write(gfc_o, gfc_out)

    def output_part(b, _):
        rows = tile_rows(b)
        xs[rows, :] = dot(act[rows, :], weights).astype(LOW)
        return 0

    lax.fori_loop(0, 4, output_part, 0)
    write(xs, outp)
    white, inverse = whitened(mid_o[...])
    c_own = cs[me].astype(F32)
    d_n2 = reduce.result()
    d_m = c_own + norm_back(d_n2, gain[...], white, inverse)
    dm_o[...] = d_m
    low = d_m.astype(LOW)
    d_o = dot_nt(low, wo[...].reshape(D, D)).astype(LOW)
    for t in range(8):
        dob[t] = d_o[:, SPAN * t : SPAN * (t + 1)]
    spread(lambda t: dob.at[t], do_all, a_send, a_recv)
    write(qm, qm_out)
    for tile in range(4):
        rows = tile_rows(tile)
        k_t = jnp.transpose(qkv[rows, SPAN : 2 * SPAN].astype(F32))
        for head in range(2):
            vt[head, :, rows] = jnp.where(head_lanes(k_t.shape, 0, head), k_t, 0.0).astype(LOW)
    write(vt, ktm_out)
    write(dob.at[me], do_all.at[me])
    write(dm_o, dm_out)
    small_o[...] = jnp.zeros_like(small_o)
    small_o[0:1, :] = jnp.sum(low.astype(F32), axis=0, keepdims=True)
    small_o[1:2, :] = jnp.sum(d_n2 * white, axis=0, keepdims=True)
    small_o[2:3, :] = jnp.sum(d_n2, axis=0, keepdims=True)
    small_o[3:4, :] = jnp.sum(c_own, axis=0, keepdims=True)
    left = jnp.concatenate([os[t, own_rows, :] for t in range(8)], axis=1)
    g_out = dot_tn(left, low).astype(LOW)
    for t in range(2):
        gop_o[t] = g_out[:, HIDDEN * t : HIDDEN * (t + 1)]
    write(gop_o, gop_out)
    all_here(yp.at[pl.ds(0, 3)], y_recv.at[4])
    p_sum = gproj_o[pl.ds(pl.multiple_of(128 * y, 128), 128), :].astype(F32)
    for k in range(1, 4):
        p_sum = p_sum + yp[k].astype(F32)
    p_mid[...] = p_sum.astype(LOW)
    write(p_mid, gproj_out)
    all_here(do_all.at[pl.ds(0, 7)], a_recv)
    all_sent(dob.at[pl.ds(0, 7)], a_send)
    for ref, sem in sends:
        all_sent(ref, sem)
    all_sent(yp.at[pl.ds(0, 3)], y_send.at[4])
    to_core.wait_send()
    for copy in written:
        copy.wait()
    cots.sent()
    all_sent(os.at[pl.ds(0, 7)], g_send)
    reduce.sent()


def middle(
    x, w_qkv, w_out, w_fc, w_proj, bias_q, bias_v, bias_f, gain1, shift1, segment, cot, bo, gain, shift
):
    outs = [
        (shaped((TOK, D), LOW), ANYWHERE),
        (shaped((TOK, D), LOW), ANYWHERE),
        (shaped((2, TOK, SPAN), LOW), ANYWHERE),
        (shaped((2, SPAN, TOK), LOW), ANYWHERE),
        (shaped((TOK, 3 * SPAN), LOW), ANYWHERE),
        (shaped((4, 8, 32, 3 * SPAN), LOW), ANYWHERE),
        (shaped((TOK, SPAN), LOW), ANYWHERE),
        (shaped((2, TOK), F32), IN_VMEM),
        (shaped((TOK, D), LOW), ANYWHERE),
        (shaped((OWN, D), F32), ANYWHERE),
        (shaped((OWN, D), F32), ANYWHERE),
        (shaped((8, OWN, SPAN), LOW), ANYWHERE),
        (shaped((D, HIDDEN), LOW), ANYWHERE),
        (shaped((128, D), LOW), ANYWHERE),
        (shaped((2, D, HIDDEN), LOW), ANYWHERE),
        (shaped((8, D), F32), IN_VMEM),
        (shaped((8, HIDDEN), F32), IN_VMEM),
        (shaped((8, 16, D), LOW), ANYWHERE),
        (shaped((8, 32, HIDDEN), LOW), ANYWHERE),
        (shaped((8, 16, D), LOW), ANYWHERE),
    ]
    scratch = [
        pltpu.VMEM((32, 4 * D), LOW),
        pltpu.VMEM((32, 3 * SPAN), LOW),
        pltpu.VMEM((16, D), LOW),
        pltpu.VMEM((32, HIDDEN), LOW),
        pltpu.VMEM((16, D), LOW),
        pltpu.VMEM((1, 3 * SPAN), F32),
        pltpu.VMEM((1, HIDDEN), F32),
        pltpu.VMEM((TOK, 3 * SPAN), LOW),
        pltpu.VMEM((4, 8, 32, 3 * SPAN), LOW),
        pltpu.VMEM((TOK, SPAN), LOW),
        pltpu.VMEM((OWN, D), F32),
        pltpu.VMEM((OWN, D), F32),
        pltpu.VMEM((D, HIDDEN), LOW),
        pltpu.VMEM((HIDDEN, D), LOW),
        pltpu.VMEM((2, D, HIDDEN), LOW),
        pltpu.VMEM((2, TOK, SPAN), LOW),
        pltpu.VMEM((2, SPAN, TOK), LOW),
        pltpu.VMEM((TOK, TILE), F32),
        pltpu.VMEM((TOK, D), LOW),
        pltpu.VMEM((8, TOK, SPAN), LOW),
        pltpu.VMEM((8, OWN, D), LOW),
        pltpu.VMEM((4, 8, 2, 16, D), LOW),
        pltpu.VMEM((4, 8, 32, HIDDEN), LOW),
        pltpu.VMEM((4, 8, 16, D), LOW),
        pltpu.VMEM((TOK, D), LOW),
        pltpu.VMEM((TOK, HIDDEN), LOW),
        pltpu.VMEM((TOK, HIDDEN), LOW),
        pltpu.VMEM((8, OWN, D), LOW),
        pltpu.VMEM((4, OWN, D), LOW),
        pltpu.VMEM((3, OWN, D), LOW),
        pltpu.VMEM((2, OWN // 2, D), LOW),
        pltpu.VMEM((2, OWN, D), LOW),
        pltpu.VMEM((8, OWN, SPAN), LOW),
        pltpu.VMEM((4, 128, D), LOW),
        pltpu.VMEM((128, D), LOW),
        DMA((6,)), DMA((9,)), DMA((2,)), DMA((12,)), DMA, DMA((7,)), DMA((4,)), DMA((4,)),
        DMA, DMA((16,)), DMA, DMA((4,)), DMA, DMA,
        DMA((5,)), DMA((5,)), DMA, DMA((8,)), DMA, DMA, DMA,
    ]
    ins = [ANYWHERE] * 5 + [IN_VMEM] * 6 + [ANYWHERE] + [IN_VMEM] * 3
    return call(middle_kernel, outs, ins, scratch, "middle", 2, vmem=60)(
        x, w_qkv, w_out, w_fc, w_proj, bias_q[None], bias_v[None], bias_f[None], gain1[None],
        shift1[None], segment, cot, bo[None], gain[None], shift[None],
    )[:17]


def ending_kernel(
    qkv_in, qm_in, ktm_in, segment, do_in, o_in, lse, outp_in, x_all, n1_in, gop_in, gfc_in, p_mid_in, wq_in, mid_in, dm_in,
    gain, bp, small, bfc,
    out_o, dtok_o, fin_o, early_o, late_o,
    qkv, do_ref, o_own, gop, gfc, p_mid, wq, mid, dm, n1,
    qm, dom, ktm, delta, dqt, dk, dv, dqkv, outp, xs, part, g_acc, gq, go, rows1,
    so, sumo, eo, lo, g_side, sn, sumn, en, ln, yf, zf, zp, f_mid,
    gy, gz, g_mid, gv, gvz, gvy, v_mid, oy, oz, o_mid, fin,
    early_v, early_z, early_y, early_w, late_v, late_z, late_y, late_w, out_low, dtok,
    loc, o_loc, ro_send, ro_recv, g_send, g_recv, rn_send, rn_recv, y_send, y_recv, z_send, z_recv,
    f_send, f_recv, s_send, s_recv,
):
    x, core, y, z = axis("x"), axis("core"), axis("y"), axis("z")
    me = 2 * x + core
    ready = greet(seq_peers() + y_peers() + z_peers())
    loads = [
        (do_in, do_ref), (o_in, o_own), (qkv_in, qkv), (qm_in, qm), (ktm_in, ktm),
        (gop_in.at[core], gop), (gfc_in.at[pl.ds(pl.multiple_of(256 * y, 256), 256)], gfc),
        (p_mid_in, p_mid), (wq_in, wq), (n1_in, n1), (x_all, xs), (mid_in, mid),
        (dm_in, dm),
    ]
    loads += [(outp_in.at[2 * lax.rem(x + j, 4) + core], outp.at[j]) for j in range(4)]
    loads = [pltpu.make_async_copy(a, b, loc.at[k]) for k, (a, b) in enumerate(loads)]
    for copy in loads:
        copy.start()
    for ref in (dqt, dk, dv, g_acc, rows1):
        ref[...] = jnp.zeros_like(ref)
    cut = segment_cut(segment)
    for copy in loads[:2]:
        copy.wait()

    def prepare(tile, _):
        rows = tile_rows(tile)
        d_o = do_ref[rows, :].astype(F32)
        prod_t = jnp.transpose(d_o * o_own[rows, :].astype(F32))
        for head in range(2):
            lanes = head_lanes(d_o.shape, 1, head)
            dom[head, rows, :] = jnp.where(lanes, d_o, 0.0).astype(LOW)
            delta[head : head + 1, rows] = jnp.sum(
                prod_t[64 * head : 64 * (head + 1)], axis=0, keepdims=True
            )
        return 0

    lax.fori_loop(0, 4, prepare, 0)
    ready()
    for copy in loads[2:8]:
        copy.wait()
    r_out = Reduce(
        None, lambda j: so.at[j], lambda j: sumo.at[j - 1], lambda j: eo.at[j // 2],
        lambda j: lo.at[j // 2], outp_in.at[pl.ds(0, 7)], OWN, ro_send, ro_recv,
        source=lambda t: outp_in.at[t], mine=lambda j: outp.at[j],
    )
    r_dn1 = Reduce(
        lambda t: part.at[t], lambda j: sn.at[j], lambda j: sumn.at[j - 1], lambda j: en.at[j // 2],
        lambda j: ln.at[j // 2], part.at[pl.ds(0, 7)], OWN, rn_send, rn_recv,
    )
    to_core = remote(gop_in.at[1 - core], g_side, g_send, g_recv, core=1 - core)
    to_core.start()
    for j in (2, 1, 3, 0):
        r_out.to_core(j)
    sends = []

    def pieces_to_z(src, land, n):
        rows = land.shape[1]
        for k in range(1, 8):
            peer = ahead("z", k, 8)
            piece = src.at[pl.ds(pl.multiple_of(rows * peer, rows), rows)]
            remote(piece, land.at[k], z_send.at[n], z_recv.at[n], z=peer).start()
        sends.append((land.at[pl.ds(0, 7)], z_send.at[n]))

    def rows_to_y(src, land, n):
        rows = land.shape[1]
        for k in range(1, 4):
            peer = ahead("y", k, 4)
            piece = src.at[pl.ds(pl.multiple_of(rows * peer, rows), rows)]
            remote(piece, land.at[k], y_send.at[n], y_recv.at[n], y=peer).start()
        sends.append((land.at[pl.ds(0, 3)], y_send.at[n]))

    def from_y(src, land, n):
        rows = land.shape[1]
        all_here(land.at[pl.ds(0, 3)], y_recv.at[n])
        return summed(src[pl.ds(pl.multiple_of(rows * y, rows), rows), :], land, 4)

    def from_z(src, land, n):
        rows = land.shape[1]
        all_here(land.at[pl.ds(0, 7)], z_recv.at[n])
        return summed(src[pl.ds(pl.multiple_of(rows * z, rows), rows), :], land, 8)

    rows_to_y(gfc_in, yf, 0)
    pieces_to_z(p_mid, zp, 0)

    def vector_to_z(src, land, n):
        for k in range(1, 8):
            remote(src, land.at[z], z_send.at[n], z_recv.at[n], z=ahead("z", k, 8)).start()
        sends.append((land.at[pl.ds(0, 7)], z_send.at[n]))

    def vector_to_y(src, z_land, y_land, n):
        all_here(z_land.at[pl.ds(0, 7)], z_recv.at[n])
        z_land[z] = src[...]
        y_land[y] = summed(z_land[0], z_land, 8)
        for k in range(1, 4):
            peer = ahead("y", k, 4)
            remote(y_land.at[y], y_land.at[y], y_send.at[n], y_recv.at[n], y=peer).start()
        sends.append((y_land.at[pl.ds(0, 3)], y_send.at[n]))

    def vector_to_group(y_land, whole, out, n):
        all_here(y_land.at[pl.ds(0, 3)], y_recv.at[n])
        whole[...] = summed(y_land[0], y_land, 4)
        spread(lambda t: whole, out, s_send.at[n - 4], s_recv.at[n - 4])
        out[me] = whole[...]

    for k in range(8):
        lanes = slice(SPAN * k, SPAN * (k + 1))
        for n in range(4):
            early_v[8 * n + k : 8 * n + k + 1, :] = small[n : n + 1, lanes]
    early_v[32:40, :] = jnp.zeros((8, SPAN), F32)
    for k in range(4):
        early_v[32 + k : 33 + k, :] = bfc[0:1, SPAN * k : SPAN * (k + 1)]
    vector_to_z(early_v, early_z, 4)

    def order(n):
        j = jnp.where(n == 0, 2, jnp.where(n == 1, 1, jnp.where(n == 2, 3, 0)))
        return lax.rem(x + j, 4)

    def pair(first, second):
        q_tile, k_tile = jnp.maximum(first, second), jnp.minimum(first, second)
        q_rows, k_rows = tile_rows(q_tile), tile_rows(k_tile)
        keys, values = qkv[k_rows, SPAN : 2 * SPAN], qkv[k_rows, 2 * SPAN :]
        key = k_tile * TILE + lax.broadcasted_iota(jnp.int32, (TILE, 1), 0)
        query = q_tile * TILE + lax.broadcasted_iota(jnp.int32, (1, TILE), 1)
        key_code = jnp.where((key >= TOK // 2) & (key < cut), 1, 0)
        query_code = jnp.where(query >= cut, 1, 2)
        allowed = (key <= query) & (key_code < query_code)
        for head in range(2):
            q_h, do_h = qm[head, q_rows, :], dom[head, q_rows, :]
            s = jnp.where(allowed, dot_nt(keys, q_h), -1e30)
            p = jnp.exp(s - lse[head : head + 1, q_rows])
            d_p = dot_nt(values, do_h)
            d_s = (p * (d_p - delta[head : head + 1, q_rows])).astype(LOW)
            dv[k_rows, :] += dot(p.astype(LOW), do_h)
            dk[k_rows, :] += dot(d_s, q_h)
            dqt[q_tile] += dot(ktm[head, :, k_rows], d_s)

    def complete(tile):
        rows = tile_rows(tile)
        low = jnp.concatenate(
            [jnp.transpose(dqt[tile]) * 0.125, dk[rows, :], dv[rows, :]], axis=1
        ).astype(LOW)
        dqkv[rows, :] = low
        d_n1 = dot_nt(low, wq[...].reshape(D, 3 * SPAN))
        part[pl.ds(2 * tile, 2)] = d_n1.astype(LOW).reshape(2, OWN, D)

    def account(tile):
        rows = tile_rows(tile)
        g_acc[...] += dot_tn(n1[rows, :], dqkv[rows, :])

    def add_sums(tile, _):
        rows = tile_rows(tile)
        white, _inv = whitened(xs[rows, :].astype(F32))
        d_n1 = part[pl.ds(2 * tile, 2)].reshape(TILE, D).astype(F32)
        rows1[0:1, :] += jnp.sum(d_n1 * white, axis=0, keepdims=True)
        rows1[1:2, :] += jnp.sum(d_n1, axis=0, keepdims=True)
        wide = dqkv[rows, :].astype(F32)
        rows1[2:3, :SPAN] += jnp.sum(wide[:, :SPAN], axis=0, keepdims=True)
        rows1[3:4, :SPAN] += jnp.sum(wide[:, 2 * SPAN :], axis=0, keepdims=True)
        return 0

    def summed(own, others, count):
        total = own.astype(F32)
        for k in range(1, count):
            total = total + others[k].astype(F32)
        return total

    for step, j in enumerate((2, 1, 3, 0)):
        tile = order(step)

        def one(r, _, tile=tile):
            pair(tile, order(r))
            return 0

        if step == 0:
            lax.fori_loop(0, 2, one, 0)
            for copy in loads[8:]:
                copy.wait()
            r_out.to_far()
            to_core.wait_recv()
            go[...] = (gop[...].astype(F32) + g_side[...].astype(F32)).astype(LOW)
            rows_to_y(go, oy, 1)
            lax.fori_loop(2, 4, one, 0)
        else:
            lax.fori_loop(step, 4, one, 0)
        if step == 1:
            for side in (1, 3):
                r_out.to_side_alone(side)
            for side in (1, 3):
                r_out.to_side_joined(side)
        complete(tile)
        r_dn1.to_core(j)
        account(tile)
        if step == 0:
            r_dn1.to_far()
        if step == 1:
            r_dn1.to_side_alone(1)
            r_dn1.to_side_joined(1)
            all_here(yf.at[pl.ds(0, 3)], y_recv.at[0])
            f_mid[...] = summed(gfc[...], yf, 4).astype(LOW)
            pieces_to_z(f_mid, zf, 1)
            vector_to_y(early_v, early_z, early_y, 4)
        if step == 2:
            r_dn1.to_side_alone(3)
            r_dn1.to_side_joined(3)

    qk, v_at = slice(0, 2 * SPAN), slice(2 * SPAN, 3 * SPAN)
    gq[...] = g_acc[:, qk].astype(LOW)
    rows_to_y(gq, gy, 2)
    for k in range(32):
        at = 128 * (k % 8) + 32 * (k // 8)
        gv[at : at + 32, :] = g_acc[32 * k : 32 * k + 32, v_at].astype(LOW)
    pieces_to_z(gv, gvz, 2)
    lax.fori_loop(0, 4, add_sums, 0)
    for k in range(8):
        lanes = slice(SPAN * k, SPAN * (k + 1))
        for n in range(2):
            late_v[8 * n + k : 8 * n + k + 1, :] = rows1[n : n + 1, lanes]
    late_v[16:24, :] = rows1[0:8, :SPAN]
    vector_to_z(late_v, late_z, 5)

    def in_halves(row, total):
        fin[row : row + 16, :HIDDEN] = total[:16].astype(LOW)
        fin[row : row + 16, HIDDEN:] = total[16:].astype(LOW)

    o_mid[...] = from_y(go, oy, 1).astype(LOW)
    pieces_to_z(o_mid, oz, 3)
    fin[0:16, :] = from_z(p_mid, zp, 0).astype(LOW)
    in_halves(16, from_z(f_mid, zf, 1))
    early = pl.ds(0, 32)
    finals = Gather(
        fin.at[early],
        lambda t: fin_o.at[t, early],
        fin_o.at[pl.ds(0, 7), early],
        32,
        f_send.at[0],
        f_recv.at[pl.ds(0, 4)],
    )
    finals.start()
    written = []

    def write(src, dst):
        written.append(pltpu.make_async_copy(src, dst, o_loc.at[len(written)]))
        written[-1].start()

    write(fin.at[early], fin_o.at[me, early])
    g_mid[...] = from_y(gq, gy, 2).astype(LOW)
    pieces_to_z(g_mid, gz, 6)
    v_mid[...] = from_z(gv, gvz, 2).astype(LOW)
    rows_to_y(v_mid, gvy, 3)
    vector_to_y(late_v, late_z, late_y, 5)
    vector_to_group(early_y, early_w, early_o, 4)
    in_halves(32, from_z(o_mid, oz, 3))
    third = pl.ds(32, 16)
    spread(lambda t: fin.at[third], fin_o.at[:, third], f_send.at[2], f_recv.at[5])
    write(fin.at[third], fin_o.at[me, third])
    finals.pass_left()
    finals.pass_right()
    vector_to_group(late_y, late_w, late_o, 5)
    own_rows = pl.ds(pl.multiple_of(me * OWN, OWN), OWN)
    white, inverse = whitened(xs[own_rows, :].astype(F32))
    out_low[...] = (mid[...] + r_out.result() + bp[...]).astype(LOW)
    write(out_low, out_o)
    total = from_z(g_mid, gz, 6)
    fin[48:64, 0 : 2 * SPAN] = total[:16].astype(LOW)
    fin[48:64, HIDDEN : HIDDEN + 2 * SPAN] = total[16:].astype(LOW)
    total = from_y(v_mid, gvy, 3)
    fin[48:64, v_at] = total[:16].astype(LOW)
    fin[48:64, HIDDEN + 2 * SPAN : HIDDEN + 3 * SPAN] = total[16:].astype(LOW)
    fin[48:64, 3 * SPAN : HIDDEN] = jnp.zeros((16, SPAN), LOW)
    fin[48:64, HIDDEN + 3 * SPAN :] = jnp.zeros((16, SPAN), LOW)
    late = pl.ds(48, 16)
    spread(lambda t: fin.at[late], fin_o.at[:, late], f_send.at[1], f_recv.at[4])
    write(fin.at[late], fin_o.at[me, late])
    finals.pass_far()
    d_n1 = r_dn1.result()
    dtok[...] = dm[...] + norm_back(d_n1, gain[...], white, inverse)
    write(dtok, dtok_o)
    finals.got_others(fin_o.at[pl.ds(0, 4), early])
    all_here(early_o.at[pl.ds(0, 7)], s_recv.at[0])
    all_here(late_o.at[pl.ds(0, 7)], s_recv.at[1])
    all_here(fin_o.at[pl.ds(0, 7), third], f_recv.at[5])
    all_here(fin_o.at[pl.ds(0, 7), late], f_recv.at[4])
    finals.sent()
    all_sent(fin_o.at[pl.ds(0, 7), late], f_send.at[1])
    all_sent(fin_o.at[pl.ds(0, 7), third], f_send.at[2])
    all_sent(early_o.at[pl.ds(0, 7)], s_send.at[0])
    all_sent(late_o.at[pl.ds(0, 7)], s_send.at[1])
    for ref, sem in sends:
        all_sent(ref, sem)
    to_core.wait_send()
    for copy in written:
        copy.wait()
    for reduce in (r_out, r_dn1):
        reduce.sent()


def reduce_scratch(rows, columns):
    return [
        pltpu.VMEM((4, rows, columns), LOW),
        pltpu.VMEM((3, rows, columns), LOW),
        pltpu.VMEM((2, rows // 2, columns), LOW),
        pltpu.VMEM((2, rows, columns), LOW),
    ]


def ending(
    qkv, qm, ktm, segment, d_o, o_own, lse, outp, x_all, n1, gop, gfc, gproj, wq, mid, dm, gain, bp, small,
    bfc,
):
    outs = [
        (shaped((OWN, D), LOW), ANYWHERE),
        (shaped((OWN, D), F32), ANYWHERE),
        (shaped((8, 64, D), LOW), ANYWHERE),
        (shaped((8, 40, SPAN), F32), IN_VMEM),
        (shaped((8, 24, SPAN), F32), IN_VMEM),
    ]
    scratch = [
        pltpu.VMEM((TOK, 3 * SPAN), LOW),
        pltpu.VMEM((TOK, SPAN), LOW),
        pltpu.VMEM((TOK, SPAN), LOW),
        pltpu.VMEM((D, HIDDEN), LOW),
        pltpu.VMEM((256, HIDDEN), LOW),
        pltpu.VMEM((128, D), LOW),
        pltpu.VMEM((4, 8, 32, 3 * SPAN), LOW),
        pltpu.VMEM((OWN, D), F32),
        pltpu.VMEM((OWN, D), F32),
        pltpu.VMEM((TOK, D), LOW),
        pltpu.VMEM((2, TOK, SPAN), LOW),
        pltpu.VMEM((2, TOK, SPAN), LOW),
        pltpu.VMEM((2, SPAN, TOK), LOW),
        pltpu.VMEM((2, TOK), F32),
        pltpu.VMEM((4, SPAN, TILE), F32),
        pltpu.VMEM((TOK, SPAN), F32),
        pltpu.VMEM((TOK, SPAN), F32),
        pltpu.VMEM((TOK, 3 * SPAN), LOW),
        pltpu.VMEM((4, OWN, D), LOW),
        pltpu.VMEM((TOK, D), LOW),
        pltpu.VMEM((8, OWN, D), LOW),
        pltpu.VMEM((D, 3 * SPAN), F32),
        pltpu.VMEM((D, 2 * SPAN), LOW),
        pltpu.VMEM((D, HIDDEN), LOW),
        pltpu.VMEM((8, D), F32),
        *reduce_scratch(OWN, D), pltpu.VMEM((D, HIDDEN), LOW), *reduce_scratch(OWN, D),
        pltpu.VMEM((4, 256, HIDDEN), LOW),
        pltpu.VMEM((8, 32, HIDDEN), LOW), pltpu.VMEM((8, 16, D), LOW),
        pltpu.VMEM((256, HIDDEN), LOW),
        pltpu.VMEM((4, 256, 2 * SPAN), LOW),
        pltpu.VMEM((8, 32, 2 * SPAN), LOW),
        pltpu.VMEM((256, 2 * SPAN), LOW),
        pltpu.VMEM((D, SPAN), LOW),
        pltpu.VMEM((8, 128, SPAN), LOW),
        pltpu.VMEM((4, 32, SPAN), LOW),
        pltpu.VMEM((128, SPAN), LOW),
        pltpu.VMEM((4, 256, HIDDEN), LOW),
        pltpu.VMEM((8, 32, HIDDEN), LOW),
        pltpu.VMEM((256, HIDDEN), LOW),
        pltpu.VMEM((64, D), LOW),
        *[
            pltpu.VMEM((*lead, rows, SPAN), F32)
            for rows in (40, 24)
            for lead in ((), (8,), (4,), ())
        ],
        pltpu.VMEM((OWN, D), LOW),
        pltpu.VMEM((OWN, D), F32),
        DMA((17,)), DMA((5,)), DMA, DMA((8,)), DMA, DMA, DMA, DMA((8,)),
        DMA((6,)), DMA((6,)), DMA((7,)), DMA((7,)), DMA((3,)), DMA((6,)), DMA((2,)), DMA((2,)),
    ]
    ins = [ANYWHERE] * 3 + [IN_VMEM, ANYWHERE, ANYWHERE, IN_VMEM] + [ANYWHERE] * 9 + [IN_VMEM] * 4
    return call(ending_kernel, outs, ins, scratch, "ending", 4, vmem=60)(
        qkv, qm, ktm, segment, d_o.reshape(TOK, SPAN), o_own, lse, outp.reshape(8, OWN, D), x_all, n1,
        gop, gfc, gproj, wq, mid, dm, gain[None], bp[None], small, bfc,
    )


def results_kernel(
    fin, early, late, out, dtok, out_o, dtok_o, gq_out, go_out, gf_out, gp_out, *rest
):
    vectors, bf_o, out_s, dtok_s, gq_o, go_o, gf_o, gp_o, loc = rest[:8], *rest[8:]
    inward = [
        pltpu.make_async_copy(out, out_s, loc.at[0]),
        pltpu.make_async_copy(dtok, dtok_s, loc.at[1]),
    ]
    outward = [
        pltpu.make_async_copy(out_s, out_o, loc.at[2]),
        pltpu.make_async_copy(dtok_s, dtok_o, loc.at[3]),
    ]
    for copy in inward:
        copy.start()
    lane = lax.broadcasted_iota(jnp.int32, (40, 128), 1) // 16
    units = []
    for t in range(8):
        gp_o[16 * t : 16 * (t + 1), :] = fin[t, 0:16, :].astype(F32)
        span = slice(SPAN * t, SPAN * (t + 1))
        for half in range(2):
            rows = slice(16 * half, 16 * (half + 1))
            at = HIDDEN * half
            for k in range(3):
                gq_o[rows, D * k + SPAN * t : D * k + SPAN * (t + 1)] = fin[
                    t, 48:64, at + SPAN * k : at + SPAN * (k + 1)
                ].astype(F32)
        bias = jnp.concatenate([early[t, 32 + k : 33 + k, :] for k in range(4)], axis=1)
        units.append(
            jnp.concatenate(
                [
                    fin[t, 16:32, :HIDDEN].astype(F32),
                    fin[t, 16:32, HIDDEN:].astype(F32),
                    jnp.broadcast_to(bias, (8, HIDDEN)),
                ],
                axis=0,
            )
        )
        for k in range(2):
            vectors[6 + k][:, span] = late[t, 18 + k : 19 + k, :]
    early_sum, late_sum = early[0], late[0]
    for t in range(1, 8):
        early_sum, late_sum = early_sum + early[t], late_sum + late[t]
    for k in range(8):
        span = slice(SPAN * k, SPAN * (k + 1))
        for n in range(2):
            vectors[n][:, span] = late_sum[8 * n + k : 8 * n + k + 1, :]
        for n in range(4):
            vectors[2 + n][:, span] = early_sum[8 * n + k : 8 * n + k + 1, :]
    for core in range(2):
        for half in range(2):
            at = slice(HIDDEN * half, HIDDEN * (half + 1))
            total = fin[core, 32:48, at].astype(F32)
            for chip in range(1, 4):
                total = total + fin[2 * chip + core, 32:48, at].astype(F32)
            go_o[16 * half : 16 * (half + 1), HIDDEN * core : HIDDEN * (core + 1)] = total
    for into, out_of in zip(inward, outward):
        into.wait()
        out_of.start()
    for src, dst in ((gq_o, gq_out), (go_o, go_out), (gp_o, gp_out)):
        outward.append(pltpu.make_async_copy(src, dst, loc.at[2 + len(outward)]))
        outward[-1].start()
    for s in range(32):
        q, p = s // 8, s % 8
        tile = jnp.zeros((40, 128), F32)
        for t in range(8):
            turned = pltpu.roll(units[t][:, 128 * q : 128 * (q + 1)], (16 * t - 16 * p) % 128, 1)
            tile = jnp.where(lane == t, turned, tile)
        gf_o[:, 128 * s : 128 * (s + 1)] = tile[:32]
        bf_o[:, 128 * s : 128 * (s + 1)] = tile[32:33]
        if s % 8 == 7:
            part = slice(D * (s // 8), D * (s // 8 + 1))
            outward.append(
                pltpu.make_async_copy(
                    gf_o.at[:, part], gf_out.at[:, part], loc.at[2 + len(outward)]
                )
            )
            outward[-1].start()
    for copy in outward:
        copy.wait()


def results(fin, early, late, out, dtok):
    outs = [
        (shaped((OWN, D), LOW), ANYWHERE),
        (shaped((OWN, D), F32), ANYWHERE),
        (shaped((32, 3 * D), F32), ANYWHERE),
        (shaped((32, D), F32), ANYWHERE),
        (shaped((32, 4 * D), F32), ANYWHERE),
        (shaped((128, D), F32), ANYWHERE),
    ]
    narrow = (shaped((1, D), F32), IN_VMEM)
    outs += [narrow] * 8 + [(shaped((1, 4 * D), F32), IN_VMEM)]
    ins = [IN_VMEM, IN_VMEM, IN_VMEM, ANYWHERE, ANYWHERE]
    scratch = [
        pltpu.VMEM((OWN, D), LOW),
        pltpu.VMEM((OWN, D), F32),
        pltpu.VMEM((32, 3 * D), F32),
        pltpu.VMEM((32, D), F32),
        pltpu.VMEM((32, 4 * D), F32),
        pltpu.VMEM((128, D), F32),
        DMA((11,)),
    ]
    return call(results_kernel, outs, ins, scratch, "results")(fin, early, late, out, dtok)


def per_device(
    tokens, segment, ln1_gain, ln1_shift, w_qkv, bias_query, bias_value, w_out, bias_out,
    ln2_gain, ln2_shift, w_fc, bias_fc, w_proj, bias_proj, cotangent,
):
    (
        x_all, n1, qm, ktm, qkv, wq, o_own, lse, outp, mid, dm, do_all, gfc, gproj, gop, small, bfc,
    ) = middle(
        tokens[0], w_qkv, w_out, w_fc, w_proj, bias_query, bias_value, bias_fc, ln1_gain, ln1_shift,
        segment, cotangent[0], bias_out, ln2_gain, ln2_shift,
    )
    out, dtok, fin, early, late = ending(
        qkv, qm, ktm, segment, do_all, o_own, lse, outp, x_all, n1, gop, gfc, gproj, wq, mid, dm,
        ln1_gain, bias_proj, small, bfc,
    )
    out, dtok, gq, go, gf, gp, *vectors = results(fin, early, late, out, dtok)
    v = [vector[0] for vector in vectors]
    return (
        out[None], dtok[None], v[0], v[1], gq, v[6], v[7], go, v[2], v[3], v[4], gf, v[8], gp, v[5],
    )


def solution(mesh):
    finer = Mesh(mesh.devices.reshape(4, 2, 4, 8), ("x", "core", "y", "z"))
    rows, whole = P(SHARD, None), P()
    tokens = P(SHARD, SEQ, None)
    return jax.shard_map(
        per_device,
        mesh=finer,
        in_specs=(
            tokens, rows, whole, whole, rows, whole, whole, rows, whole, whole, whole, rows,
            whole, rows, whole, tokens,
        ),
        out_specs=(
            tokens, tokens, whole, whole, rows, whole, whole, rows, whole, whole, whole, rows,
            whole, rows, whole,
        ),
        check_vma=False,
    )
```

```python
import functools

import jax
import jax.numpy as jnp
from jax import lax
from jax.experimental import pallas as pl
from jax.experimental.pallas import tpu as pltpu
from jax.sharding import Mesh
from jax.sharding import PartitionSpec as P

SEQ = ("x", "core")
SHARD = ("y", "z")
F32 = jnp.float32
LOW = jnp.bfloat16
MIB = 2**20
TOK = 2048
OWN = 256
TILE = 512
D = 1024
HIDDEN = 512
SPAN = 128
GELU_A = 0.7978845608028654
GELU_B = 0.044715

IN_VMEM = pl.BlockSpec(memory_space=pltpu.VMEM)
IN_SMEM = pl.BlockSpec(memory_space=pltpu.SMEM)
ANYWHERE = pl.BlockSpec(memory_space=pl.ANY)
DMA = pltpu.SemaphoreType.DMA


def shaped(shape, dtype):
    return jax.ShapeDtypeStruct(shape, dtype)


def remote(src, dst, send, recv, **device):
    return pltpu.make_async_remote_copy(
        src_ref=src,
        dst_ref=dst,
        send_sem=send,
        recv_sem=recv,
        device_id=device,
        device_id_type=pl.DeviceIdType.MESH,
    )


def axis(name):
    return lax.axis_index(name)


def ahead(name, k, count):
    return lax.rem(axis(name) + k, count)


def seq_peers():
    core = axis("core")
    return [
        {"x": ahead("x", j, 4), "core": lax.rem(core + i, 2)}
        for j in range(4)
        for i in range(2)
        if (j, i) != (0, 0)
    ]


def near_peers():
    return [{"x": ahead("x", 1, 4)}, {"x": ahead("x", 3, 4)}, {"core": 1 - axis("core")}]


def y_peers():
    return [{"y": ahead("y", k, 4)} for k in range(1, 4)]


def z_peers():
    return [{"z": ahead("z", k, 8)} for k in range(1, 8)]


def greet(peers):
    sem = pltpu.get_barrier_semaphore()
    for peer in peers:
        pl.semaphore_signal(sem, inc=1, device_id=peer, device_id_type=pl.DeviceIdType.MESH)
    return lambda: pl.semaphore_wait(sem, len(peers))


def dot(a, b):
    return jnp.dot(a, b, preferred_element_type=F32)


def dot_nt(a, b):
    return lax.dot_general(a, b, (((1,), (1,)), ((), ())), preferred_element_type=F32)


def dot_tn(a, b):
    return lax.dot_general(a, b, (((0,), (0,)), ((), ())), preferred_element_type=F32)


def whitened(values):
    mean = jnp.mean(values, axis=-1, keepdims=True)
    centered = values - mean
    spread = jnp.mean(centered * centered, axis=-1, keepdims=True)
    inverse = lax.rsqrt(spread + 1e-05)
    return centered * inverse, inverse


def norm_back(grad, gain, white, inverse):
    d_white = grad * gain
    first = jnp.mean(d_white, axis=-1, keepdims=True)
    second = jnp.mean(d_white * white, axis=-1, keepdims=True)
    return inverse * (d_white - first - white * second)


class Gather:
    def __init__(self, src, at, seven, rows, send, recv, cut=None):
        x, core = axis("x"), axis("core")
        other = 1 - core
        right, far, left = (lax.rem(x + k, 4) for k in (1, 2, 3))
        cut = cut or rows // 2
        low, high = pl.ds(0, cut), pl.ds(cut, rows - cut)
        mine, r, f, l = (at(2 * k + core) for k in (x, right, far, left))
        self.seven = seven
        self.send, self.recv = send, recv
        self.single = recv.shape[0] == 4
        slots = (0, 1, 3, 2, 2) + ((3, 3, 3) if self.single else (4, 5, 6))
        self.plan = [
            (src, mine, {"x": right}),
            (src, mine, {"x": left}),
            (src, mine, {"core": other}),
            (l.at[low], l.at[low], {"x": right}),
            (r.at[high], r.at[high], {"x": left}),
            (l, l, {"core": other}),
            (r, r, {"core": other}),
            (f, f, {"core": other}),
        ]
        self.slots = slots
        self.block = mine
        self.blocks = dict(
            mine=2 * x + core,
            mine_o=2 * x + other,
            left=2 * left + core,
            left_o=2 * left + other,
            right=2 * right + core,
            right_o=2 * right + other,
            far=2 * far + core,
            far_o=2 * far + other,
        )

    def copy(self, k):
        src, dst, device = self.plan[k]
        return remote(src, dst, self.send, self.recv.at[self.slots[k]], **device)

    def start(self):
        for k in (0, 1, 2):
            self.copy(k).start()

    def got(self, slot):
        remote(self.block, self.block, self.send, self.recv.at[slot], core=0).wait_recv()

    def got_others(self, four):
        remote(four, four, self.send, self.recv.at[3], core=0).wait_recv()

    def pass_left(self):
        self.got(0)
        self.copy(3).start()
        self.copy(5).start()

    def pass_right(self):
        self.got(1)
        self.copy(4).start()
        self.copy(6).start()

    def pass_far(self):
        self.got(2)
        self.copy(7).start()

    def sent(self):
        remote(self.seven, self.seven, self.send, self.recv.at[0], core=0).wait_send()


def all_sent(ref, send):
    remote(ref, ref, send, send, core=0).wait_send()


def all_here(ref, recv):
    remote(ref, ref, recv, recv, core=0).wait_recv()


class Reduce:
    def __init__(self, part, from_core, total, from_side, land, seven, rows, send, recv, mine=None, exchanged=False):
        self.seven = seven
        self.exchanged = exchanged
        self.mine = mine or (lambda j: part(2 * self.chip(j) + self.core))
        self.part, self.from_core, self.total = part, from_core, total
        self.from_side, self.land = from_side, land
        self.send, self.recv = send, recv
        self.x, self.core = axis("x"), axis("core")
        self.half = rows // 2

    def chip(self, j):
        return lax.rem(self.x + j, 4)

    def core_copy(self, j):
        return remote(
            self.part(2 * self.chip(j) + 1 - self.core),
            self.from_core(j),
            self.send,
            self.recv.at[j],
            core=1 - self.core,
        )

    def side_copy(self, j):
        rows = pl.ds(0 if j == 1 else self.half, self.half)
        n = 4 + j // 2
        return remote(
            self.total(2).at[rows],
            self.from_side(j),
            self.send,
            self.recv.at[n],
            x=self.chip(j),
        )

    def chip_copy(self, j, rows):
        n = 6 + j // 2
        return remote(
            self.total(j).at[rows],
            self.land(j).at[rows],
            self.send,
            self.recv.at[n],
            x=self.chip(j),
        )

    def pair(self, j, rows):
        return self.mine(j)[rows, :].astype(F32) + self.from_core(j)[rows, :].astype(F32)

    def to_core(self, j):
        self.core_copy(j).start()

    def core_here(self, j):
        if not self.exchanged:
            self.core_copy(j).wait_recv()

    def to_far(self):
        self.core_here(2)
        self.total(2)[...] = self.pair(2, slice(None)).astype(LOW)
        self.side_copy(1).start()
        self.side_copy(3).start()

    def halves(self, j):
        low, high = pl.ds(0, self.half), pl.ds(self.half, self.half)
        return (low, high) if j == 1 else (high, low)

    def to_side_alone(self, j):
        self.core_here(j)
        rows = self.halves(j)[1]
        self.total(j)[rows, :] = self.pair(j, rows).astype(LOW)
        self.chip_copy(j, rows).start()

    def to_side_joined(self, j):
        self.side_copy(j).wait_recv()
        rows = self.halves(j)[0]
        more = self.from_side(j)[...].astype(F32)
        self.total(j)[rows, :] = (self.pair(j, rows) + more).astype(LOW)
        self.chip_copy(j, rows).start()

    def result(self):
        self.core_here(0)
        total = self.pair(0, slice(None))
        for j in (1, 3):
            self.chip_copy(j, pl.ds(0, 2 * self.half)).wait_recv()
            total = total + self.land(j)[...].astype(F32)
        return total

    def sent(self):
        all_sent(self.seven, self.send)


def call(kernel, outs, ins, scratch, name, number=None, vmem=56):
    extra = {} if number is None else dict(collective_id=number, has_side_effects=True)
    return pl.pallas_call(
        kernel,
        out_shape=[shape for shape, _ in outs],
        in_specs=ins,
        out_specs=[spec for _, spec in outs],
        scratch_shapes=scratch,
        name=name,
        compiler_params=pltpu.CompilerParams(vmem_limit_bytes=vmem * MIB, **extra),
    )


def chosen_units(values, seq):
    lane = lax.broadcasted_iota(jnp.int32, (values.shape[0], 128), 1)
    tiles = []
    for q in range(4):
        tile = jnp.zeros((values.shape[0], 128), F32)
        for p in range(8):
            at = 128 * (8 * q + p)
            shift = lax.rem(16 * p - 16 * seq + 128, 128)
            turned = pltpu.roll(values[:, at : at + 128], shift, 1)
            tile = jnp.where((lane // 16) == p, turned, tile)
        tiles.append(tile)
    return jnp.concatenate(tiles, axis=1)


def segment_cut(segment):
    return jnp.sum(jnp.where(segment[...] < 2, 1, 0))


def head_lanes(shape, dim, head):
    return (lax.broadcasted_iota(jnp.int32, shape, dim) // 64) == head


def masked_scores(scores, cut, q_tile, k_tile):
    shape = scores.shape
    key = k_tile * TILE + lax.broadcasted_iota(jnp.int32, shape, 0)
    query = q_tile * TILE + lax.broadcasted_iota(jnp.int32, shape, 1)
    allowed = key <= query
    if q_tile >= 2:
        allowed = allowed & ((key >= cut) | (query < cut))
    return jnp.where(allowed, scores, -1e30)


def tile_rows(tile):
    if isinstance(tile, int):
        return pl.ds(tile * TILE, TILE)
    return pl.ds(pl.multiple_of(tile * TILE, TILE), TILE)


def spread(src, dst, send, recv):
    x, core = axis("x"), axis("core")
    me = 2 * x + core
    for j in (2, 1, 3, 0):
        for i in range(2):
            if (j, i) != (0, 0):
                to_x, to_c = lax.rem(x + j, 4), lax.rem(core + i, 2)
                remote(src(2 * to_x + to_c), dst.at[me], send, recv, x=to_x, core=to_c).start()


def middle_kernel(
    x_own, w_qkv, w_out, w_fc, w_proj, bias_q, bias_v, bias_f, gain1, shift1, segment, cot, bo, gain,
    shift,
    xall_o, n1_out, qm_out, ktm_out, qkv_out, wq_out, o_out, lse, outp, mid_out, dm_out, do_all, gfc_out, gproj_out, gop_out,
    small_o, bfc_o, outp_o, gop_other, p_out, fz_out, woz, wfz, wpz,
    w_fc_s, wq, wo_in, wf_in, wp_in, bias, bf, qkv, wq_o, o_o, mid_o, dm_o, gfc_o, gproj_o, gop_o, qm, vt, scores, xs, os, cs, wo, wf, wp, n2, da, act, part, from_core, total, from_side, land, dob,
    yp, p_mid, fz, fz_sum, in_loc, loc, x_loc, out_loc, x_send, x_recv, z_send, z_recv, g_send, g_recv, c_send, c_recv, wo_send, wo_recv,
    y_send, y_recv, r_send, r_recv, a_send, a_recv, o_loc, ro_send, ro_recv, go_send, go_recv, p_loc,
):
    x, core, y, z = axis("x"), axis("core"), axis("y"), axis("z")
    me = 2 * x + core
    ready = greet(seq_peers() + y_peers() + z_peers())
    span = pl.ds(pl.multiple_of(SPAN * me, SPAN), SPAN)
    inputs = [(w_fc, w_fc_s)]
    for k in range(3):
        at = pl.ds(pl.multiple_of(k * D + SPAN * me, SPAN), SPAN)
        inputs.append((w_qkv.at[:, at], wq.at[:, k * SPAN : (k + 1) * SPAN]))
    inputs.append((w_out.at[pl.ds(pl.multiple_of(16 * core, 16), 16)], wo_in))
    inputs.append((w_proj.at[pl.ds(pl.multiple_of(16 * me, 16), 16)], wp_in))
    inputs = [pltpu.make_async_copy(a, b, in_loc.at[k]) for k, (a, b) in enumerate(inputs)]
    for copy in inputs:
        copy.start()
    bias[:, :SPAN] = bias_q[:, span]
    bias[:, SPAN : 2 * SPAN] = jnp.zeros((1, SPAN), F32)
    bias[:, 2 * SPAN :] = bias_v[:, span]
    bf[...] = chosen_units(jnp.broadcast_to(bias_f[...], (8, 4 * D)), me)[0:1]
    for copy in inputs:
        copy.wait()
    wf_in[...] = chosen_units(w_fc_s[...].astype(F32), me).astype(LOW)
    cut = segment_cut(segment)
    written = []

    def write(src, dst):
        n = len(written)
        written.append(pltpu.make_async_copy(src, dst, out_loc.at[n]))
        written[-1].start()

    tokens = Gather(
        x_own, lambda t: xs.at[pl.ds(t * OWN, OWN)], xs.at[pl.ds(0, 7 * OWN)], OWN, x_send, x_recv
    )
    cots = Gather(cot, lambda t: cs.at[t], cs.at[pl.ds(0, 7)], OWN, c_send, c_recv)
    blocks = tokens.blocks
    half = wo.at[:, :, core]
    own_z = [(wq, wq_o.at[y, z]), (wo_in, woz.at[z]), (wf_in, wfz.at[z]), (wp_in, wpz.at[z])]
    whole_z = [wq_o.at[y], woz, wfz, wpz]
    local = own_z + [(x_own, xs.at[pl.ds(pl.multiple_of(OWN * me, OWN), OWN)]), (cot, cs.at[me])]
    local = [pltpu.make_async_copy(a, b, loc.at[k]) for k, (a, b) in enumerate(local)]
    for copy in local:
        copy.start()
    sends, own_y = [], {}

    def along_z(n):
        own, dst = own_z[n]
        for k in range(1, 8):
            remote(own, dst, z_send.at[n], z_recv.at[n], z=ahead("z", k, 8)).start()
        sends.append((whole_z[n].at[pl.ds(0, 7)], z_send.at[n]))

    def along_y(n):
        src, to = [(wq_o.at[y], wq_o), (woz, half), (wfz, wf), (wpz, wp)][n]
        for k in range(1, 4):
            remote(src, to.at[y], y_send.at[n], y_recv.at[n], y=ahead("y", k, 4)).start()
        sends.append((to.at[pl.ds(0, 3)], y_send.at[n]))
        if n:
            own_y[n] = pltpu.make_async_copy(src, to.at[y], loc.at[5 + n])
            own_y[n].start()

    def arrived(along, n):
        if along == "z":
            all_here(whole_z[n].at[pl.ds(0, 7)], z_recv.at[n])
        else:
            all_here((wq_o, half, wf, wp)[n].at[pl.ds(0, 3)], y_recv.at[n])
            if n:
                own_y[n].wait()

    ready()
    along_z(0)
    tokens.start()
    for copy in local:
        copy.wait()
    local = []

    def block_rows(block):
        return pl.ds(pl.multiple_of(OWN * block, OWN), OWN)

    def put(name):
        base = OWN * blocks[name]

        def one(i, _):
            rows = pl.ds(pl.multiple_of(base + i * 128, 128), 128)
            white, _inv = whitened(xs[rows, :].astype(F32))
            n2[rows, :] = (white * gain1[...] + shift1[...]).astype(LOW)
            return 0

        lax.fori_loop(0, OWN // 128, one, 0)
        rows = block_rows(blocks[name])
        pltpu.make_async_copy(xs.at[rows], xall_o.at[rows], x_loc.at[0]).start()
        pltpu.make_async_copy(n2.at[rows], n1_out.at[rows], x_loc.at[1]).start()

    def project(name):
        rows = block_rows(blocks[name])
        weights = wq_o[...].reshape(D, 3 * SPAN)
        qkv[rows, :] = (dot(n2[rows, :], weights) + bias[...]).astype(LOW)

    put("mine")
    arrived("z", 0)
    along_y(0)
    along_z(1)
    tokens.got(3)
    put("mine_o")
    arrived("z", 1)
    along_z(2)
    tokens.pass_left()
    tokens.pass_right()
    put("left")
    put("right")
    tokens.got(4)
    put("left_o")
    tokens.got(5)
    put("right_o")
    arrived("y", 0)
    along_y(1)
    write(wq_o, wq_out)
    for name in ("mine", "mine_o", "left", "right"):
        project(name)
    tokens.pass_far()
    cots.start()
    put("far")
    for name in ("left_o", "right_o", "far"):
        project(name)
    tokens.got(6)
    put("far_o")
    project("far_o")
    write(qkv, qkv_out)
    arrived("z", 2)
    along_z(3)
    along_y(2)
    for tile in range(4):
        rows = tile_rows(tile)
        q = qkv[rows, :SPAN].astype(F32) * 0.125
        v_t = jnp.transpose(qkv[rows, 2 * SPAN :].astype(F32))
        for head in range(2):
            qm[head, rows, :] = jnp.where(head_lanes(q.shape, 1, head), q, 0.0).astype(LOW)
            vt[head, :, rows] = jnp.where(head_lanes(v_t.shape, 0, head), v_t, 1.0).astype(LOW)

    def heads_of(tile):
        rows = tile_rows(tile)
        return Gather(
            o_o.at[rows],
            lambda t: os.at[t, rows],
            None,
            TILE,
            g_send,
            g_recv.at[pl.ds(4 * tile, 4)],
        )

    def pass_near(tile):
        gather = heads_of(tile)
        gather.pass_left()
        gather.pass_right()

    def weigh_pair(n, first):
        tile = jnp.where(n >= 6, 3, jnp.where(n >= 3, 2, jnp.where(n >= 1, 1, 0)))
        k_tile = n - tile * (tile + 1) // 2
        slot = lax.rem(n, 2)
        q_rows, k_rows = tile_rows(tile), tile_rows(k_tile)
        key = k_tile * TILE + lax.broadcasted_iota(jnp.int32, (TILE, 1), 0)
        query = tile * TILE + lax.broadcasted_iota(jnp.int32, (1, TILE), 1)
        key_code = jnp.where((key >= TOK // 2) & (key < cut), 1, 0)
        query_code = jnp.where(query >= cut, 1, 2)
        allowed = (key <= query) & (key_code < query_code)
        keep = pltpu.make_async_copy(
            act.at[pl.ds(pl.multiple_of(2 * TILE * slot, 2 * TILE), 2 * TILE)],
            p_out.at[4 * tile + k_tile],
            p_loc.at[slot],
        )

        @pl.when(n >= first + 2)
        def _():
            keep.wait()

        keys = qkv[k_rows, SPAN : 2 * SPAN]
        for head in range(2):
            s = jnp.where(allowed, dot_nt(keys, qm[head, q_rows, :]), -1e30)
            p = jnp.exp(s - lse[head : head + 1, q_rows])
            at = pl.multiple_of(2 * TILE * slot + TILE * head, TILE)
            act[pl.ds(at, TILE), :] = p.astype(LOW)
        keep.start()
        return first

    def weigh_pairs(first, stop):
        lax.fori_loop(first, stop, weigh_pair, first)
        for slot in range(2):
            rows = pl.ds(2 * TILE * slot, 2 * TILE)
            pltpu.make_async_copy(act.at[rows], p_out.at[slot], p_loc.at[slot]).wait()

    for tile in range(4):
        q_rows = tile_rows(tile)
        free = min(tile, 2)
        outs = []
        for head in range(2):

            def score(k_tile, peak, masked, tile=tile, q_rows=q_rows, head=head):
                rows = tile_rows(k_tile)
                s = dot_nt(qkv[rows, SPAN : 2 * SPAN], qm[head, q_rows, :])
                if masked:
                    s = masked_scores(s, cut, tile, k_tile)
                scores[rows, :] = s
                return jnp.maximum(peak, jnp.max(s, axis=0, keepdims=True))

            peak = jnp.full((1, TILE), -3e38, F32)
            for k_tile in range(tile + 1):
                peak = score(k_tile, peak, k_tile >= free)

            sums = jnp.zeros((SPAN, TILE), F32)
            for k_tile in range(tile + 1):
                rows = tile_rows(k_tile)
                e = jnp.exp(scores[rows, :] - peak).astype(LOW)
                sums = sums + dot(vt[head, :, rows], e)
            weight = sums[64:65] if head == 0 else sums[0:1]
            lse[head : head + 1, q_rows] = peak + jnp.log(weight)
            outs.append(sums[64 * head : 64 * (head + 1)] / weight)
        o_o[q_rows, :] = jnp.transpose(jnp.concatenate(outs, axis=0)).astype(LOW)
        pltpu.make_async_copy(o_o.at[q_rows], os.at[me, q_rows], o_loc).start()
        heads_of(tile).start()
        if tile == 1:
            weigh_pairs(0, 3)
        if tile >= 1:
            pass_near(tile - 1)
        if tile == 2:
            heads_of(0).pass_far()
        if tile == 1:
            arrived("y", 1)
            to_core = remote(half, half, wo_send, wo_recv, core=1 - core)
            to_core.start()
        if tile == 2:
            arrived("z", 3)
            along_y(3)
    write(o_o, o_out)
    pltpu.make_async_copy(xs, xall_o, x_loc.at[0]).wait()
    pltpu.make_async_copy(n2, n1_out, x_loc.at[1]).wait()
    pltpu.make_async_copy(o_o, os.at[me], o_loc).wait()
    tokens.sent()
    to_core.wait_recv()

    def middle_of(rows):
        left = jnp.concatenate([os[t, rows, :] for t in range(8)], axis=1)
        return xs[rows, :].astype(F32) + dot(left, wo[...].reshape(D, D)) + bo[...]

    def forward(b, _):
        rows = tile_rows(b)
        gather = heads_of(b)

        @pl.when(b == 0)
        def _():
            heads_of(1).pass_far()

        @pl.when(b == 1)
        def _():
            heads_of(2).pass_far()
            pass_near(3)
            cots.pass_left()
            cots.pass_right()

        @pl.when(b == 2)
        def _():
            heads_of(3).pass_far()

        @pl.when(b == 3)
        def _():
            cots.pass_far()

        gather.got_others(os.at[pl.ds(0, 4), rows])
        white, _inv = whitened(middle_of(rows))
        low = (white * gain[...] + shift[...]).astype(LOW)
        n2[rows, :] = low

        @pl.when(b == 0)
        def _():
            arrived("y", 2)

        v = dot(low, wf[...].reshape(D, HIDDEN)) + bf[...]
        square = v * v
        t = jnp.tanh(GELU_A * v * (1.0 + GELU_B * square))
        half = 0.5 * (1.0 + t)
        act[rows, :] = (v * half).astype(LOW)
        slope = 0.5 * GELU_A * (1.0 + 3.0 * GELU_B * square)
        da[rows, :] = (half + v * (1.0 - t * t) * slope).astype(LOW)
        return 0

    lax.fori_loop(0, 4, forward, 0)
    arrived("y", 3)
    cots.got_others(cs.at[pl.ds(0, 4)])
    reduce = Reduce(
        lambda t: part.at[t],
        lambda j: from_core.at[j],
        lambda j: total.at[j - 1],
        lambda j: from_side.at[j // 2],
        lambda j: land.at[j // 2],
        part.at[pl.ds(0, 7)],
        OWN,
        r_send,
        r_recv,
    )
    weights = wp[...].reshape(HIDDEN, D)
    bfc_o[...] = jnp.zeros_like(bfc_o)

    def backward(j):
        chip = lax.rem(x + j, 4)
        rows = tile_rows(chip)
        c_low = cs[pl.ds(2 * chip, 2)].reshape(TILE, D)
        low = (dot_nt(c_low, weights) * da[rows, :].astype(F32)).astype(LOW)
        da[rows, :] = low
        bfc_o[0:1, :] += jnp.sum(low.astype(F32), axis=0, keepdims=True)
        d_n2 = dot_nt(low, wf[...].reshape(D, HIDDEN))
        part[pl.ds(2 * chip, 2)] = d_n2.astype(LOW).reshape(2, OWN, D)

    order = (2, 1, 3, 0)

    def back_step(i, _):
        j = jnp.where(i == 0, 2, jnp.where(i == 1, 1, jnp.where(i == 2, 3, 0)))
        backward(j)
        for n, j in enumerate(order):

            @pl.when(i == n)
            def _(n=n, j=j):
                reduce.to_core(j)
                if n == 0:
                    reduce.to_far()
                if n == 2:
                    reduce.to_side_alone(1)
                if n == 3:
                    reduce.to_side_alone(3)
                    reduce.to_side_joined(1)
                    reduce.to_side_joined(3)

        return 0

    lax.fori_loop(0, 4, back_step, 0)
    own_rows = pl.ds(pl.multiple_of(me * OWN, OWN), OWN)
    middle = middle_of(own_rows)
    mid_o[...] = middle
    write(mid_o, mid_out)
    gproj_o[...] = dot_tn(act[...], cs[...].reshape(TOK, D)).astype(LOW)
    for k in range(1, 4):
        peer = ahead("y", k, 4)
        piece = gproj_o.at[pl.ds(pl.multiple_of(128 * peer, 128), 128)]
        remote(piece, yp.at[k], y_send.at[4], y_recv.at[4], y=peer).start()
    g_fc = dot_tn(n2[...], da[...]).astype(LOW)
    gfc_o[...] = g_fc[:, : HIDDEN // 2]
    for k in range(32):
        at = 128 * (k % 8) + 32 * (k // 8)
        n2[at : at + 32, : HIDDEN // 2] = g_fc[32 * k : 32 * k + 32, HIDDEN // 2 :]
    for k in range(1, 8):
        peer = ahead("z", k, 8)
        piece = n2.at[pl.ds(pl.multiple_of(128 * peer, 128), 128), pl.ds(0, HIDDEN // 2)]
        remote(piece, fz.at[k], z_send.at[4], z_recv.at[4], z=peer).start()
    sends.append((fz.at[pl.ds(0, 7)], z_send.at[4]))
    write(gfc_o, gfc_out)

    def output_part(b, _):
        rows = tile_rows(b)
        xs[rows, :] = dot(act[rows, :], weights).astype(LOW)
        return 0

    lax.fori_loop(0, 4, output_part, 0)
    for j in range(4):
        block = 2 * lax.rem(x + j, 4) + core
        write(xs.at[block_rows(block)], outp.at[j])
        other = 2 * lax.rem(x + j, 4) + 1 - core
        remote(xs.at[block_rows(other)], outp_o.at[j], ro_send, ro_recv, core=1 - core).start()
    white, inverse = whitened(mid_o[...])
    c_own = cs[me].astype(F32)
    d_n2 = reduce.result()
    d_m = c_own + norm_back(d_n2, gain[...], white, inverse)
    dm_o[...] = d_m
    low = d_m.astype(LOW)
    d_o = dot_nt(low, wo[...].reshape(D, D)).astype(LOW)
    for t in range(8):
        dob[t] = d_o[:, SPAN * t : SPAN * (t + 1)]
    spread(lambda t: dob.at[t], do_all, a_send, a_recv)
    write(qm, qm_out)
    for tile in range(4):
        rows = tile_rows(tile)
        k_t = jnp.transpose(qkv[rows, SPAN : 2 * SPAN].astype(F32))
        for head in range(2):
            vt[head, :, rows] = jnp.where(head_lanes(k_t.shape, 0, head), k_t, 0.0).astype(LOW)
    write(vt, ktm_out)
    write(dob.at[me], do_all.at[me])
    write(dm_o, dm_out)
    small_o[...] = jnp.zeros_like(small_o)
    small_o[0:1, :] = jnp.sum(low.astype(F32), axis=0, keepdims=True)
    small_o[1:2, :] = jnp.sum(d_n2 * white, axis=0, keepdims=True)
    small_o[2:3, :] = jnp.sum(d_n2, axis=0, keepdims=True)
    small_o[3:4, :] = jnp.sum(c_own, axis=0, keepdims=True)
    left = jnp.concatenate([os[t, own_rows, :] for t in range(8)], axis=1)
    g_out = dot_tn(left, low).astype(LOW)
    for t in range(2):
        gop_o[t] = g_out[:, HIDDEN * t : HIDDEN * (t + 1)]
    write(gop_o.at[core], gop_out)
    remote(gop_o.at[1 - core], gop_other, go_send, go_recv, core=1 - core).start()

    weigh_pairs(3, 10)
    all_here(fz.at[pl.ds(0, 7)], z_recv.at[4])
    f_sum = n2[pl.ds(pl.multiple_of(128 * z, 128), 128), : HIDDEN // 2].astype(F32)
    for k in range(1, 8):
        f_sum = f_sum + fz[k].astype(F32)
    fz_sum[...] = f_sum.astype(LOW)
    write(fz_sum, fz_out)
    all_here(yp.at[pl.ds(0, 3)], y_recv.at[4])
    p_sum = gproj_o[pl.ds(pl.multiple_of(128 * y, 128), 128), :].astype(F32)
    for k in range(1, 4):
        p_sum = p_sum + yp[k].astype(F32)
    p_mid[...] = p_sum.astype(LOW)
    write(p_mid, gproj_out)
    all_here(outp_o, ro_recv)
    all_sent(outp_o, ro_send)
    all_here(gop_other, go_recv)
    all_sent(gop_other, go_send)
    all_here(do_all.at[pl.ds(0, 7)], a_recv)
    all_sent(dob.at[pl.ds(0, 7)], a_send)
    for ref, sem in sends:
        all_sent(ref, sem)
    all_sent(yp.at[pl.ds(0, 3)], y_send.at[4])
    to_core.wait_send()
    for copy in written:
        copy.wait()
    cots.sent()
    all_sent(os.at[pl.ds(0, 7)], g_send)
    reduce.sent()


def middle(
    x, w_qkv, w_out, w_fc, w_proj, bias_q, bias_v, bias_f, gain1, shift1, segment, cot, bo, gain, shift
):
    outs = [
        (shaped((TOK, D), LOW), ANYWHERE),
        (shaped((TOK, D), LOW), ANYWHERE),
        (shaped((2, TOK, SPAN), LOW), ANYWHERE),
        (shaped((2, SPAN, TOK), LOW), ANYWHERE),
        (shaped((TOK, 3 * SPAN), LOW), ANYWHERE),
        (shaped((4, 8, 32, 3 * SPAN), LOW), ANYWHERE),
        (shaped((TOK, SPAN), LOW), ANYWHERE),
        (shaped((2, TOK), F32), IN_VMEM),
        (shaped((4, OWN, D), LOW), ANYWHERE),
        (shaped((OWN, D), F32), ANYWHERE),
        (shaped((OWN, D), F32), ANYWHERE),
        (shaped((8, OWN, SPAN), LOW), ANYWHERE),
        (shaped((D, HIDDEN // 2), LOW), ANYWHERE),
        (shaped((128, D), LOW), ANYWHERE),
        (shaped((D, HIDDEN), LOW), ANYWHERE),
        (shaped((8, D), F32), IN_VMEM),
        (shaped((8, HIDDEN), F32), IN_VMEM),
        (shaped((4, OWN, D), LOW), ANYWHERE),
        (shaped((D, HIDDEN), LOW), ANYWHERE),
        (shaped((16, 2 * TILE, TILE), LOW), ANYWHERE),
        (shaped((128, HIDDEN // 2), LOW), ANYWHERE),
        (shaped((8, 16, D), LOW), ANYWHERE),
        (shaped((8, 32, HIDDEN), LOW), ANYWHERE),
        (shaped((8, 16, D), LOW), ANYWHERE),
    ]
    scratch = [
        pltpu.VMEM((32, 4 * D), LOW),
        pltpu.VMEM((32, 3 * SPAN), LOW),
        pltpu.VMEM((16, D), LOW),
        pltpu.VMEM((32, HIDDEN), LOW),
        pltpu.VMEM((16, D), LOW),
        pltpu.VMEM((1, 3 * SPAN), F32),
        pltpu.VMEM((1, HIDDEN), F32),
        pltpu.VMEM((TOK, 3 * SPAN), LOW),
        pltpu.VMEM((4, 8, 32, 3 * SPAN), LOW),
        pltpu.VMEM((TOK, SPAN), LOW),
        pltpu.VMEM((OWN, D), F32),
        pltpu.VMEM((OWN, D), F32),
        pltpu.VMEM((D, HIDDEN // 2), LOW),
        pltpu.VMEM((HIDDEN, D), LOW),
        pltpu.VMEM((2, D, HIDDEN), LOW),
        pltpu.VMEM((2, TOK, SPAN), LOW),
        pltpu.VMEM((2, SPAN, TOK), LOW),
        pltpu.VMEM((TOK, TILE), F32),
        pltpu.VMEM((TOK, D), LOW),
        pltpu.VMEM((8, TOK, SPAN), LOW),
        pltpu.VMEM((8, OWN, D), LOW),
        pltpu.VMEM((4, 8, 2, 16, D), LOW),
        pltpu.VMEM((4, 8, 32, HIDDEN), LOW),
        pltpu.VMEM((4, 8, 16, D), LOW),
        pltpu.VMEM((TOK, D), LOW),
        pltpu.VMEM((TOK, HIDDEN), LOW),
        pltpu.VMEM((TOK, HIDDEN), LOW),
        pltpu.VMEM((8, OWN, D), LOW),
        pltpu.VMEM((4, OWN, D), LOW),
        pltpu.VMEM((3, OWN, D), LOW),
        pltpu.VMEM((2, OWN // 2, D), LOW),
        pltpu.VMEM((2, OWN, D), LOW),
        pltpu.VMEM((8, OWN, SPAN), LOW),
        pltpu.VMEM((4, 128, D), LOW),
        pltpu.VMEM((128, D), LOW),
        pltpu.VMEM((8, 128, HIDDEN // 2), LOW),
        pltpu.VMEM((128, HIDDEN // 2), LOW),
        DMA((6,)), DMA((9,)), DMA((2,)), DMA((16,)), DMA, DMA((7,)), DMA((5,)), DMA((5,)),
        DMA, DMA((16,)), DMA, DMA((4,)), DMA, DMA,
        DMA((5,)), DMA((5,)), DMA, DMA((8,)), DMA, DMA, DMA, DMA, DMA, DMA, DMA, DMA((2,)),
    ]
    ins = [ANYWHERE] * 5 + [IN_VMEM] * 6 + [ANYWHERE] + [IN_VMEM] * 3
    return call(middle_kernel, outs, ins, scratch, "middle", 2, vmem=60)(
        x, w_qkv, w_out, w_fc, w_proj, bias_q[None], bias_v[None], bias_f[None], gain1[None],
        shift1[None], segment, cot, bo[None], gain[None], shift[None],
    )[:21]


def ending_kernel(
    qkv_in, qm_in, ktm_in, do_in, o_in, outp_in, outp_o, x_all, n1_in, gop_in, gop_other, gfc_in, fz_in,
    p_mid_in, p_in, wq_in, mid_in, dm_in, gain, bp, small, bfc,
    out_o, dtok_o, fin_o, early_o, late_o,
    vals, do_ref, o_own, go, gfc, f2, p_mid, wq, mid, dm, n1, p_buf,
    qm, dom, ktm, delta, dqt, dk, dv, dqkv, outp, xs, part, g_acc, gq, rows1,
    so, sumo, eo, lo, g_side, f2y, sn, sumn, en, ln, yf, zf, zp, f_mid,
    gy, gz, g_mid, gv, gvz, gvy, v_mid, oy, oz, o_mid, fin,
    early_v, early_z, early_y, early_w, late_v, late_z, late_y, late_w, out_low, dtok,
    loc, p_loc, o_loc, ro_send, ro_recv, rn_send, rn_recv, y_send, y_recv, z_send, z_recv,
    f_send, f_recv, s_send, s_recv,
):
    x, core, y, z = axis("x"), axis("core"), axis("y"), axis("z")
    me = 2 * x + core
    ready = greet(seq_peers() + y_peers() + z_peers())

    def order(n):
        j = jnp.where(n == 0, 2, jnp.where(n == 1, 1, jnp.where(n == 2, 3, 0)))
        return lax.rem(x + j, 4)

    def load_pair(first, second, slot):
        number = 4 * jnp.maximum(first, second) + jnp.minimum(first, second)
        return pltpu.make_async_copy(p_in.at[number], p_buf.at[slot], p_loc.at[slot])

    loads = [
        (do_in, do_ref), (o_in, o_own), (qkv_in.at[:, pl.ds(2 * SPAN, SPAN)], vals), (qm_in, qm),
        (ktm_in, ktm), (gfc_in.at[pl.ds(pl.multiple_of(256 * y, 256), 256)], gfc), (fz_in, f2),
        (p_mid_in, p_mid), (outp_in, outp), (outp_o, so), (gop_in, go),
        (gop_other, g_side), (wq_in, wq), (n1_in, n1), (x_all, xs), (mid_in, mid),
        (dm_in, dm),
    ]
    loads = [pltpu.make_async_copy(a, b, loc.at[k]) for k, (a, b) in enumerate(loads)]
    for copy in loads[:10]:
        copy.start()
    load_pair(order(0), order(0), 0).start()
    load_pair(order(0), order(1), 1).start()
    for ref in (dqt, dk, dv, g_acc, rows1):
        ref[...] = jnp.zeros_like(ref)
    for copy in loads[:2]:
        copy.wait()

    def prepare(tile, _):
        rows = tile_rows(tile)
        d_o = do_ref[rows, :].astype(F32)
        prod_t = jnp.transpose(d_o * o_own[rows, :].astype(F32))
        for head in range(2):
            lanes = head_lanes(d_o.shape, 1, head)
            dom[head, rows, :] = jnp.where(lanes, d_o, 0.0).astype(LOW)
            delta[head : head + 1, rows] = jnp.sum(
                prod_t[64 * head : 64 * (head + 1)], axis=0, keepdims=True
            )
        return 0

    lax.fori_loop(0, 4, prepare, 0)
    for copy in loads[10:14]:
        copy.start()
    ready()
    for copy in loads[2:8]:
        copy.wait()
    r_out = Reduce(
        None, lambda j: so.at[j], lambda j: sumo.at[j - 1], lambda j: eo.at[j // 2],
        lambda j: lo.at[j // 2], outp_in.at[pl.ds(0, 3)], OWN, ro_send, ro_recv,
        mine=lambda j: outp.at[j], exchanged=True,
    )
    r_dn1 = Reduce(
        lambda t: part.at[t], lambda j: sn.at[j], lambda j: sumn.at[j - 1], lambda j: en.at[j // 2],
        lambda j: ln.at[j // 2], part.at[pl.ds(0, 7)], OWN, rn_send, rn_recv,
    )
    sends = []

    def pieces_to_z(src, land, n):
        rows = land.shape[1]
        for k in range(1, 8):
            peer = ahead("z", k, 8)
            piece = src.at[pl.ds(pl.multiple_of(rows * peer, rows), rows)]
            remote(piece, land.at[k], z_send.at[n], z_recv.at[n], z=peer).start()
        sends.append((land.at[pl.ds(0, 7)], z_send.at[n]))

    def rows_to_y(src, land, n):
        rows = land.shape[1]
        for k in range(1, 4):
            peer = ahead("y", k, 4)
            piece = src.at[pl.ds(pl.multiple_of(rows * peer, rows), rows)]
            remote(piece, land.at[k], y_send.at[n], y_recv.at[n], y=peer).start()
        sends.append((land.at[pl.ds(0, 3)], y_send.at[n]))

    def from_y(src, land, n):
        rows = land.shape[1]
        all_here(land.at[pl.ds(0, 3)], y_recv.at[n])
        return summed(src[pl.ds(pl.multiple_of(rows * y, rows), rows), :], land, 4)

    def from_z(src, land, n):
        rows = land.shape[1]
        all_here(land.at[pl.ds(0, 7)], z_recv.at[n])
        return summed(src[pl.ds(pl.multiple_of(rows * z, rows), rows), :], land, 8)

    rows_to_y(gfc_in, yf, 0)
    for copy in loads[8:10]:
        copy.wait()
    r_out.to_far()
    rows_to_y(f2, f2y, 6)
    pieces_to_z(p_mid, zp, 0)

    def vector_to_z(src, land, n):
        for k in range(1, 8):
            remote(src, land.at[z], z_send.at[n], z_recv.at[n], z=ahead("z", k, 8)).start()
        sends.append((land.at[pl.ds(0, 7)], z_send.at[n]))

    def vector_to_y(src, z_land, y_land, n):
        all_here(z_land.at[pl.ds(0, 7)], z_recv.at[n])
        z_land[z] = src[...]
        y_land[y] = summed(z_land[0], z_land, 8)
        for k in range(1, 4):
            peer = ahead("y", k, 4)
            remote(y_land.at[y], y_land.at[y], y_send.at[n], y_recv.at[n], y=peer).start()
        sends.append((y_land.at[pl.ds(0, 3)], y_send.at[n]))

    def vector_to_group(y_land, whole, out, n):
        all_here(y_land.at[pl.ds(0, 3)], y_recv.at[n])
        whole[...] = summed(y_land[0], y_land, 4)
        spread(lambda t: whole, out, s_send.at[n - 4], s_recv.at[n - 4])
        out[me] = whole[...]

    for k in range(8):
        lanes = slice(SPAN * k, SPAN * (k + 1))
        for n in range(4):
            early_v[8 * n + k : 8 * n + k + 1, :] = small[n : n + 1, lanes]
    early_v[32:40, :] = jnp.zeros((8, SPAN), F32)
    for k in range(4):
        early_v[32 + k : 33 + k, :] = bfc[0:1, SPAN * k : SPAN * (k + 1)]
    vector_to_z(early_v, early_z, 4)

    def pair(first, second, slot):
        q_tile, k_tile = jnp.maximum(first, second), jnp.minimum(first, second)
        q_rows, k_rows = tile_rows(q_tile), tile_rows(k_tile)
        for head in range(2):
            q_h, do_h = qm[head, q_rows, :], dom[head, q_rows, :]
            p = p_buf[slot, TILE * head : TILE * (head + 1), :]
            d_p = dot_nt(vals[k_rows, :], do_h)
            d_s = (p.astype(F32) * (d_p - delta[head : head + 1, q_rows])).astype(LOW)
            dv[k_rows, :] += dot(p, do_h)
            dk[k_rows, :] += dot(d_s, q_h)
            dqt[q_tile] += dot(ktm[head, :, k_rows], d_s)

    def complete(tile):
        rows = tile_rows(tile)
        low = jnp.concatenate(
            [jnp.transpose(dqt[tile]) * 0.125, dk[rows, :], dv[rows, :]], axis=1
        ).astype(LOW)
        dqkv[rows, :] = low
        d_n1 = dot_nt(low, wq[...].reshape(D, 3 * SPAN))
        part[pl.ds(2 * tile, 2)] = d_n1.astype(LOW).reshape(2, OWN, D)

    def account(tile):
        rows = tile_rows(tile)
        g_acc[...] += dot_tn(n1[rows, :], dqkv[rows, :])

    def add_sums(tile, _):
        rows = tile_rows(tile)
        white, _inv = whitened(xs[rows, :].astype(F32))
        d_n1 = part[pl.ds(2 * tile, 2)].reshape(TILE, D).astype(F32)
        rows1[0:1, :] += jnp.sum(d_n1 * white, axis=0, keepdims=True)
        rows1[1:2, :] += jnp.sum(d_n1, axis=0, keepdims=True)
        wide = dqkv[rows, :].astype(F32)
        rows1[2:3, :SPAN] += jnp.sum(wide[:, :SPAN], axis=0, keepdims=True)
        rows1[3:4, :SPAN] += jnp.sum(wide[:, 2 * SPAN :], axis=0, keepdims=True)
        return 0

    def summed(own, others, count):
        total = own.astype(F32)
        for k in range(1, count):
            total = total + others[k].astype(F32)
        return total

    for step, j in enumerate((2, 1, 3, 0)):
        tile = order(step)

        def one(r, _, tile=tile, step=step):
            slot = lax.rem((0, 4, 7, 9)[step] + r - step, 2)
            load_pair(tile, order(r), slot).wait()
            pair(tile, order(r), slot)
            if step < 2:
                over = r + 2 - 4
                first = jnp.where(over < 0, step, step + 1)
                second = jnp.where(over < 0, r + 2, step + 1 + over)
                load_pair(order(first), order(second), slot).start()
            if step == 2:

                @pl.when(r == 2)
                def _():
                    load_pair(order(3), order(3), slot).start()

            return 0

        if step == 0:
            lax.fori_loop(0, 2, one, 0)
            for copy in loads[10:12]:
                copy.wait()
            go[...] = (go[...].astype(F32) + g_side[...].astype(F32)).astype(LOW)
            rows_to_y(go, oy, 1)
            lax.fori_loop(2, 4, one, 0)
            for copy in loads[12:14]:
                copy.wait()
            for copy in loads[14:]:
                copy.start()
            r_out.to_side_alone(1)
            r_out.to_side_alone(3)
        else:
            lax.fori_loop(step, 4, one, 0)
        if step == 3:
            o_mid[...] = from_y(go, oy, 1).astype(LOW)
            pieces_to_z(o_mid, oz, 3)
        complete(tile)
        r_dn1.to_core(j)
        account(tile)
        if step == 0:
            r_dn1.to_far()
        if step == 1:
            r_out.to_side_joined(1)
            r_out.to_side_joined(3)
            r_dn1.to_side_alone(1)
            all_here(yf.at[pl.ds(0, 3)], y_recv.at[0])
            f_mid[...] = summed(gfc[...], yf, 4).astype(LOW)
            pieces_to_z(f_mid, zf, 1)
        if step == 2:
            r_dn1.to_side_alone(3)
            vector_to_y(early_v, early_z, early_y, 4)

    qk, v_at = slice(0, 2 * SPAN), slice(2 * SPAN, 3 * SPAN)
    gq[...] = g_acc[:, qk].astype(LOW)
    rows_to_y(gq, gy, 2)
    r_dn1.to_side_joined(1)
    r_dn1.to_side_joined(3)
    for copy in loads[14:]:
        copy.wait()
    lax.fori_loop(0, 4, add_sums, 0)
    for k in range(8):
        lanes = slice(SPAN * k, SPAN * (k + 1))
        for n in range(2):
            late_v[8 * n + k : 8 * n + k + 1, :] = rows1[n : n + 1, lanes]
    late_v[16:24, :] = rows1[0:8, :SPAN]
    vector_to_z(late_v, late_z, 5)
    for k in range(32):
        at = 128 * (k % 8) + 32 * (k // 8)
        gv[at : at + 32, :] = g_acc[32 * k : 32 * k + 32, v_at].astype(LOW)
    pieces_to_z(gv, gvz, 2)

    def in_halves(row, total):
        fin[row : row + 16, :HIDDEN] = total[:16].astype(LOW)
        fin[row : row + 16, HIDDEN:] = total[16:].astype(LOW)

    fin[0:16, :] = from_z(p_mid, zp, 0).astype(LOW)
    in_halves(16, jnp.concatenate([from_z(f_mid, zf, 1), from_y(f2, f2y, 6)], axis=1))
    early = pl.ds(0, 32)
    finals = Gather(
        fin.at[early],
        lambda t: fin_o.at[t, early],
        fin_o.at[pl.ds(0, 7), early],
        32,
        f_send.at[0],
        f_recv.at[pl.ds(0, 4)],
    )
    finals.start()
    written = []

    def write(src, dst):
        written.append(pltpu.make_async_copy(src, dst, o_loc.at[len(written)]))
        written[-1].start()

    write(fin.at[early], fin_o.at[me, early])
    vector_to_group(early_y, early_w, early_o, 4)
    vector_to_y(late_v, late_z, late_y, 5)
    g_mid[...] = from_y(gq, gy, 2).astype(LOW)
    pieces_to_z(g_mid, gz, 6)
    v_mid[...] = from_z(gv, gvz, 2).astype(LOW)
    rows_to_y(v_mid, gvy, 3)
    vector_to_group(late_y, late_w, late_o, 5)
    in_halves(32, from_z(o_mid, oz, 3))
    third = pl.ds(32, 16)
    spread(lambda t: fin.at[third], fin_o.at[:, third], f_send.at[2], f_recv.at[5])
    write(fin.at[third], fin_o.at[me, third])
    finals.pass_left()
    finals.pass_right()
    own_rows = pl.ds(pl.multiple_of(me * OWN, OWN), OWN)
    white, inverse = whitened(xs[own_rows, :].astype(F32))
    total = from_z(g_mid, gz, 6)
    fin[48:64, 0 : 2 * SPAN] = total[:16].astype(LOW)
    fin[48:64, HIDDEN : HIDDEN + 2 * SPAN] = total[16:].astype(LOW)
    total = from_y(v_mid, gvy, 3)
    fin[48:64, v_at] = total[:16].astype(LOW)
    fin[48:64, HIDDEN + 2 * SPAN : HIDDEN + 3 * SPAN] = total[16:].astype(LOW)
    fin[48:64, 3 * SPAN : HIDDEN] = jnp.zeros((16, SPAN), LOW)
    fin[48:64, HIDDEN + 3 * SPAN :] = jnp.zeros((16, SPAN), LOW)
    late = pl.ds(48, 16)
    spread(lambda t: fin.at[late], fin_o.at[:, late], f_send.at[1], f_recv.at[4])
    write(fin.at[late], fin_o.at[me, late])
    out_low[...] = (mid[...] + r_out.result() + bp[...]).astype(LOW)
    write(out_low, out_o)
    finals.pass_far()
    d_n1 = r_dn1.result()
    dtok[...] = dm[...] + norm_back(d_n1, gain[...], white, inverse)
    write(dtok, dtok_o)
    finals.got_others(fin_o.at[pl.ds(0, 4), early])
    all_here(early_o.at[pl.ds(0, 7)], s_recv.at[0])
    all_here(late_o.at[pl.ds(0, 7)], s_recv.at[1])
    all_here(fin_o.at[pl.ds(0, 7), third], f_recv.at[5])
    all_here(fin_o.at[pl.ds(0, 7), late], f_recv.at[4])
    finals.sent()
    all_sent(fin_o.at[pl.ds(0, 7), late], f_send.at[1])
    all_sent(fin_o.at[pl.ds(0, 7), third], f_send.at[2])
    all_sent(early_o.at[pl.ds(0, 7)], s_send.at[0])
    all_sent(late_o.at[pl.ds(0, 7)], s_send.at[1])
    for ref, sem in sends:
        all_sent(ref, sem)
    for copy in written:
        copy.wait()
    for reduce in (r_out, r_dn1):
        reduce.sent()


def reduce_scratch(rows, columns):
    return [
        pltpu.VMEM((4, rows, columns), LOW),
        pltpu.VMEM((3, rows, columns), LOW),
        pltpu.VMEM((2, rows // 2, columns), LOW),
        pltpu.VMEM((2, rows, columns), LOW),
    ]


def ending(
    qkv, qm, ktm, d_o, o_own, outp, outp_o, x_all, n1, gop, gop_other, gfc, fz, gproj, p, wq, mid, dm,
    gain, bp, small, bfc,
):
    outs = [
        (shaped((OWN, D), LOW), ANYWHERE),
        (shaped((OWN, D), F32), ANYWHERE),
        (shaped((8, 64, D), LOW), ANYWHERE),
        (shaped((8, 40, SPAN), F32), IN_VMEM),
        (shaped((8, 24, SPAN), F32), IN_VMEM),
    ]
    scratch = [
        pltpu.VMEM((TOK, SPAN), LOW),
        pltpu.VMEM((TOK, SPAN), LOW),
        pltpu.VMEM((TOK, SPAN), LOW),
        pltpu.VMEM((D, HIDDEN), LOW),
        pltpu.VMEM((256, HIDDEN // 2), LOW),
        pltpu.VMEM((128, HIDDEN // 2), LOW),
        pltpu.VMEM((128, D), LOW),
        pltpu.VMEM((4, 8, 32, 3 * SPAN), LOW),
        pltpu.VMEM((OWN, D), F32),
        pltpu.VMEM((OWN, D), F32),
        pltpu.VMEM((TOK, D), LOW),
        pltpu.VMEM((2, 2 * TILE, TILE), LOW),
        pltpu.VMEM((2, TOK, SPAN), LOW),
        pltpu.VMEM((2, TOK, SPAN), LOW),
        pltpu.VMEM((2, SPAN, TOK), LOW),
        pltpu.VMEM((2, TOK), F32),
        pltpu.VMEM((4, SPAN, TILE), F32),
        pltpu.VMEM((TOK, SPAN), F32),
        pltpu.VMEM((TOK, SPAN), F32),
        pltpu.VMEM((TOK, 3 * SPAN), LOW),
        pltpu.VMEM((4, OWN, D), LOW),
        pltpu.VMEM((TOK, D), LOW),
        pltpu.VMEM((8, OWN, D), LOW),
        pltpu.VMEM((D, 3 * SPAN), F32),
        pltpu.VMEM((D, 2 * SPAN), LOW),
        pltpu.VMEM((8, D), F32),
        *reduce_scratch(OWN, D),
        pltpu.VMEM((D, HIDDEN), LOW),
        pltpu.VMEM((4, 32, HIDDEN // 2), LOW),
        *reduce_scratch(OWN, D),
        pltpu.VMEM((4, 256, HIDDEN // 2), LOW),
        pltpu.VMEM((8, 32, HIDDEN // 2), LOW), pltpu.VMEM((8, 16, D), LOW),
        pltpu.VMEM((256, HIDDEN // 2), LOW),
        pltpu.VMEM((4, 256, 2 * SPAN), LOW),
        pltpu.VMEM((8, 32, 2 * SPAN), LOW),
        pltpu.VMEM((256, 2 * SPAN), LOW),
        pltpu.VMEM((D, SPAN), LOW),
        pltpu.VMEM((8, 128, SPAN), LOW),
        pltpu.VMEM((4, 32, SPAN), LOW),
        pltpu.VMEM((128, SPAN), LOW),
        pltpu.VMEM((4, 256, HIDDEN), LOW),
        pltpu.VMEM((8, 32, HIDDEN), LOW),
        pltpu.VMEM((256, HIDDEN), LOW),
        pltpu.VMEM((64, D), LOW),
        *[
            pltpu.VMEM((*lead, rows, SPAN), F32)
            for rows in (40, 24)
            for lead in ((), (8,), (4,), ())
        ],
        pltpu.VMEM((OWN, D), LOW),
        pltpu.VMEM((OWN, D), F32),
        DMA((17,)), DMA((2,)), DMA((5,)), DMA, DMA((8,)), DMA, DMA((8,)),
        DMA((7,)), DMA((7,)), DMA((7,)), DMA((7,)), DMA((3,)), DMA((6,)), DMA((2,)), DMA((2,)),
    ]
    ins = [ANYWHERE] * 18 + [IN_VMEM] * 4
    return call(ending_kernel, outs, ins, scratch, "ending", 4, vmem=60)(
        qkv, qm, ktm, d_o.reshape(TOK, SPAN), o_own, outp, outp_o, x_all, n1, gop, gop_other, gfc, fz,
        gproj, p, wq, mid, dm, gain[None], bp[None], small, bfc,
    )


def results_kernel(
    fin, early, late, out, dtok, out_o, dtok_o, gq_out, go_out, gf_out, gp_out, *rest
):
    vectors, bf_o, out_s, dtok_s, gq_o, go_o, gf_o, gp_o, loc = rest[:8], *rest[8:]
    inward = [
        pltpu.make_async_copy(out, out_s, loc.at[0]),
        pltpu.make_async_copy(dtok, dtok_s, loc.at[1]),
    ]
    outward = [
        pltpu.make_async_copy(out_s, out_o, loc.at[2]),
        pltpu.make_async_copy(dtok_s, dtok_o, loc.at[3]),
    ]
    for copy in inward:
        copy.start()
    lane = lax.broadcasted_iota(jnp.int32, (40, 128), 1) // 16
    units = []
    for t in range(8):
        gp_o[16 * t : 16 * (t + 1), :] = fin[t, 0:16, :].astype(F32)
        span = slice(SPAN * t, SPAN * (t + 1))
        for half in range(2):
            rows = slice(16 * half, 16 * (half + 1))
            at = HIDDEN * half
            for k in range(3):
                gq_o[rows, D * k + SPAN * t : D * k + SPAN * (t + 1)] = fin[
                    t, 48:64, at + SPAN * k : at + SPAN * (k + 1)
                ].astype(F32)
        bias = jnp.concatenate([early[t, 32 + k : 33 + k, :] for k in range(4)], axis=1)
        units.append(
            jnp.concatenate(
                [
                    fin[t, 16:32, :HIDDEN].astype(F32),
                    fin[t, 16:32, HIDDEN:].astype(F32),
                    jnp.broadcast_to(bias, (8, HIDDEN)),
                ],
                axis=0,
            )
        )
        for k in range(2):
            vectors[6 + k][:, span] = late[t, 18 + k : 19 + k, :]
    early_sum, late_sum = early[0], late[0]
    for t in range(1, 8):
        early_sum, late_sum = early_sum + early[t], late_sum + late[t]
    for k in range(8):
        span = slice(SPAN * k, SPAN * (k + 1))
        for n in range(2):
            vectors[n][:, span] = late_sum[8 * n + k : 8 * n + k + 1, :]
        for n in range(4):
            vectors[2 + n][:, span] = early_sum[8 * n + k : 8 * n + k + 1, :]
    for core in range(2):
        for half in range(2):
            at = slice(HIDDEN * half, HIDDEN * (half + 1))
            total = fin[core, 32:48, at].astype(F32)
            for chip in range(1, 4):
                total = total + fin[2 * chip + core, 32:48, at].astype(F32)
            go_o[16 * half : 16 * (half + 1), HIDDEN * core : HIDDEN * (core + 1)] = total
    for into, out_of in zip(inward, outward):
        into.wait()
        out_of.start()
    for src, dst in ((gq_o, gq_out), (go_o, go_out), (gp_o, gp_out)):
        outward.append(pltpu.make_async_copy(src, dst, loc.at[2 + len(outward)]))
        outward[-1].start()
    for s in range(32):
        q, p = s // 8, s % 8
        tile = jnp.zeros((40, 128), F32)
        for t in range(8):
            turned = pltpu.roll(units[t][:, 128 * q : 128 * (q + 1)], (16 * t - 16 * p) % 128, 1)
            tile = jnp.where(lane == t, turned, tile)
        gf_o[:, 128 * s : 128 * (s + 1)] = tile[:32]
        bf_o[:, 128 * s : 128 * (s + 1)] = tile[32:33]
        if s % 8 == 7:
            part = slice(D * (s // 8), D * (s // 8 + 1))
            outward.append(
                pltpu.make_async_copy(
                    gf_o.at[:, part], gf_out.at[:, part], loc.at[2 + len(outward)]
                )
            )
            outward[-1].start()
    for copy in outward:
        copy.wait()


def results(fin, early, late, out, dtok):
    outs = [
        (shaped((OWN, D), LOW), ANYWHERE),
        (shaped((OWN, D), F32), ANYWHERE),
        (shaped((32, 3 * D), F32), ANYWHERE),
        (shaped((32, D), F32), ANYWHERE),
        (shaped((32, 4 * D), F32), ANYWHERE),
        (shaped((128, D), F32), ANYWHERE),
    ]
    narrow = (shaped((1, D), F32), IN_VMEM)
    outs += [narrow] * 8 + [(shaped((1, 4 * D), F32), IN_VMEM)]
    ins = [IN_VMEM, IN_VMEM, IN_VMEM, ANYWHERE, ANYWHERE]
    scratch = [
        pltpu.VMEM((OWN, D), LOW),
        pltpu.VMEM((OWN, D), F32),
        pltpu.VMEM((32, 3 * D), F32),
        pltpu.VMEM((32, D), F32),
        pltpu.VMEM((32, 4 * D), F32),
        pltpu.VMEM((128, D), F32),
        DMA((11,)),
    ]
    return call(results_kernel, outs, ins, scratch, "results")(fin, early, late, out, dtok)


def per_device(
    tokens, segment, ln1_gain, ln1_shift, w_qkv, bias_query, bias_value, w_out, bias_out,
    ln2_gain, ln2_shift, w_fc, bias_fc, w_proj, bias_proj, cotangent,
):
    (
        x_all, n1, qm, ktm, qkv, wq, o_own, _, outp, mid, dm, do_all, gfc, gproj, gop, small, bfc,
        outp_o, gop_other, p, fz,
    ) = middle(
        tokens[0], w_qkv, w_out, w_fc, w_proj, bias_query, bias_value, bias_fc, ln1_gain, ln1_shift,
        segment, cotangent[0], bias_out, ln2_gain, ln2_shift,
    )
    out, dtok, fin, early, late = ending(
        qkv, qm, ktm, do_all, o_own, outp, outp_o, x_all, n1, gop, gop_other, gfc, fz, gproj, p, wq,
        mid, dm, ln1_gain, bias_proj, small, bfc,
    )
    out, dtok, gq, go, gf, gp, *vectors = results(fin, early, late, out, dtok)
    v = [vector[0] for vector in vectors]
    return (
        out[None], dtok[None], v[0], v[1], gq, v[6], v[7], go, v[2], v[3], v[4], gf, v[8], gp, v[5],
    )


def solution(mesh):
    finer = Mesh(mesh.devices.reshape(4, 2, 4, 8), ("x", "core", "y", "z"))
    rows, whole = P(SHARD, None), P()
    tokens = P(SHARD, SEQ, None)
    return jax.shard_map(
        per_device,
        mesh=finer,
        in_specs=(
            tokens, rows, whole, whole, rows, whole, whole, rows, whole, whole, whole, rows,
            whole, rows, whole, tokens,
        ),
        out_specs=(
            tokens, tokens, whole, whole, rows, whole, whole, rows, whole, whole, whole, rows,
            whole, rows, whole,
        ),
        check_vma=False,
    )
```

```python
import functools

import jax
import jax.numpy as jnp
from jax import lax
from jax.experimental import pallas as pl
from jax.experimental.pallas import tpu as pltpu
from jax.sharding import Mesh
from jax.sharding import PartitionSpec as P

SEQ = ("x", "core")
SHARD = ("y", "z")
F32 = jnp.float32
LOW = jnp.bfloat16
MIB = 2**20
TOK = 2048
OWN = 256
TILE = 512
D = 1024
HIDDEN = 512
SPAN = 128
GELU_A = 0.7978845608028654
GELU_B = 0.044715

IN_VMEM = pl.BlockSpec(memory_space=pltpu.VMEM)
IN_SMEM = pl.BlockSpec(memory_space=pltpu.SMEM)
ANYWHERE = pl.BlockSpec(memory_space=pl.ANY)
DMA = pltpu.SemaphoreType.DMA


def shaped(shape, dtype):
    return jax.ShapeDtypeStruct(shape, dtype)


def remote(src, dst, send, recv, **device):
    return pltpu.make_async_remote_copy(
        src_ref=src,
        dst_ref=dst,
        send_sem=send,
        recv_sem=recv,
        device_id=device,
        device_id_type=pl.DeviceIdType.MESH,
    )


def axis(name):
    return lax.axis_index(name)


def ahead(name, k, count):
    return lax.rem(axis(name) + k, count)


def seq_peers():
    core = axis("core")
    return [
        {"x": ahead("x", j, 4), "core": lax.rem(core + i, 2)}
        for j in range(4)
        for i in range(2)
        if (j, i) != (0, 0)
    ]


def near_peers():
    return [{"x": ahead("x", 1, 4)}, {"x": ahead("x", 3, 4)}, {"core": 1 - axis("core")}]


def y_peers():
    return [{"y": ahead("y", k, 4)} for k in range(1, 4)]


def z_peers():
    return [{"z": ahead("z", k, 8)} for k in range(1, 8)]


def greet(peers):
    sem = pltpu.get_barrier_semaphore()
    for peer in peers:
        pl.semaphore_signal(sem, inc=1, device_id=peer, device_id_type=pl.DeviceIdType.MESH)
    return lambda: pl.semaphore_wait(sem, len(peers))


def dot(a, b):
    return jnp.dot(a, b, preferred_element_type=F32)


def dot_nt(a, b):
    return lax.dot_general(a, b, (((1,), (1,)), ((), ())), preferred_element_type=F32)


def dot_tn(a, b):
    return lax.dot_general(a, b, (((0,), (0,)), ((), ())), preferred_element_type=F32)


def whitened(values):
    mean = jnp.mean(values, axis=-1, keepdims=True)
    centered = values - mean
    spread = jnp.mean(centered * centered, axis=-1, keepdims=True)
    inverse = lax.rsqrt(spread + 1e-05)
    return centered * inverse, inverse


def norm_back(grad, gain, white, inverse):
    d_white = grad * gain
    first = jnp.mean(d_white, axis=-1, keepdims=True)
    second = jnp.mean(d_white * white, axis=-1, keepdims=True)
    return inverse * (d_white - first - white * second)


class Gather:
    def __init__(self, src, at, seven, rows, send, recv, cut=None):
        x, core = axis("x"), axis("core")
        other = 1 - core
        right, far, left = (lax.rem(x + k, 4) for k in (1, 2, 3))
        cut = cut or rows // 2
        low, high = pl.ds(0, cut), pl.ds(cut, rows - cut)
        mine, r, f, l = (at(2 * k + core) for k in (x, right, far, left))
        self.seven = seven
        self.send, self.recv = send, recv
        self.single = recv.shape[0] == 4
        slots = (0, 1, 3, 2, 2) + ((3, 3, 3) if self.single else (4, 5, 6))
        self.plan = [
            (src, mine, {"x": right}),
            (src, mine, {"x": left}),
            (src, mine, {"core": other}),
            (l.at[low], l.at[low], {"x": right}),
            (r.at[high], r.at[high], {"x": left}),
            (l, l, {"core": other}),
            (r, r, {"core": other}),
            (f, f, {"core": other}),
        ]
        self.slots = slots
        self.block = mine
        self.blocks = dict(
            mine=2 * x + core,
            mine_o=2 * x + other,
            left=2 * left + core,
            left_o=2 * left + other,
            right=2 * right + core,
            right_o=2 * right + other,
            far=2 * far + core,
            far_o=2 * far + other,
        )

    def copy(self, k):
        src, dst, device = self.plan[k]
        return remote(src, dst, self.send, self.recv.at[self.slots[k]], **device)

    def start(self):
        for k in (0, 1, 2):
            self.copy(k).start()

    def got(self, slot):
        remote(self.block, self.block, self.send, self.recv.at[slot], core=0).wait_recv()

    def got_others(self, four):
        remote(four, four, self.send, self.recv.at[3], core=0).wait_recv()

    def pass_left(self):
        self.got(0)
        self.copy(3).start()
        self.copy(5).start()

    def pass_right(self):
        self.got(1)
        self.copy(4).start()
        self.copy(6).start()

    def pass_far(self):
        self.got(2)
        self.copy(7).start()

    def sent(self):
        remote(self.seven, self.seven, self.send, self.recv.at[0], core=0).wait_send()


def all_sent(ref, send):
    remote(ref, ref, send, send, core=0).wait_send()


def all_here(ref, recv):
    remote(ref, ref, recv, recv, core=0).wait_recv()


class Reduce:
    def __init__(self, part, from_core, total, from_side, land, seven, rows, send, recv, mine=None, exchanged=False):
        self.seven = seven
        self.exchanged = exchanged
        self.mine = mine or (lambda j: part(2 * self.chip(j) + self.core))
        self.part, self.from_core, self.total = part, from_core, total
        self.from_side, self.land = from_side, land
        self.send, self.recv = send, recv
        self.x, self.core = axis("x"), axis("core")
        self.half = rows // 2

    def chip(self, j):
        return lax.rem(self.x + j, 4)

    def core_copy(self, j):
        return remote(
            self.part(2 * self.chip(j) + 1 - self.core),
            self.from_core(j),
            self.send,
            self.recv.at[j],
            core=1 - self.core,
        )

    def side_copy(self, j):
        rows = pl.ds(0 if j == 1 else self.half, self.half)
        n = 4 + j // 2
        return remote(
            self.total(2).at[rows],
            self.from_side(j),
            self.send,
            self.recv.at[n],
            x=self.chip(j),
        )

    def chip_copy(self, j, rows):
        n = 6 + j // 2
        return remote(
            self.total(j).at[rows],
            self.land(j).at[rows],
            self.send,
            self.recv.at[n],
            x=self.chip(j),
        )

    def pair(self, j, rows):
        return self.mine(j)[rows, :].astype(F32) + self.from_core(j)[rows, :].astype(F32)

    def to_core(self, j):
        self.core_copy(j).start()

    def core_here(self, j):
        if not self.exchanged:
            self.core_copy(j).wait_recv()

    def to_far(self):
        self.core_here(2)
        self.total(2)[...] = self.pair(2, slice(None)).astype(LOW)
        self.side_copy(1).start()
        self.side_copy(3).start()

    def halves(self, j):
        low, high = pl.ds(0, self.half), pl.ds(self.half, self.half)
        return (low, high) if j == 1 else (high, low)

    def to_side_alone(self, j):
        self.core_here(j)
        rows = self.halves(j)[1]
        self.total(j)[rows, :] = self.pair(j, rows).astype(LOW)
        self.chip_copy(j, rows).start()

    def to_side_joined(self, j):
        self.side_copy(j).wait_recv()
        rows = self.halves(j)[0]
        more = self.from_side(j)[...].astype(F32)
        self.total(j)[rows, :] = (self.pair(j, rows) + more).astype(LOW)
        self.chip_copy(j, rows).start()

    def result(self):
        self.core_here(0)
        total = self.pair(0, slice(None))
        for j in (1, 3):
            self.chip_copy(j, pl.ds(0, 2 * self.half)).wait_recv()
            total = total + self.land(j)[...].astype(F32)
        return total

    def sent(self):
        all_sent(self.seven, self.send)


def call(kernel, outs, ins, scratch, name, number=None, vmem=56):
    extra = {} if number is None else dict(collective_id=number, has_side_effects=True)
    return pl.pallas_call(
        kernel,
        out_shape=[shape for shape, _ in outs],
        in_specs=ins,
        out_specs=[spec for _, spec in outs],
        scratch_shapes=scratch,
        name=name,
        compiler_params=pltpu.CompilerParams(vmem_limit_bytes=vmem * MIB, **extra),
    )


def chosen_units(values, seq):
    lane = lax.broadcasted_iota(jnp.int32, (values.shape[0], 128), 1)
    tiles = []
    for q in range(4):
        tile = jnp.zeros((values.shape[0], 128), F32)
        for p in range(8):
            at = 128 * (8 * q + p)
            shift = lax.rem(16 * p - 16 * seq + 128, 128)
            turned = pltpu.roll(values[:, at : at + 128], shift, 1)
            tile = jnp.where((lane // 16) == p, turned, tile)
        tiles.append(tile)
    return jnp.concatenate(tiles, axis=1)


def segment_cut(segment):
    return jnp.sum(jnp.where(segment[...] < 2, 1, 0))


def head_lanes(shape, dim, head):
    return (lax.broadcasted_iota(jnp.int32, shape, dim) // 64) == head


def masked_scores(scores, cut, q_tile, k_tile):
    shape = scores.shape
    key = k_tile * TILE + lax.broadcasted_iota(jnp.int32, shape, 0)
    query = q_tile * TILE + lax.broadcasted_iota(jnp.int32, shape, 1)
    allowed = key <= query
    if q_tile >= 2:
        allowed = allowed & ((key >= cut) | (query < cut))
    return jnp.where(allowed, scores, -1e30)


def tile_rows(tile):
    if isinstance(tile, int):
        return pl.ds(tile * TILE, TILE)
    return pl.ds(pl.multiple_of(tile * TILE, TILE), TILE)


def spread(src, dst, send, recv):
    x, core = axis("x"), axis("core")
    me = 2 * x + core
    for j in (2, 1, 3, 0):
        for i in range(2):
            if (j, i) != (0, 0):
                to_x, to_c = lax.rem(x + j, 4), lax.rem(core + i, 2)
                remote(src(2 * to_x + to_c), dst.at[me], send, recv, x=to_x, core=to_c).start()


def middle_kernel(
    x_own, w_qkv, w_out, w_fc, w_proj, bias_q, bias_v, bias_f, gain1, shift1, segment, cot, bo, gain,
    shift,
    xall_o, n1_out, qm_out, ktm_out, qkv_out, wq_out, o_out, lse, outp, mid_out, dm_out, do_all, gfc_out, gproj_out, gop_out,
    small_o, bfc_o, outp_o, gop_other, p_out, fz_out, woz, wfz, wpz,
    w_fc_s, wq, wo_in, wf_in, wp_in, bias, bf, qkv, wq_o, o_o, mid_o, dm_o, gfc_o, gproj_o, gop_o, qm, vt, scores, xs, os, cs, wo, wf, wp, n2, da, act, part, from_core, total, from_side, land, dob,
    yp, p_mid, fz, fz_sum, in_loc, loc, x_loc, out_loc, x_send, x_recv, z_send, z_recv, g_send, g_recv, c_send, c_recv, wo_send, wo_recv,
    y_send, y_recv, r_send, r_recv, a_send, a_recv, o_loc, ro_send, ro_recv, go_send, go_recv, p_loc,
):
    x, core, y, z = axis("x"), axis("core"), axis("y"), axis("z")
    me = 2 * x + core
    ready = greet(seq_peers() + y_peers() + z_peers())
    span = pl.ds(pl.multiple_of(SPAN * me, SPAN), SPAN)
    inputs = [(w_fc, w_fc_s)]
    for k in range(3):
        at = pl.ds(pl.multiple_of(k * D + SPAN * me, SPAN), SPAN)
        inputs.append((w_qkv.at[:, at], wq.at[:, k * SPAN : (k + 1) * SPAN]))
    inputs.append((w_out.at[pl.ds(pl.multiple_of(16 * core, 16), 16)], wo_in))
    inputs.append((w_proj.at[pl.ds(pl.multiple_of(16 * me, 16), 16)], wp_in))
    inputs = [pltpu.make_async_copy(a, b, in_loc.at[k]) for k, (a, b) in enumerate(inputs)]
    for copy in inputs:
        copy.start()
    bias[:, :SPAN] = bias_q[:, span]
    bias[:, SPAN : 2 * SPAN] = jnp.zeros((1, SPAN), F32)
    bias[:, 2 * SPAN :] = bias_v[:, span]
    bf[...] = chosen_units(jnp.broadcast_to(bias_f[...], (8, 4 * D)), me)[0:1]
    for copy in inputs:
        copy.wait()
    wf_in[...] = chosen_units(w_fc_s[...].astype(F32), me).astype(LOW)
    cut = segment_cut(segment)
    written = []

    def write(src, dst):
        n = len(written)
        written.append(pltpu.make_async_copy(src, dst, out_loc.at[n]))
        written[-1].start()

    tokens = Gather(
        x_own, lambda t: xs.at[pl.ds(t * OWN, OWN)], xs.at[pl.ds(0, 7 * OWN)], OWN, x_send, x_recv
    )
    cots = Gather(cot, lambda t: cs.at[t], cs.at[pl.ds(0, 7)], OWN, c_send, c_recv)
    blocks = tokens.blocks
    half = wo.at[:, :, core]
    own_z = [(wq, wq_o.at[y, z]), (wo_in, woz.at[z]), (wf_in, wfz.at[z]), (wp_in, wpz.at[z])]
    whole_z = [wq_o.at[y], woz, wfz, wpz]
    local = own_z + [(x_own, xs.at[pl.ds(pl.multiple_of(OWN * me, OWN), OWN)]), (cot, cs.at[me])]
    local = [pltpu.make_async_copy(a, b, loc.at[k]) for k, (a, b) in enumerate(local)]
    for copy in local:
        copy.start()
    sends, own_y = [], {}

    def along_z(n):
        own, dst = own_z[n]
        for k in range(1, 8):
            remote(own, dst, z_send.at[n], z_recv.at[n], z=ahead("z", k, 8)).start()
        sends.append((whole_z[n].at[pl.ds(0, 7)], z_send.at[n]))

    def along_y(n):
        src, to = [(wq_o.at[y], wq_o), (woz, half), (wfz, wf), (wpz, wp)][n]
        for k in range(1, 4):
            remote(src, to.at[y], y_send.at[n], y_recv.at[n], y=ahead("y", k, 4)).start()
        sends.append((to.at[pl.ds(0, 3)], y_send.at[n]))
        if n:
            own_y[n] = pltpu.make_async_copy(src, to.at[y], loc.at[5 + n])
            own_y[n].start()

    def arrived(along, n):
        if along == "z":
            all_here(whole_z[n].at[pl.ds(0, 7)], z_recv.at[n])
        else:
            all_here((wq_o, half, wf, wp)[n].at[pl.ds(0, 3)], y_recv.at[n])
            if n:
                own_y[n].wait()

    ready()
    along_z(0)
    tokens.start()
    for copy in local:
        copy.wait()
    local = []

    def block_rows(block):
        return pl.ds(pl.multiple_of(OWN * block, OWN), OWN)

    def put(name):
        base = OWN * blocks[name]

        def one(i, _):
            rows = pl.ds(pl.multiple_of(base + i * 128, 128), 128)
            white, _inv = whitened(xs[rows, :].astype(F32))
            n2[rows, :] = (white * gain1[...] + shift1[...]).astype(LOW)
            return 0

        lax.fori_loop(0, OWN // 128, one, 0)
        rows = block_rows(blocks[name])
        pltpu.make_async_copy(xs.at[rows], xall_o.at[rows], x_loc.at[0]).start()
        pltpu.make_async_copy(n2.at[rows], n1_out.at[rows], x_loc.at[1]).start()

    def project(name):
        rows = block_rows(blocks[name])
        weights = wq_o[...].reshape(D, 3 * SPAN)
        qkv[rows, :] = (dot(n2[rows, :], weights) + bias[...]).astype(LOW)

    put("mine")
    arrived("z", 0)
    along_y(0)
    along_z(1)
    tokens.got(3)
    put("mine_o")
    arrived("z", 1)
    along_z(2)
    tokens.pass_left()
    tokens.pass_right()
    put("left")
    put("right")
    tokens.got(4)
    put("left_o")
    tokens.got(5)
    put("right_o")
    arrived("y", 0)
    along_y(1)
    write(wq_o, wq_out)
    for name in ("mine", "mine_o", "left", "right"):
        project(name)
    tokens.pass_far()
    cots.start()
    put("far")
    for name in ("left_o", "right_o", "far"):
        project(name)
    tokens.got(6)
    put("far_o")
    project("far_o")
    write(qkv, qkv_out)
    arrived("z", 2)
    along_z(3)
    along_y(2)
    for tile in range(4):
        rows = tile_rows(tile)
        q = qkv[rows, :SPAN].astype(F32) * 0.125
        v_t = jnp.transpose(qkv[rows, 2 * SPAN :].astype(F32))
        for head in range(2):
            qm[head, rows, :] = jnp.where(head_lanes(q.shape, 1, head), q, 0.0).astype(LOW)
            vt[head, :, rows] = jnp.where(head_lanes(v_t.shape, 0, head), v_t, 1.0).astype(LOW)

    def heads_of(tile):
        rows = tile_rows(tile)
        return Gather(
            o_o.at[rows],
            lambda t: os.at[t, rows],
            None,
            TILE,
            g_send,
            g_recv.at[pl.ds(4 * tile, 4)],
        )

    def pass_near(tile):
        gather = heads_of(tile)
        gather.pass_left()
        gather.pass_right()

    def weigh_pair(n, first):
        tile = jnp.where(n >= 6, 3, jnp.where(n >= 3, 2, jnp.where(n >= 1, 1, 0)))
        k_tile = n - tile * (tile + 1) // 2
        slot = lax.rem(n, 2)
        q_rows, k_rows = tile_rows(tile), tile_rows(k_tile)
        key = k_tile * TILE + lax.broadcasted_iota(jnp.int32, (TILE, 1), 0)
        query = tile * TILE + lax.broadcasted_iota(jnp.int32, (1, TILE), 1)
        key_code = jnp.where((key >= TOK // 2) & (key < cut), 1, 0)
        query_code = jnp.where(query >= cut, 1, 2)
        allowed = (key <= query) & (key_code < query_code)
        keep = pltpu.make_async_copy(
            act.at[pl.ds(pl.multiple_of(2 * TILE * slot, 2 * TILE), 2 * TILE)],
            p_out.at[4 * tile + k_tile],
            p_loc.at[slot],
        )

        @pl.when(n >= first + 2)
        def _():
            keep.wait()

        keys = qkv[k_rows, SPAN : 2 * SPAN]
        for head in range(2):
            s = jnp.where(allowed, dot_nt(keys, qm[head, q_rows, :]), -1e30)
            p = jnp.exp(s - lse[head : head + 1, q_rows])
            at = pl.multiple_of(2 * TILE * slot + TILE * head, TILE)
            act[pl.ds(at, TILE), :] = p.astype(LOW)
        keep.start()
        return first

    def weigh_pairs(first, stop):
        lax.fori_loop(first, stop, weigh_pair, first)
        for slot in range(2):
            rows = pl.ds(2 * TILE * slot, 2 * TILE)
            pltpu.make_async_copy(act.at[rows], p_out.at[slot], p_loc.at[slot]).wait()

    for tile in range(4):
        q_rows = tile_rows(tile)
        free = min(tile, 2)
        outs = []
        for head in range(2):

            def score(k_tile, peak, masked, tile=tile, q_rows=q_rows, head=head):
                rows = tile_rows(k_tile)
                s = dot_nt(qkv[rows, SPAN : 2 * SPAN], qm[head, q_rows, :])
                if masked:
                    s = masked_scores(s, cut, tile, k_tile)
                scores[rows, :] = s
                return jnp.maximum(peak, jnp.max(s, axis=0, keepdims=True))

            peak = jnp.full((1, TILE), -3e38, F32)
            for k_tile in range(tile + 1):
                peak = score(k_tile, peak, k_tile >= free)

            sums = jnp.zeros((SPAN, TILE), F32)
            for k_tile in range(tile + 1):
                rows = tile_rows(k_tile)
                e = jnp.exp(scores[rows, :] - peak).astype(LOW)
                sums = sums + dot(vt[head, :, rows], e)
            weight = sums[64:65] if head == 0 else sums[0:1]
            lse[head : head + 1, q_rows] = peak + jnp.log(weight)
            outs.append(sums[64 * head : 64 * (head + 1)] / weight)
        o_o[q_rows, :] = jnp.transpose(jnp.concatenate(outs, axis=0)).astype(LOW)
        pltpu.make_async_copy(o_o.at[q_rows], os.at[me, q_rows], o_loc).start()
        heads_of(tile).start()
        if tile == 1:
            weigh_pairs(0, 3)
        if tile >= 1:
            pass_near(tile - 1)
        if tile == 2:
            heads_of(0).pass_far()
        if tile == 1:
            arrived("y", 1)
            to_core = remote(half, half, wo_send, wo_recv, core=1 - core)
            to_core.start()
        if tile == 2:
            arrived("z", 3)
            along_y(3)
    write(o_o, o_out)
    pltpu.make_async_copy(xs, xall_o, x_loc.at[0]).wait()
    pltpu.make_async_copy(n2, n1_out, x_loc.at[1]).wait()
    pltpu.make_async_copy(o_o, os.at[me], o_loc).wait()
    tokens.sent()
    to_core.wait_recv()

    def middle_of(rows):
        left = jnp.concatenate([os[t, rows, :] for t in range(8)], axis=1)
        return xs[rows, :].astype(F32) + dot(left, wo[...].reshape(D, D)) + bo[...]

    def forward(b, _):
        rows = tile_rows(b)
        gather = heads_of(b)

        @pl.when(b == 0)
        def _():
            heads_of(1).pass_far()

        @pl.when(b == 1)
        def _():
            heads_of(2).pass_far()
            pass_near(3)
            cots.pass_left()
            cots.pass_right()

        @pl.when(b == 2)
        def _():
            heads_of(3).pass_far()

        @pl.when(b == 3)
        def _():
            cots.pass_far()

        gather.got_others(os.at[pl.ds(0, 4), rows])
        white, _inv = whitened(middle_of(rows))
        low = (white * gain[...] + shift[...]).astype(LOW)
        n2[rows, :] = low

        @pl.when(b == 0)
        def _():
            arrived("y", 2)

        v = dot(low, wf[...].reshape(D, HIDDEN)) + bf[...]
        square = v * v
        t = jnp.tanh(GELU_A * v * (1.0 + GELU_B * square))
        half = 0.5 * (1.0 + t)
        act[rows, :] = (v * half).astype(LOW)
        slope = 0.5 * GELU_A * (1.0 + 3.0 * GELU_B * square)
        da[rows, :] = (half + v * (1.0 - t * t) * slope).astype(LOW)
        return 0

    lax.fori_loop(0, 4, forward, 0)
    arrived("y", 3)
    cots.got_others(cs.at[pl.ds(0, 4)])
    reduce = Reduce(
        lambda t: part.at[t],
        lambda j: from_core.at[j],
        lambda j: total.at[j - 1],
        lambda j: from_side.at[j // 2],
        lambda j: land.at[j // 2],
        part.at[pl.ds(0, 7)],
        OWN,
        r_send,
        r_recv,
    )
    weights = wp[...].reshape(HIDDEN, D)
    bfc_o[...] = jnp.zeros_like(bfc_o)

    def backward(j):
        chip = lax.rem(x + j, 4)
        rows = tile_rows(chip)
        c_low = cs[pl.ds(2 * chip, 2)].reshape(TILE, D)
        low = (dot_nt(c_low, weights) * da[rows, :].astype(F32)).astype(LOW)
        da[rows, :] = low
        bfc_o[0:1, :] += jnp.sum(low.astype(F32), axis=0, keepdims=True)
        d_n2 = dot_nt(low, wf[...].reshape(D, HIDDEN))
        part[pl.ds(2 * chip, 2)] = d_n2.astype(LOW).reshape(2, OWN, D)

    order = (2, 1, 3, 0)

    def back_step(i, _):
        j = jnp.where(i == 0, 2, jnp.where(i == 1, 1, jnp.where(i == 2, 3, 0)))
        backward(j)
        for n, j in enumerate(order):

            @pl.when(i == n)
            def _(n=n, j=j):
                reduce.to_core(j)
                if n == 0:
                    reduce.to_far()
                if n == 2:
                    reduce.to_side_alone(1)
                if n == 3:
                    reduce.to_side_alone(3)
                    reduce.to_side_joined(1)
                    reduce.to_side_joined(3)

        return 0

    lax.fori_loop(0, 4, back_step, 0)
    own_rows = pl.ds(pl.multiple_of(me * OWN, OWN), OWN)
    middle = middle_of(own_rows)
    mid_o[...] = middle
    write(mid_o, mid_out)
    gproj_o[...] = dot_tn(act[...], cs[...].reshape(TOK, D)).astype(LOW)
    for k in range(1, 4):
        peer = ahead("y", k, 4)
        piece = gproj_o.at[pl.ds(pl.multiple_of(128 * peer, 128), 128)]
        remote(piece, yp.at[k], y_send.at[4], y_recv.at[4], y=peer).start()
    g_fc = dot_tn(n2[...], da[...]).astype(LOW)
    gfc_o[...] = g_fc[:, : HIDDEN // 2]
    for k in range(32):
        at = 128 * (k % 8) + 32 * (k // 8)
        n2[at : at + 32, : HIDDEN // 2] = g_fc[32 * k : 32 * k + 32, HIDDEN // 2 :]
    for k in range(1, 8):
        peer = ahead("z", k, 8)
        piece = n2.at[pl.ds(pl.multiple_of(128 * peer, 128), 128), pl.ds(0, HIDDEN // 2)]
        remote(piece, fz.at[k], z_send.at[4], z_recv.at[4], z=peer).start()
    sends.append((fz.at[pl.ds(0, 7)], z_send.at[4]))
    write(gfc_o, gfc_out)

    def output_part(b, _):
        rows = tile_rows(b)
        xs[rows, :] = dot(act[rows, :], weights).astype(LOW)
        return 0

    lax.fori_loop(0, 4, output_part, 0)
    for j in range(4):
        block = 2 * lax.rem(x + j, 4) + core
        write(xs.at[block_rows(block)], outp.at[j])
        other = 2 * lax.rem(x + j, 4) + 1 - core
        remote(xs.at[block_rows(other)], outp_o.at[j], ro_send, ro_recv, core=1 - core).start()
    white, inverse = whitened(mid_o[...])
    c_own = cs[me].astype(F32)
    d_n2 = reduce.result()
    d_m = c_own + norm_back(d_n2, gain[...], white, inverse)
    dm_o[...] = d_m
    low = d_m.astype(LOW)
    d_o = dot_nt(low, wo[...].reshape(D, D)).astype(LOW)
    for t in range(8):
        dob[t] = d_o[:, SPAN * t : SPAN * (t + 1)]
    spread(lambda t: dob.at[t], do_all, a_send, a_recv)
    write(qm, qm_out)
    for tile in range(4):
        rows = tile_rows(tile)
        k_t = jnp.transpose(qkv[rows, SPAN : 2 * SPAN].astype(F32))
        for head in range(2):
            vt[head, :, rows] = jnp.where(head_lanes(k_t.shape, 0, head), k_t, 0.0).astype(LOW)
    write(vt, ktm_out)
    write(dob.at[me], do_all.at[me])
    write(dm_o, dm_out)
    small_o[...] = jnp.zeros_like(small_o)
    small_o[0:1, :] = jnp.sum(low.astype(F32), axis=0, keepdims=True)
    small_o[1:2, :] = jnp.sum(d_n2 * white, axis=0, keepdims=True)
    small_o[2:3, :] = jnp.sum(d_n2, axis=0, keepdims=True)
    small_o[3:4, :] = jnp.sum(c_own, axis=0, keepdims=True)
    left = jnp.concatenate([os[t, own_rows, :] for t in range(8)], axis=1)
    g_out = dot_tn(left, low).astype(LOW)
    for t in range(2):
        gop_o[t] = g_out[:, HIDDEN * t : HIDDEN * (t + 1)]
    write(gop_o.at[core], gop_out)
    remote(gop_o.at[1 - core], gop_other, go_send, go_recv, core=1 - core).start()

    weigh_pairs(3, 10)
    all_here(fz.at[pl.ds(0, 7)], z_recv.at[4])
    f_sum = n2[pl.ds(pl.multiple_of(128 * z, 128), 128), : HIDDEN // 2].astype(F32)
    for k in range(1, 8):
        f_sum = f_sum + fz[k].astype(F32)
    fz_sum[...] = f_sum.astype(LOW)
    write(fz_sum, fz_out)
    all_here(yp.at[pl.ds(0, 3)], y_recv.at[4])
    p_sum = gproj_o[pl.ds(pl.multiple_of(128 * y, 128), 128), :].astype(F32)
    for k in range(1, 4):
        p_sum = p_sum + yp[k].astype(F32)
    p_mid[...] = p_sum.astype(LOW)
    write(p_mid, gproj_out)
    all_here(outp_o, ro_recv)
    all_sent(outp_o, ro_send)
    all_here(gop_other, go_recv)
    all_sent(gop_other, go_send)
    all_here(do_all.at[pl.ds(0, 7)], a_recv)
    all_sent(dob.at[pl.ds(0, 7)], a_send)
    for ref, sem in sends:
        all_sent(ref, sem)
    all_sent(yp.at[pl.ds(0, 3)], y_send.at[4])
    to_core.wait_send()
    for copy in written:
        copy.wait()
    cots.sent()
    all_sent(os.at[pl.ds(0, 7)], g_send)
    reduce.sent()


def middle(
    x, w_qkv, w_out, w_fc, w_proj, bias_q, bias_v, bias_f, gain1, shift1, segment, cot, bo, gain, shift
):
    outs = [
        (shaped((TOK, D), LOW), ANYWHERE),
        (shaped((TOK, D), LOW), ANYWHERE),
        (shaped((2, TOK, SPAN), LOW), ANYWHERE),
        (shaped((2, SPAN, TOK), LOW), ANYWHERE),
        (shaped((TOK, 3 * SPAN), LOW), ANYWHERE),
        (shaped((4, 8, 32, 3 * SPAN), LOW), ANYWHERE),
        (shaped((TOK, SPAN), LOW), ANYWHERE),
        (shaped((2, TOK), F32), IN_VMEM),
        (shaped((4, OWN, D), LOW), ANYWHERE),
        (shaped((OWN, D), F32), ANYWHERE),
        (shaped((OWN, D), F32), ANYWHERE),
        (shaped((8, OWN, SPAN), LOW), ANYWHERE),
        (shaped((D, HIDDEN // 2), LOW), ANYWHERE),
        (shaped((128, D), LOW), ANYWHERE),
        (shaped((D, HIDDEN), LOW), ANYWHERE),
        (shaped((8, D), F32), IN_VMEM),
        (shaped((8, HIDDEN), F32), IN_VMEM),
        (shaped((4, OWN, D), LOW), ANYWHERE),
        (shaped((D, HIDDEN), LOW), ANYWHERE),
        (shaped((16, 2 * TILE, TILE), LOW), ANYWHERE),
        (shaped((128, HIDDEN // 2), LOW), ANYWHERE),
        (shaped((8, 16, D), LOW), ANYWHERE),
        (shaped((8, 32, HIDDEN), LOW), ANYWHERE),
        (shaped((8, 16, D), LOW), ANYWHERE),
    ]
    scratch = [
        pltpu.VMEM((32, 4 * D), LOW),
        pltpu.VMEM((32, 3 * SPAN), LOW),
        pltpu.VMEM((16, D), LOW),
        pltpu.VMEM((32, HIDDEN), LOW),
        pltpu.VMEM((16, D), LOW),
        pltpu.VMEM((1, 3 * SPAN), F32),
        pltpu.VMEM((1, HIDDEN), F32),
        pltpu.VMEM((TOK, 3 * SPAN), LOW),
        pltpu.VMEM((4, 8, 32, 3 * SPAN), LOW),
        pltpu.VMEM((TOK, SPAN), LOW),
        pltpu.VMEM((OWN, D), F32),
        pltpu.VMEM((OWN, D), F32),
        pltpu.VMEM((D, HIDDEN // 2), LOW),
        pltpu.VMEM((HIDDEN, D), LOW),
        pltpu.VMEM((2, D, HIDDEN), LOW),
        pltpu.VMEM((2, TOK, SPAN), LOW),
        pltpu.VMEM((2, SPAN, TOK), LOW),
        pltpu.VMEM((TOK, TILE), F32),
        pltpu.VMEM((TOK, D), LOW),
        pltpu.VMEM((8, TOK, SPAN), LOW),
        pltpu.VMEM((8, OWN, D), LOW),
        pltpu.VMEM((4, 8, 2, 16, D), LOW),
        pltpu.VMEM((4, 8, 32, HIDDEN), LOW),
        pltpu.VMEM((4, 8, 16, D), LOW),
        pltpu.VMEM((TOK, D), LOW),
        pltpu.VMEM((TOK, HIDDEN), LOW),
        pltpu.VMEM((TOK, HIDDEN), LOW),
        pltpu.VMEM((8, OWN, D), LOW),
        pltpu.VMEM((4, OWN, D), LOW),
        pltpu.VMEM((3, OWN, D), LOW),
        pltpu.VMEM((2, OWN // 2, D), LOW),
        pltpu.VMEM((2, OWN, D), LOW),
        pltpu.VMEM((8, OWN, SPAN), LOW),
        pltpu.VMEM((4, 128, D), LOW),
        pltpu.VMEM((128, D), LOW),
        pltpu.VMEM((8, 128, HIDDEN // 2), LOW),
        pltpu.VMEM((128, HIDDEN // 2), LOW),
        DMA((6,)), DMA((9,)), DMA((2,)), DMA((16,)), DMA, DMA((7,)), DMA((5,)), DMA((5,)),
        DMA, DMA((16,)), DMA, DMA((4,)), DMA, DMA,
        DMA((5,)), DMA((5,)), DMA, DMA((8,)), DMA, DMA, DMA, DMA, DMA, DMA, DMA, DMA((2,)),
    ]
    ins = [ANYWHERE] * 5 + [IN_VMEM] * 6 + [ANYWHERE] + [IN_VMEM] * 3
    return call(middle_kernel, outs, ins, scratch, "middle", 2, vmem=60)(
        x, w_qkv, w_out, w_fc, w_proj, bias_q[None], bias_v[None], bias_f[None], gain1[None],
        shift1[None], segment, cot, bo[None], gain[None], shift[None],
    )[:21]


def ending_kernel(
    qkv_in, qm_in, ktm_in, do_in, o_in, outp_in, outp_o, x_all, n1_in, gop_in, gop_other, gfc_in, fz_in,
    p_mid_in, p_in, wq_in, mid_in, dm_in, gain, bp, small, bfc,
    out_o, dtok_o, fin_o, early_o, late_o,
    vals, do_ref, o_own, go, gfc, f2, p_mid, wq, mid, dm, n1, p_buf,
    qm, dom, ktm, delta, dqt, dk, dv, dqkv, outp, xs, part, g_acc, gq, rows1,
    so, sumo, eo, lo, g_side, f2y, sn, sumn, en, ln, yf, zf, zp, f_mid,
    gy, gz, g_mid, gv, gvz, gvy, v_mid, oy, oz, o_mid, fin,
    early_v, early_z, early_y, early_w, late_v, late_z, late_y, late_w, out_low, dtok,
    loc, p_loc, o_loc, ro_send, ro_recv, rn_send, rn_recv, y_send, y_recv, z_send, z_recv,
    f_send, f_recv, s_send, s_recv,
):
    x, core, y, z = axis("x"), axis("core"), axis("y"), axis("z")
    me = 2 * x + core
    ready = greet(seq_peers() + y_peers() + z_peers())

    def order(n):
        j = jnp.where(n == 0, 2, jnp.where(n == 1, 1, jnp.where(n == 2, 3, 0)))
        return lax.rem(x + j, 4)

    def load_pair(first, second, slot):
        number = 4 * jnp.maximum(first, second) + jnp.minimum(first, second)
        return pltpu.make_async_copy(p_in.at[number], p_buf.at[slot], p_loc.at[slot])

    loads = [
        (do_in, do_ref), (o_in, o_own), (qkv_in.at[:, pl.ds(2 * SPAN, SPAN)], vals), (qm_in, qm),
        (ktm_in, ktm), (gfc_in.at[pl.ds(pl.multiple_of(256 * y, 256), 256)], gfc), (fz_in, f2),
        (p_mid_in, p_mid), (outp_in, outp), (outp_o, so), (gop_in, go),
        (gop_other, g_side), (wq_in, wq), (n1_in, n1), (x_all, xs), (mid_in, mid),
        (dm_in, dm),
    ]
    loads = [pltpu.make_async_copy(a, b, loc.at[k]) for k, (a, b) in enumerate(loads)]
    for copy in loads[:10]:
        copy.start()
    load_pair(order(0), order(0), 0).start()
    load_pair(order(0), order(1), 1).start()
    for ref in (dqt, dk, dv, g_acc, rows1):
        ref[...] = jnp.zeros_like(ref)
    for copy in loads[:2]:
        copy.wait()

    def prepare(tile, _):
        rows = tile_rows(tile)
        d_o = do_ref[rows, :].astype(F32)
        prod_t = jnp.transpose(d_o * o_own[rows, :].astype(F32))
        for head in range(2):
            lanes = head_lanes(d_o.shape, 1, head)
            dom[head, rows, :] = jnp.where(lanes, d_o, 0.0).astype(LOW)
            delta[head : head + 1, rows] = jnp.sum(
                prod_t[64 * head : 64 * (head + 1)], axis=0, keepdims=True
            )
        return 0

    lax.fori_loop(0, 4, prepare, 0)
    for copy in loads[10:14]:
        copy.start()
    ready()
    for copy in loads[2:8]:
        copy.wait()
    r_out = Reduce(
        None, lambda j: so.at[j], lambda j: sumo.at[j - 1], lambda j: eo.at[j // 2],
        lambda j: lo.at[j // 2], outp_in.at[pl.ds(0, 3)], OWN, ro_send, ro_recv,
        mine=lambda j: outp.at[j], exchanged=True,
    )
    r_dn1 = Reduce(
        lambda t: part.at[t], lambda j: sn.at[j], lambda j: sumn.at[j - 1], lambda j: en.at[j // 2],
        lambda j: ln.at[j // 2], part.at[pl.ds(0, 7)], OWN, rn_send, rn_recv,
    )
    sends = []

    def pieces_to_z(src, land, n):
        rows = land.shape[1]
        for k in range(1, 8):
            peer = ahead("z", k, 8)
            piece = src.at[pl.ds(pl.multiple_of(rows * peer, rows), rows)]
            remote(piece, land.at[k], z_send.at[n], z_recv.at[n], z=peer).start()
        sends.append((land.at[pl.ds(0, 7)], z_send.at[n]))

    def rows_to_y(src, land, n):
        rows = land.shape[1]
        for k in range(1, 4):
            peer = ahead("y", k, 4)
            piece = src.at[pl.ds(pl.multiple_of(rows * peer, rows), rows)]
            remote(piece, land.at[k], y_send.at[n], y_recv.at[n], y=peer).start()
        sends.append((land.at[pl.ds(0, 3)], y_send.at[n]))

    def from_y(src, land, n):
        rows = land.shape[1]
        all_here(land.at[pl.ds(0, 3)], y_recv.at[n])
        return summed(src[pl.ds(pl.multiple_of(rows * y, rows), rows), :], land, 4)

    def from_z(src, land, n):
        rows = land.shape[1]
        all_here(land.at[pl.ds(0, 7)], z_recv.at[n])
        return summed(src[pl.ds(pl.multiple_of(rows * z, rows), rows), :], land, 8)

    rows_to_y(gfc_in, yf, 0)
    for copy in loads[8:10]:
        copy.wait()
    r_out.to_far()
    rows_to_y(f2, f2y, 6)
    pieces_to_z(p_mid, zp, 0)

    def vector_to_z(src, land, n):
        for k in range(1, 8):
            remote(src, land.at[z], z_send.at[n], z_recv.at[n], z=ahead("z", k, 8)).start()
        sends.append((land.at[pl.ds(0, 7)], z_send.at[n]))

    def vector_to_y(src, z_land, y_land, n):
        all_here(z_land.at[pl.ds(0, 7)], z_recv.at[n])
        z_land[z] = src[...]
        y_land[y] = summed(z_land[0], z_land, 8)
        for k in range(1, 4):
            peer = ahead("y", k, 4)
            remote(y_land.at[y], y_land.at[y], y_send.at[n], y_recv.at[n], y=peer).start()
        sends.append((y_land.at[pl.ds(0, 3)], y_send.at[n]))

    def vector_to_group(y_land, whole, out, n):
        all_here(y_land.at[pl.ds(0, 3)], y_recv.at[n])
        whole[...] = summed(y_land[0], y_land, 4)
        spread(lambda t: whole, out, s_send.at[n - 4], s_recv.at[n - 4])
        out[me] = whole[...]

    for k in range(8):
        lanes = slice(SPAN * k, SPAN * (k + 1))
        for n in range(4):
            early_v[8 * n + k : 8 * n + k + 1, :] = small[n : n + 1, lanes]
    early_v[32:40, :] = jnp.zeros((8, SPAN), F32)
    for k in range(4):
        early_v[32 + k : 33 + k, :] = bfc[0:1, SPAN * k : SPAN * (k + 1)]
    vector_to_z(early_v, early_z, 4)

    def pair(first, second, slot):
        q_tile, k_tile = jnp.maximum(first, second), jnp.minimum(first, second)
        q_rows, k_rows = tile_rows(q_tile), tile_rows(k_tile)
        for head in range(2):
            q_h, do_h = qm[head, q_rows, :], dom[head, q_rows, :]
            p = p_buf[slot, TILE * head : TILE * (head + 1), :]
            d_p = dot_nt(vals[k_rows, :], do_h)
            d_s = (p.astype(F32) * (d_p - delta[head : head + 1, q_rows])).astype(LOW)
            dv[k_rows, :] += dot(p, do_h)
            dk[k_rows, :] += dot(d_s, q_h)
            dqt[q_tile] += dot(ktm[head, :, k_rows], d_s)

    def complete(tile):
        rows = tile_rows(tile)
        low = jnp.concatenate(
            [jnp.transpose(dqt[tile]) * 0.125, dk[rows, :], dv[rows, :]], axis=1
        ).astype(LOW)
        dqkv[rows, :] = low
        d_n1 = dot_nt(low, wq[...].reshape(D, 3 * SPAN))
        part[pl.ds(2 * tile, 2)] = d_n1.astype(LOW).reshape(2, OWN, D)

    def account(tile):
        rows = tile_rows(tile)
        g_acc[...] += dot_tn(n1[rows, :], dqkv[rows, :])

    def add_sums(tile, _):
        rows = tile_rows(tile)
        white, _inv = whitened(xs[rows, :].astype(F32))
        d_n1 = part[pl.ds(2 * tile, 2)].reshape(TILE, D).astype(F32)
        rows1[0:1, :] += jnp.sum(d_n1 * white, axis=0, keepdims=True)
        rows1[1:2, :] += jnp.sum(d_n1, axis=0, keepdims=True)
        wide = dqkv[rows, :].astype(F32)
        rows1[2:3, :SPAN] += jnp.sum(wide[:, :SPAN], axis=0, keepdims=True)
        rows1[3:4, :SPAN] += jnp.sum(wide[:, 2 * SPAN :], axis=0, keepdims=True)
        return 0

    def summed(own, others, count):
        total = own.astype(F32)
        for k in range(1, count):
            total = total + others[k].astype(F32)
        return total

    for step, j in enumerate((2, 1, 3, 0)):
        tile = order(step)

        def one(r, _, tile=tile, step=step):
            slot = lax.rem((0, 4, 7, 9)[step] + r - step, 2)
            load_pair(tile, order(r), slot).wait()
            pair(tile, order(r), slot)
            if step < 2:
                over = r + 2 - 4
                first = jnp.where(over < 0, step, step + 1)
                second = jnp.where(over < 0, r + 2, step + 1 + over)
                load_pair(order(first), order(second), slot).start()
            if step == 2:

                @pl.when(r == 2)
                def _():
                    load_pair(order(3), order(3), slot).start()

            return 0

        if step == 0:
            lax.fori_loop(0, 2, one, 0)
            for copy in loads[10:12]:
                copy.wait()
            go[...] = (go[...].astype(F32) + g_side[...].astype(F32)).astype(LOW)
            rows_to_y(go, oy, 1)
            lax.fori_loop(2, 4, one, 0)
            for copy in loads[12:14]:
                copy.wait()
            for copy in loads[14:]:
                copy.start()
            r_out.to_side_alone(1)
            r_out.to_side_alone(3)
        else:
            lax.fori_loop(step, 4, one, 0)
        complete(tile)
        r_dn1.to_core(j)
        account(tile)
        if step == 0:
            r_dn1.to_far()
        if step == 1:
            r_out.to_side_joined(1)
            r_out.to_side_joined(3)
            r_dn1.to_side_alone(1)
            all_here(yf.at[pl.ds(0, 3)], y_recv.at[0])
            f_mid[...] = summed(gfc[...], yf, 4).astype(LOW)
            pieces_to_z(f_mid, zf, 1)
        if step == 2:
            r_dn1.to_side_alone(3)
            vector_to_y(early_v, early_z, early_y, 4)

    qk, v_at = slice(0, 2 * SPAN), slice(2 * SPAN, 3 * SPAN)
    gq[...] = g_acc[:, qk].astype(LOW)
    rows_to_y(gq, gy, 2)
    for k in range(32):
        at = 128 * (k % 8) + 32 * (k // 8)
        gv[at : at + 32, :] = g_acc[32 * k : 32 * k + 32, v_at].astype(LOW)
    pieces_to_z(gv, gvz, 2)
    o_mid[...] = from_y(go, oy, 1).astype(LOW)
    pieces_to_z(o_mid, oz, 3)
    r_dn1.to_side_joined(1)
    r_dn1.to_side_joined(3)
    for copy in loads[14:]:
        copy.wait()
    lax.fori_loop(0, 4, add_sums, 0)
    for k in range(8):
        lanes = slice(SPAN * k, SPAN * (k + 1))
        for n in range(2):
            late_v[8 * n + k : 8 * n + k + 1, :] = rows1[n : n + 1, lanes]
    late_v[16:24, :] = rows1[0:8, :SPAN]
    vector_to_z(late_v, late_z, 5)

    def in_halves(row, total):
        fin[row : row + 16, :HIDDEN] = total[:16].astype(LOW)
        fin[row : row + 16, HIDDEN:] = total[16:].astype(LOW)

    fin[0:16, :] = from_z(p_mid, zp, 0).astype(LOW)
    in_halves(16, jnp.concatenate([from_z(f_mid, zf, 1), from_y(f2, f2y, 6)], axis=1))
    early = pl.ds(0, 32)
    finals = Gather(
        fin.at[early],
        lambda t: fin_o.at[t, early],
        fin_o.at[pl.ds(0, 7), early],
        32,
        f_send.at[0],
        f_recv.at[pl.ds(0, 4)],
    )
    finals.start()
    written = []

    def write(src, dst):
        written.append(pltpu.make_async_copy(src, dst, o_loc.at[len(written)]))
        written[-1].start()

    write(fin.at[early], fin_o.at[me, early])
    vector_to_group(early_y, early_w, early_o, 4)
    vector_to_y(late_v, late_z, late_y, 5)
    g_mid[...] = from_y(gq, gy, 2).astype(LOW)
    pieces_to_z(g_mid, gz, 6)
    v_mid[...] = from_z(gv, gvz, 2).astype(LOW)
    rows_to_y(v_mid, gvy, 3)
    vector_to_group(late_y, late_w, late_o, 5)
    in_halves(32, from_z(o_mid, oz, 3))
    third = pl.ds(32, 16)
    spread(lambda t: fin.at[third], fin_o.at[:, third], f_send.at[2], f_recv.at[5])
    write(fin.at[third], fin_o.at[me, third])
    finals.pass_left()
    finals.pass_right()
    own_rows = pl.ds(pl.multiple_of(me * OWN, OWN), OWN)
    white, inverse = whitened(xs[own_rows, :].astype(F32))
    total = from_z(g_mid, gz, 6)
    fin[48:64, 0 : 2 * SPAN] = total[:16].astype(LOW)
    fin[48:64, HIDDEN : HIDDEN + 2 * SPAN] = total[16:].astype(LOW)
    total = from_y(v_mid, gvy, 3)
    fin[48:64, v_at] = total[:16].astype(LOW)
    fin[48:64, HIDDEN + 2 * SPAN : HIDDEN + 3 * SPAN] = total[16:].astype(LOW)
    fin[48:64, 3 * SPAN : HIDDEN] = jnp.zeros((16, SPAN), LOW)
    fin[48:64, HIDDEN + 3 * SPAN :] = jnp.zeros((16, SPAN), LOW)
    late = pl.ds(48, 16)
    spread(lambda t: fin.at[late], fin_o.at[:, late], f_send.at[1], f_recv.at[4])
    write(fin.at[late], fin_o.at[me, late])
    out_low[...] = (mid[...] + r_out.result() + bp[...]).astype(LOW)
    write(out_low, out_o)
    finals.pass_far()
    d_n1 = r_dn1.result()
    dtok[...] = dm[...] + norm_back(d_n1, gain[...], white, inverse)
    write(dtok, dtok_o)
    finals.got_others(fin_o.at[pl.ds(0, 4), early])
    all_here(early_o.at[pl.ds(0, 7)], s_recv.at[0])
    all_here(late_o.at[pl.ds(0, 7)], s_recv.at[1])
    all_here(fin_o.at[pl.ds(0, 7), third], f_recv.at[5])
    all_here(fin_o.at[pl.ds(0, 7), late], f_recv.at[4])
    finals.sent()
    all_sent(fin_o.at[pl.ds(0, 7), late], f_send.at[1])
    all_sent(fin_o.at[pl.ds(0, 7), third], f_send.at[2])
    all_sent(early_o.at[pl.ds(0, 7)], s_send.at[0])
    all_sent(late_o.at[pl.ds(0, 7)], s_send.at[1])
    for ref, sem in sends:
        all_sent(ref, sem)
    for copy in written:
        copy.wait()
    for reduce in (r_out, r_dn1):
        reduce.sent()


def reduce_scratch(rows, columns):
    return [
        pltpu.VMEM((4, rows, columns), LOW),
        pltpu.VMEM((3, rows, columns), LOW),
        pltpu.VMEM((2, rows // 2, columns), LOW),
        pltpu.VMEM((2, rows, columns), LOW),
    ]


def ending(
    qkv, qm, ktm, d_o, o_own, outp, outp_o, x_all, n1, gop, gop_other, gfc, fz, gproj, p, wq, mid, dm,
    gain, bp, small, bfc,
):
    outs = [
        (shaped((OWN, D), LOW), ANYWHERE),
        (shaped((OWN, D), F32), ANYWHERE),
        (shaped((8, 64, D), LOW), ANYWHERE),
        (shaped((8, 40, SPAN), F32), IN_VMEM),
        (shaped((8, 24, SPAN), F32), IN_VMEM),
    ]
    scratch = [
        pltpu.VMEM((TOK, SPAN), LOW),
        pltpu.VMEM((TOK, SPAN), LOW),
        pltpu.VMEM((TOK, SPAN), LOW),
        pltpu.VMEM((D, HIDDEN), LOW),
        pltpu.VMEM((256, HIDDEN // 2), LOW),
        pltpu.VMEM((128, HIDDEN // 2), LOW),
        pltpu.VMEM((128, D), LOW),
        pltpu.VMEM((4, 8, 32, 3 * SPAN), LOW),
        pltpu.VMEM((OWN, D), F32),
        pltpu.VMEM((OWN, D), F32),
        pltpu.VMEM((TOK, D), LOW),
        pltpu.VMEM((2, 2 * TILE, TILE), LOW),
        pltpu.VMEM((2, TOK, SPAN), LOW),
        pltpu.VMEM((2, TOK, SPAN), LOW),
        pltpu.VMEM((2, SPAN, TOK), LOW),
        pltpu.VMEM((2, TOK), F32),
        pltpu.VMEM((4, SPAN, TILE), F32),
        pltpu.VMEM((TOK, SPAN), F32),
        pltpu.VMEM((TOK, SPAN), F32),
        pltpu.VMEM((TOK, 3 * SPAN), LOW),
        pltpu.VMEM((4, OWN, D), LOW),
        pltpu.VMEM((TOK, D), LOW),
        pltpu.VMEM((8, OWN, D), LOW),
        pltpu.VMEM((D, 3 * SPAN), F32),
        pltpu.VMEM((D, 2 * SPAN), LOW),
        pltpu.VMEM((8, D), F32),
        *reduce_scratch(OWN, D),
        pltpu.VMEM((D, HIDDEN), LOW),
        pltpu.VMEM((4, 32, HIDDEN // 2), LOW),
        *reduce_scratch(OWN, D),
        pltpu.VMEM((4, 256, HIDDEN // 2), LOW),
        pltpu.VMEM((8, 32, HIDDEN // 2), LOW), pltpu.VMEM((8, 16, D), LOW),
        pltpu.VMEM((256, HIDDEN // 2), LOW),
        pltpu.VMEM((4, 256, 2 * SPAN), LOW),
        pltpu.VMEM((8, 32, 2 * SPAN), LOW),
        pltpu.VMEM((256, 2 * SPAN), LOW),
        pltpu.VMEM((D, SPAN), LOW),
        pltpu.VMEM((8, 128, SPAN), LOW),
        pltpu.VMEM((4, 32, SPAN), LOW),
        pltpu.VMEM((128, SPAN), LOW),
        pltpu.VMEM((4, 256, HIDDEN), LOW),
        pltpu.VMEM((8, 32, HIDDEN), LOW),
        pltpu.VMEM((256, HIDDEN), LOW),
        pltpu.VMEM((64, D), LOW),
        *[
            pltpu.VMEM((*lead, rows, SPAN), F32)
            for rows in (40, 24)
            for lead in ((), (8,), (4,), ())
        ],
        pltpu.VMEM((OWN, D), LOW),
        pltpu.VMEM((OWN, D), F32),
        DMA((17,)), DMA((2,)), DMA((5,)), DMA, DMA((8,)), DMA, DMA((8,)),
        DMA((7,)), DMA((7,)), DMA((7,)), DMA((7,)), DMA((3,)), DMA((6,)), DMA((2,)), DMA((2,)),
    ]
    ins = [ANYWHERE] * 18 + [IN_VMEM] * 4
    return call(ending_kernel, outs, ins, scratch, "ending", 4, vmem=60)(
        qkv, qm, ktm, d_o.reshape(TOK, SPAN), o_own, outp, outp_o, x_all, n1, gop, gop_other, gfc, fz,
        gproj, p, wq, mid, dm, gain[None], bp[None], small, bfc,
    )


def results_kernel(
    fin, early, late, out, dtok, out_o, dtok_o, gq_out, go_out, gf_out, gp_out, *rest
):
    vectors, bf_o, out_s, dtok_s, gq_o, go_o, gf_o, gp_o, loc = rest[:8], *rest[8:]
    inward = [
        pltpu.make_async_copy(out, out_s, loc.at[0]),
        pltpu.make_async_copy(dtok, dtok_s, loc.at[1]),
    ]
    outward = [
        pltpu.make_async_copy(out_s, out_o, loc.at[2]),
        pltpu.make_async_copy(dtok_s, dtok_o, loc.at[3]),
    ]
    for copy in inward:
        copy.start()
    lane = lax.broadcasted_iota(jnp.int32, (40, 128), 1) // 16
    units = []
    for t in range(8):
        gp_o[16 * t : 16 * (t + 1), :] = fin[t, 0:16, :].astype(F32)
        span = slice(SPAN * t, SPAN * (t + 1))
        for half in range(2):
            rows = slice(16 * half, 16 * (half + 1))
            at = HIDDEN * half
            for k in range(3):
                gq_o[rows, D * k + SPAN * t : D * k + SPAN * (t + 1)] = fin[
                    t, 48:64, at + SPAN * k : at + SPAN * (k + 1)
                ].astype(F32)
        bias = jnp.concatenate([early[t, 32 + k : 33 + k, :] for k in range(4)], axis=1)
        units.append(
            jnp.concatenate(
                [
                    fin[t, 16:32, :HIDDEN].astype(F32),
                    fin[t, 16:32, HIDDEN:].astype(F32),
                    jnp.broadcast_to(bias, (8, HIDDEN)),
                ],
                axis=0,
            )
        )
        for k in range(2):
            vectors[6 + k][:, span] = late[t, 18 + k : 19 + k, :]
    early_sum, late_sum = early[0], late[0]
    for t in range(1, 8):
        early_sum, late_sum = early_sum + early[t], late_sum + late[t]
    for k in range(8):
        span = slice(SPAN * k, SPAN * (k + 1))
        for n in range(2):
            vectors[n][:, span] = late_sum[8 * n + k : 8 * n + k + 1, :]
        for n in range(4):
            vectors[2 + n][:, span] = early_sum[8 * n + k : 8 * n + k + 1, :]
    for core in range(2):
        for half in range(2):
            at = slice(HIDDEN * half, HIDDEN * (half + 1))
            total = fin[core, 32:48, at].astype(F32)
            for chip in range(1, 4):
                total = total + fin[2 * chip + core, 32:48, at].astype(F32)
            go_o[16 * half : 16 * (half + 1), HIDDEN * core : HIDDEN * (core + 1)] = total
    for into, out_of in zip(inward, outward):
        into.wait()
        out_of.start()
    for src, dst in ((gq_o, gq_out), (go_o, go_out), (gp_o, gp_out)):
        outward.append(pltpu.make_async_copy(src, dst, loc.at[2 + len(outward)]))
        outward[-1].start()
    for s in range(32):
        q, p = s // 8, s % 8
        tile = jnp.zeros((40, 128), F32)
        for t in range(8):
            turned = pltpu.roll(units[t][:, 128 * q : 128 * (q + 1)], (16 * t - 16 * p) % 128, 1)
            tile = jnp.where(lane == t, turned, tile)
        gf_o[:, 128 * s : 128 * (s + 1)] = tile[:32]
        bf_o[:, 128 * s : 128 * (s + 1)] = tile[32:33]
        if s % 8 == 7:
            part = slice(D * (s // 8), D * (s // 8 + 1))
            outward.append(
                pltpu.make_async_copy(
                    gf_o.at[:, part], gf_out.at[:, part], loc.at[2 + len(outward)]
                )
            )
            outward[-1].start()
    for copy in outward:
        copy.wait()


def results(fin, early, late, out, dtok):
    outs = [
        (shaped((OWN, D), LOW), ANYWHERE),
        (shaped((OWN, D), F32), ANYWHERE),
        (shaped((32, 3 * D), F32), ANYWHERE),
        (shaped((32, D), F32), ANYWHERE),
        (shaped((32, 4 * D), F32), ANYWHERE),
        (shaped((128, D), F32), ANYWHERE),
    ]
    narrow = (shaped((1, D), F32), IN_VMEM)
    outs += [narrow] * 8 + [(shaped((1, 4 * D), F32), IN_VMEM)]
    ins = [IN_VMEM, IN_VMEM, IN_VMEM, ANYWHERE, ANYWHERE]
    scratch = [
        pltpu.VMEM((OWN, D), LOW),
        pltpu.VMEM((OWN, D), F32),
        pltpu.VMEM((32, 3 * D), F32),
        pltpu.VMEM((32, D), F32),
        pltpu.VMEM((32, 4 * D), F32),
        pltpu.VMEM((128, D), F32),
        DMA((11,)),
    ]
    return call(results_kernel, outs, ins, scratch, "results")(fin, early, late, out, dtok)


def per_device(
    tokens, segment, ln1_gain, ln1_shift, w_qkv, bias_query, bias_value, w_out, bias_out,
    ln2_gain, ln2_shift, w_fc, bias_fc, w_proj, bias_proj, cotangent,
):
    (
        x_all, n1, qm, ktm, qkv, wq, o_own, _, outp, mid, dm, do_all, gfc, gproj, gop, small, bfc,
        outp_o, gop_other, p, fz,
    ) = middle(
        tokens[0], w_qkv, w_out, w_fc, w_proj, bias_query, bias_value, bias_fc, ln1_gain, ln1_shift,
        segment, cotangent[0], bias_out, ln2_gain, ln2_shift,
    )
    out, dtok, fin, early, late = ending(
        qkv, qm, ktm, do_all, o_own, outp, outp_o, x_all, n1, gop, gop_other, gfc, fz, gproj, p, wq,
        mid, dm, ln1_gain, bias_proj, small, bfc,
    )
    out, dtok, gq, go, gf, gp, *vectors = results(fin, early, late, out, dtok)
    v = [vector[0] for vector in vectors]
    return (
        out[None], dtok[None], v[0], v[1], gq, v[6], v[7], go, v[2], v[3], v[4], gf, v[8], gp, v[5],
    )


def solution(mesh):
    finer = Mesh(mesh.devices.reshape(4, 2, 4, 8), ("x", "core", "y", "z"))
    rows, whole = P(SHARD, None), P()
    tokens = P(SHARD, SEQ, None)
    return jax.shard_map(
        per_device,
        mesh=finer,
        in_specs=(
            tokens, rows, whole, whole, rows, whole, whole, rows, whole, whole, whole, rows,
            whole, rows, whole, tokens,
        ),
        out_specs=(
            tokens, tokens, whole, whole, rows, whole, whole, rows, whole, whole, whole, rows,
            whole, rows, whole,
        ),
        check_vma=False,
    )
```
